32 devices in a mesh: mp: 4 (over y, x), dp: 4 (over z), rep: 2 (over core).
Axes of the slice: x: 2, y: 2, z: 4, core: 2. Of those that a mesh axis runs over, the one named last changes fastest.
Arguments:
- states: bfloat16 [256, 32, 768], P(None, ('dp', 'rep')), may hold values from -26 to 26
- memory: bfloat16 [1024, 32, 768], P('mp', ('dp', 'rep')), may hold values from -6 to 6
- target_mask: int32 [32, 256], P(('dp', 'rep')), may hold values 0 or 1
- memory_length: int32 [32], P(('dp', 'rep')), may hold values from 512 to 1024, as said below
- norm_self: float32 [768], replicated, may hold values from 0.25 to 1.75
- self_query: bfloat16 [768, 768], P(None, 'mp'), may hold values from -0.02734375 to 0.02734375
- self_key: bfloat16 [768, 768], P(None, 'mp'), may hold values from -0.21875 to 0.21875
- self_value: bfloat16 [768, 768], P(None, 'mp'), may hold values from -0.21875 to 0.21875
- self_out: bfloat16 [768, 768], P('mp'), may hold values from -1.25 to 1.25
- bias_table: float32 [32, 12], P(None, 'mp'), may hold values from -4 to 4
- norm_cross: float32 [768], replicated, may hold values from 0.25 to 1.75
- cross_query: bfloat16 [768, 768], P(None, 'mp'), may hold values from -0.02734375 to 0.02734375
- cross_key: bfloat16 [768, 768], P(None, 'mp'), may hold values from -0.21875 to 0.21875
- cross_value: bfloat16 [768, 768], P(None, 'mp'), may hold values from -0.21875 to 0.21875
- cross_out: bfloat16 [768, 768], P('mp'), may hold values from -2.5 to 2.5
- norm_ffn: float32 [768], replicated, may hold values from 0.25 to 1.75
- ffn_gate: bfloat16 [768, 2048], P(None, 'mp'), may hold values from -0.21875 to 0.21875
- ffn_up: bfloat16 [768, 2048], P(None, 'mp'), may hold values from -0.21875 to 0.21875
- ffn_down: bfloat16 [2048, 768], P('mp'), may hold values from -0.125 to 0.125
- cotangent: bfloat16 [256, 32, 768], P('mp', ('dp', 'rep')), may hold values from -6 to 6
Outputs:
- block_out: bfloat16 [256, 32, 768], P('mp', ('dp', 'rep'))
- states_grad: float32 [256, 32, 768], P('mp', ('dp', 'rep'))
- memory_grad: float32 [1024, 32, 768], P('mp', ('dp', 'rep'))
- norm_self_grad: float32 [768], replicated
- self_query_grad: float32 [768, 768], P(None, 'mp')
- self_key_grad: float32 [768, 768], P(None, 'mp')
- self_value_grad: float32 [768, 768], P(None, 'mp')
- self_out_grad: float32 [768, 768], P('mp')
- bias_table_grad: float32 [32, 12], P(None, 'mp')
- norm_cross_grad: float32 [768], replicated
- cross_query_grad: float32 [768, 768], P(None, 'mp')
- cross_key_grad: float32 [768, 768], P(None, 'mp')
- cross_value_grad: float32 [768, 768], P(None, 'mp')
- cross_out_grad: float32 [768, 768], P('mp')
- norm_ffn_grad: float32 [768], replicated
- ffn_gate_grad: float32 [768, 2048], P(None, 'mp')
- ffn_up_grad: float32 [768, 2048], P(None, 'mp')
- ffn_down_grad: float32 [2048, 768], P('mp')
The draws below stay inside these ranges and needn't reach their ends.
Inputs may be any that keep to these rules, and one draw needn't show every extreme that they name: `memory_length`: each sequence has 512 or 1024 live memory slots; among the sequences of one index of dp and rep at least one has 1024.
All inputs are finite; a program needn't handle non-finite values. No bound on the sum of `target_mask` on one device may be relied on, other than what follows from the above.
Results may differ from the reference program's by a relative error of at most 0.022.
Values may be sent and summed in bfloat16 or wider, within the bound.
A program may use at most 192 MiB of HBM per device.

```python
import math
import jax
import jax.numpy as jnp
from jax import lax

D = 768
HEADS = 12
HEAD = 64
FF = 2048
BUCKETS = 32
TGT = 256
MEM = 1024
SEQ_DEV = 4
BATCH = 32


def draw_states(key, part):
    key = jax.random.fold_in(key, 11)
    key_cols, key_rows, key_base = jax.random.split(key, 3)
    columns = jnp.exp(jax.random.uniform(key_cols, (D,), jnp.float32, -1.15, 1.15))
    row_scale = jnp.exp(jax.random.uniform(key_rows, (TGT, BATCH, 1), jnp.float32, -0.7, 0.7))
    base = jnp.clip(jax.random.normal(key_base, (TGT, BATCH, D), jnp.float32), -4.0, 4.0)
    return (base * row_scale * columns).astype(jnp.bfloat16)


def draw_memory_length(key, part):
    key = jax.random.fold_in(key, 23)
    key_half, key_pick = jax.random.split(key)
    halves = jax.random.randint(key_half, (BATCH,), 1, 3) * (MEM // 2)
    chosen = jax.random.randint(key_pick, (BATCH // SEQ_DEV,), 0, SEQ_DEV)
    full_one = jnp.arange(BATCH) % SEQ_DEV == jnp.repeat(chosen, SEQ_DEV)
    return jnp.where(full_one, MEM, halves).astype(jnp.int32)


def touch_ends(values, key, low, high):
    place = [jax.random.randint(jax.random.fold_in(key, axis), (), 0, length) for axis, length in enumerate(values.shape)]
    longest = values.shape.index(max(values.shape))
    neighbour = place[:longest] + [(place[longest] + 1) % values.shape[longest]] + place[longest + 1:]
    return values.at[tuple(place)].set(low).at[tuple(neighbour)].set(high)


def steps_of(own_key, dims, cuts, low, largest):
    def one(position, parts):
        heights = jax.random.uniform(jax.random.fold_in(jax.random.fold_in(own_key, 6), position), (parts,), jnp.float32, low / len(cuts), largest / len(cuts))
        return jnp.repeat(jnp.exp(heights), dims[position] // parts).reshape((-1,) + (1,) * (len(dims) - position - 1))

    factor_of = one(*cuts[0])
    for cut in cuts[1:]:
        factor_of = factor_of * one(*cut)
    return factor_of


def bell_draw(stream_key, dims, spread, most, pieces=(), held_as=jnp.bfloat16):
    level = steps_of(stream_key, dims, pieces, -0.22, 0.18) if pieces else 1.0
    values = jax.random.normal(stream_key, dims, jnp.float32) * spread * level
    return jnp.minimum(jnp.maximum(values, -most), most).astype(held_as)


def setup_inputs(seed: int = 0) -> dict:
    splits = jax.random.split(jax.random.key(seed), 21)
    return {
        "states": draw_states(jax.random.fold_in(splits[20], 71), 0),
        "memory": bell_draw(splits[1], (MEM, BATCH, D), 1.0, 6.0, ((0, 4), (1, 8))),
        "target_mask": touch_ends((jax.random.randint(splits[2], (BATCH, TGT), 0, 8) < 7).astype(jnp.int32), jax.random.fold_in(splits[2], 1), 0, 1),
        "memory_length": draw_memory_length(jax.random.fold_in(splits[20], 71), 0),
        "norm_self": jnp.clip(1.0 + 0.15 * jax.random.normal(splits[4], (D,), jnp.float32), 0.25, 1.75),
        "self_query": bell_draw(splits[5], (D, HEADS * HEAD), (D * HEAD) ** -0.5, 0.02734375, ((1, 4),)),
        "self_key": bell_draw(splits[6], (D, HEADS * HEAD), D ** -0.5, 0.21875, ((1, 4),)),
        "self_value": bell_draw(splits[7], (D, HEADS * HEAD), D ** -0.5, 0.21875, ((1, 4),)),
        "self_out": bell_draw(splits[8], (HEADS * HEAD, D), (HEADS * HEAD * 8 // TGT) ** -0.5, 1.25, ((0, 4),)),
        "bias_table": bell_draw(splits[9], (BUCKETS, HEADS), 1.0, 4.0, ((1, 4),), jnp.float32),
        "norm_cross": jnp.clip(1.0 + 0.15 * jax.random.normal(splits[10], (D,), jnp.float32), 0.25, 1.75),
        "cross_query": bell_draw(splits[11], (D, HEADS * HEAD), (D * HEAD) ** -0.5, 0.02734375, ((1, 4),)),
        "cross_key": bell_draw(splits[12], (D, HEADS * HEAD), D ** -0.5, 0.21875, ((1, 4),)),
        "cross_value": bell_draw(splits[13], (D, HEADS * HEAD), D ** -0.5, 0.21875, ((1, 4),)),
        "cross_out": bell_draw(splits[14], (HEADS * HEAD, D), (HEADS * HEAD * 8 // MEM) ** -0.5, 2.5, ((0, 4),)),
        "norm_ffn": jnp.clip(1.0 + 0.15 * jax.random.normal(splits[15], (D,), jnp.float32), 0.25, 1.75),
        "ffn_gate": bell_draw(splits[16], (D, FF), D ** -0.5, 0.21875, ((1, 4),)),
        "ffn_up": bell_draw(splits[17], (D, FF), D ** -0.5, 0.21875, ((1, 4),)),
        "ffn_down": bell_draw(splits[18], (FF, D), FF ** -0.5, 0.125, ((0, 4),)),
        "cotangent": bell_draw(splits[19], (TGT, BATCH, D), 1.0, 6.0, ((0, 4), (1, 8))),
    }


eps = 1e-06
group_size = 4
highest_precision = lax.Precision.HIGHEST
bucket_edges = [math.ceil(16 * 8 ** (level / 16)) for level in range(1, 16)]

@jax.custom_vjp
def low(v):
    return lax.optimization_barrier(v.astype(jnp.bfloat16)).astype(jnp.float32)

@jax.custom_vjp
def low_back(v):
    return v

def low_keep(v):
    return (low(v), None)

def low_pass(kept, grad):
    return (grad,)

def back_keep(v):
    return (v, None)

def back_low(kept, grad):
    return (low(grad),)
low.defvjp(low_keep, low_pass)
low_back.defvjp(back_keep, back_low)

def bucket_of(offset):
    edge_list = jnp.array(bucket_edges, dtype=jnp.int32)
    passed = lax.optimization_barrier(jnp.sum((offset[..., None] >= edge_list).astype(jnp.int32), axis=-1))
    return jnp.minimum(offset, 16) + passed

def normalize(values, gain):
    return values * lax.rsqrt(lax.optimization_barrier(jnp.mean(values * values, axis=-1, keepdims=True)) + eps) * gain

def project(values, weight):
    return low(low_back(jnp.dot(values, weight, precision=highest_precision)))

def attend(query_rows, key_rows, value_rows, relative_position_bias, allowed):
    query_per_head = query_rows.reshape(query_rows.shape[0], -1, HEAD)
    key_per_head = key_rows.reshape(key_rows.shape[0], -1, HEAD)
    value_per_head = value_rows.reshape(value_rows.shape[0], -1, HEAD)
    attention_scores = jnp.einsum('kel,sel->eks', query_per_head, key_per_head, precision=highest_precision) + relative_position_bias
    attention_scores = low_back(jnp.where(allowed, attention_scores, -1e+30))
    attention_mix = low(jax.nn.softmax(attention_scores, axis=-1))
    combined_heads = jnp.einsum('qku,uql->kql', attention_mix, value_per_head, precision=highest_precision)
    return low(low_back(combined_heads.reshape(query_rows.shape[0], -1)))

def layer(params, states, memory, mask_row, length):
    norm_self, self_query, self_key, self_value, self_out, bias_table, norm_cross, cross_query, cross_key, cross_value, cross_out, norm_ffn, ffn_gate, ffn_up, ffn_down = params
    positions = jnp.arange(TGT, dtype=jnp.int32)
    distance = jnp.maximum(positions[:, None] - positions[None, :], 0)
    relative_position_bias = jnp.transpose(jnp.take(bias_table, bucket_of(distance), axis=0), (2, 0, 1))
    diagonal = positions[:, None] == positions[None, :]
    self_ok = (positions[:, None] >= positions[None, :]) & ((mask_row[None, :] != 0) | diagonal)
    cross_ok = (jnp.arange(MEM, dtype=jnp.int32) < length)[None, :]
    normed = low(normalize(states, norm_self))
    attended = attend(project(normed, self_query), project(normed, self_key), project(normed, self_value), relative_position_bias, self_ok[None])
    first_sum = states + low_back(jnp.dot(attended, self_out, precision=highest_precision))
    normed = low(normalize(first_sum, norm_cross))
    attended = attend(project(normed, cross_query), project(memory, cross_key), project(memory, cross_value), 0.0, cross_ok[None])
    second_sum = first_sum + low_back(jnp.dot(attended, cross_out, precision=highest_precision))
    normed = low(normalize(second_sum, norm_ffn))
    gate_part = low_back(jnp.dot(normed, ffn_gate, precision=highest_precision))
    up_part = low_back(jnp.dot(normed, ffn_up, precision=highest_precision))
    hidden = low(jax.nn.gelu(gate_part, approximate=True) * up_part)
    return second_sum + low_back(jnp.dot(hidden, ffn_down, precision=highest_precision))

def reference(states, memory, target_mask, memory_length, norm_self, self_query, self_key, self_value, self_out, bias_table, norm_cross, cross_query, cross_key, cross_value, cross_out, norm_ffn, ffn_gate, ffn_up, ffn_down, cotangent):
    params = tuple((weight.astype(jnp.float32) for weight in (norm_self, self_query, self_key, self_value, self_out, bias_table, norm_cross, cross_query, cross_key, cross_value, cross_out, norm_ffn, ffn_gate, ffn_up, ffn_down)))
    groups = BATCH // group_size

    def arrange(values, row_len):
        return jnp.transpose(values.astype(jnp.float32), (1, 0, 2)).reshape(groups, group_size, row_len, D)
    inputs = (arrange(states, TGT), arrange(memory, MEM), target_mask.reshape(groups, group_size, TGT), memory_length.reshape(groups, group_size), arrange(cotangent, TGT))

    def advance(running, group_inputs):
        seq_states, seq_memory, seq_mask, seq_length, seq_cotangent = group_inputs

        def run(weights, state_group, memory_group):
            return jax.vmap(lambda state_one, memory_one, mask_one, length_one: layer(weights, state_one, memory_one, mask_one, length_one))(state_group, memory_group, seq_mask, seq_length)
        result, pullback = jax.vjp(run, params, seq_states, seq_memory)
        weight_grads, state_grads, memory_grads = pullback(seq_cotangent)
        running = jax.tree.map(lambda running_sum, addend: running_sum + addend, running, weight_grads)
        return (running, (result.astype(jnp.bfloat16), state_grads, memory_grads))
    begin = jax.tree.map(jnp.zeros_like, params)
    running, (results, state_grads, memory_grads) = lax.scan(advance, begin, inputs)

    def restore(values, row_len):
        return jnp.transpose(values.reshape(BATCH, row_len, D), (1, 0, 2))
    return (restore(results, TGT), restore(state_grads, TGT), restore(memory_grads, MEM), running[0], running[1], running[2], running[3], running[4], running[5], running[6], running[7], running[8], running[9], running[10], running[11], running[12], running[13], running[14])
```

```python
import math
import types

import jax
import jax.numpy as jnp
from jax import lax
from jax.experimental import pallas as pl
from jax.experimental.pallas import tpu as pltpu
from jax.sharding import PartitionSpec as P

eps = 1e-06
bucket_edges = [math.ceil(16 * 8 ** (level / 16)) for level in range(1, 16)]
BF = jnp.bfloat16
F32 = jnp.float32
NEG = -1e30
MESH = pl.DeviceIdType.MESH
WAYS = 4
CK, CV, SO, CQ, CO = range(5)


def bucket_of(offset):
    edge_list = jnp.array(bucket_edges, dtype=jnp.int32)
    passed = jnp.sum((offset[..., None] >= edge_list).astype(jnp.int32), axis=-1)
    return jnp.minimum(offset, 16) + passed


def dots(a, b, ca, cb):
    return lax.dot_general(a, b, (((ca,), (cb,)), ((), ())), preferred_element_type=F32)


def nn(a, b):
    return dots(a, b, 1, 0)


def nt(a, b):
    return dots(a, b, 1, 1)


def tn(a, b):
    return dots(a, b, 0, 0)


def rms(v, g):
    return v * lax.rsqrt(jnp.mean(v * v, axis=-1, keepdims=True) + eps) * g


def rms_back(v, g, n):
    r = lax.rsqrt(jnp.mean(v * v, axis=-1, keepdims=True) + eps)
    ng = n * g
    return r * ng - v * (r * r * r) * jnp.mean(ng * v, axis=-1, keepdims=True), n * v * r


def gelu_parts(a):
    c = math.sqrt(2 / math.pi)
    t = jnp.tanh(c * (a + 0.044715 * a * a * a))
    half = 0.5 * (1 + t)
    return half * a, half + 0.5 * a * (1 - t * t) * c * (1 + 3 * 0.044715 * a * a)


def place():
    return lax.axis_index("mp"), lax.axis_index("dp"), lax.axis_index("rep")


def peer(k):
    m, z, r = place()
    return (m ^ k, z, r)


def partner():
    m, z, r = place()
    return (m, z, 1 - r)


def greet(core):
    barrier = pltpu.get_barrier_semaphore()
    for k in range(1, WAYS):
        pl.semaphore_signal(barrier, inc=1, device_id=peer(k), device_id_type=MESH)
    if core:
        pl.semaphore_signal(barrier, inc=1, device_id=partner(), device_id_type=MESH)
    pl.semaphore_wait(barrier, WAYS - 1 + core)


def send(src, dst, sems, at, to):
    return pltpu.make_async_remote_copy(
        src_ref=src, dst_ref=dst, send_sem=sems[0].at[at], recv_sem=sems[1].at[at], device_id=to, device_id_type=MESH
    )


def run_kernel(name, phases, ins, outs, scratch, cid, flops=0):
    names = list(ins) + list(outs) + list(scratch)

    def body(*refs):
        held = types.SimpleNamespace(**dict(zip(names, refs)))
        for phase in phases:
            phase(held)

    got = pl.pallas_call(
        body,
        name=name,
        out_shape=[jax.ShapeDtypeStruct(shape, dtype) for shape, dtype, _ in outs.values()],
        in_specs=[pl.BlockSpec(memory_space=space) for _, space in ins.values()],
        out_specs=[pl.BlockSpec(memory_space=space) for _, _, space in outs.values()],
        scratch_shapes=list(scratch.values()),
        compiler_params=pltpu.CompilerParams(
            collective_id=cid, has_side_effects=True, vmem_limit_bytes=60 * 2**20
        ),
        cost_estimate=pl.CostEstimate(flops=flops, bytes_accessed=flops // 200, transcendentals=0),
    )(*[array for array, _ in ins.values()])
    return dict(zip(outs, got))


V, ANY, SM = pltpu.VMEM, pl.ANY, pltpu.SMEM


def dma(*shape):
    return pltpu.SemaphoreType.DMA(shape)


def start_sends(R):
    m, z, r = place()
    quarter = R.mem.shape[1]
    sh = R.wa.shape[1]
    half = sh // 2
    greet(1)
    own = pltpu.make_async_copy(R.mem.at[m], R.memf.at[pl.ds(m * quarter, quarter)], R.l_sem.at[0])
    own.start()
    mine = pltpu.make_async_copy(R.wa, R.waf.at[:, pl.ds(m * sh, sh)], R.l_sem.at[1])
    mine.start()
    R.local = [own, mine]
    R.mem_copies, R.wa_copies, R.fw_copies, R.cot_copies = {}, {}, {}, {}
    rows = pl.ds(m * quarter, quarter)
    for k in range(1, WAYS):
        copy = send(R.mem.at[m ^ k], R.memf.at[rows], (R.mem_s, R.mem_r), k, peer(k))
        copy.start()
        R.mem_copies[k] = copy
    rows = pl.ds(m * sh + r * half, half)
    for part, (lo, n) in enumerate(((0, 2), (2, 3))):
        for k in range(1, WAYS):
            copy = send(
                R.wa.at[pl.ds(lo, n), pl.ds(r * half, half)],
                R.waf.at[pl.ds(lo, n), rows],
                (R.wa_s, R.wa_r),
                part * WAYS + k,
                peer(k),
            )
            copy.start()
            R.wa_copies[part, k] = copy


def send_cot(R):
    m, z, r = place()
    tc = R.cot.shape[1]
    rows = pl.ds(m * tc, tc)
    own = pltpu.make_async_copy(R.cot, R.upall.at[:, rows], R.l_sem.at[2])
    own.start()
    R.local.append(own)
    for k in range(1, WAYS):
        copy = send(R.cot, R.upall.at[:, rows], (R.cot_s, R.cot_r), k, peer(k))
        copy.start()
        R.cot_copies[k] = copy


def forward(R, part):
    m, z, r = place()
    sh = R.wa.shape[1]
    half = sh // 2
    lo, n = ((0, 2), (2, 3))[part]
    for k in range(1, WAYS):
        R.wa_copies[part, k].wait_recv()
        view = R.waf.at[pl.ds(lo, n), pl.ds((m ^ k) * sh + r * half, half)]
        copy = send(view, view, (R.fw_s, R.fw_r), part * WAYS + k, partner())
        copy.start()
        R.fw_copies[part, k] = copy


def self_allowed(R, s):
    T = R.st.shape[1]
    j = lax.broadcasted_iota(jnp.int32, (T, T), 0)
    i = lax.broadcasted_iota(jnp.int32, (T, T), 1)
    return (j == i) | ((j < i) & (R.mask[s] != 0))


def toeplitz(R, h):
    T = R.st.shape[1]
    rows = jnp.broadcast_to(R.vec[h], (T, T))
    return pltpu.roll(rows, 0, 1, stride=1, stride_axis=0)


def self_forward(R):
    m, z, r = place()
    _, T, D = R.st.shape
    HW = R.ws.shape[0] // 3
    heads = R.vec.shape[0]
    hd = HW // heads
    for h in range(heads):
        R.et[h] = toeplitz(R, h)
    R.att_copies = {}

    def one(s):
        normed = rms(R.st[s].astype(F32), R.g_self[...]).astype(BF)
        R.qs[s] = nt(R.ws[0:HW], normed).astype(BF)
        R.ks[s] = nt(normed, R.ws[HW : 2 * HW]).astype(BF)
        R.vs[s] = nt(R.ws[2 * HW : 3 * HW], normed).astype(BF)
        allowed = self_allowed(R, s)
        for h in range(heads):
            rows = slice(h * hd, (h + 1) * hd)
            parts = [R.qs[s, rows] if g == h else jnp.zeros((hd, T), BF) for g in range(heads)]
            scores = nn(R.ks[s], jnp.concatenate(parts, axis=0)) + R.et[h]
            scores = jnp.where(allowed, scores, NEG)
            top = jnp.max(scores, axis=0, keepdims=True)
            weights = jnp.exp(scores - top)
            total = jnp.sum(weights, axis=0, keepdims=True)
            mix = (weights * (1 / total)).astype(BF)
            R.atp[s, rows] = nn(R.vs[s, rows], mix).astype(BF)
            R.lse_s[s, h] = top + jnp.log(total)

    def step(k, carry):
        s = m ^ k
        one(s)
        send(R.atp.at[s], R.att.at[pl.ds(m * HW, HW)], (R.att_s, R.att_r), k, (s, z, r)).start()
        return carry

    lax.fori_loop(1, WAYS, step, 0)
    one(m)
    R.att[pl.ds(pl.multiple_of(m * HW, HW), HW)] = R.atp[m]


def wait_att(R):
    m, z, r = place()
    HW = R.ws.shape[0] // 3
    for k in range(1, WAYS):
        send(R.atp.at[m ^ k], R.att.at[pl.ds(m * HW, HW)], (R.att_s, R.att_r), k, peer(k)).wait()


def cross_kv(R):
    for copy in R.local:
        copy.wait()
    for copy in R.mem_copies.values():
        copy.wait()
    for k in range(1, WAYS):
        R.wa_copies[0, k].wait_send()
        R.fw_copies[0, k].wait()
    M = R.memf.shape[0]
    step = 256

    def rows(i, carry):
        at = pl.ds(pl.multiple_of(i * step, step), step)
        block = R.memf[at]
        k = nt(block, R.waf[CK]).astype(BF)
        R.kc[at] = k
        v = nt(block, R.waf[CV]).astype(BF)
        R.vc[at] = v
        R.kct[:, at] = k.T
        R.vct[:, at] = v.T
        return carry

    lax.fori_loop(0, M // step, rows, 0)


def after_self(R):
    m, z, r = place()
    for k in range(1, WAYS):
        R.wa_copies[1, k].wait_send()
        R.fw_copies[1, k].wait()
    first = R.st[m].astype(F32) + tn(R.att[...], R.waf[SO])
    R.first[...] = first
    normed = rms(first, R.g_cross[...]).astype(BF)
    R.qc[...] = nt(R.waf[CQ], normed).astype(BF)


def padded_head(ref, p, a, hd):
    T = ref.shape[1]
    rows = ref[pl.ds(pl.multiple_of(p * 2 * hd + a * hd, hd), hd)]
    zero = jnp.zeros((hd, T), BF)
    return jnp.concatenate([rows, zero] if a == 0 else [zero, rows], axis=0)


def live_slots(R):
    m, z, r = place()
    M, T = R.memf.shape[0], R.qc.shape[1]
    return lax.broadcasted_iota(jnp.int32, (M, T), 0) < R.lens[m]


def cross_forward(R):
    hd = R.qs.shape[1] // R.vec.shape[0]
    heads = R.qc.shape[0] // hd

    def pair(p, carry):
        lanes = pl.ds(pl.multiple_of(p * 2 * hd, 2 * hd), 2 * hd)
        for a in range(2):
            rows = pl.ds(pl.multiple_of(p * 2 * hd + a * hd, hd), hd)
            scores = nn(R.kc[:, lanes], padded_head(R.qc, p, a, hd))
            scores = jnp.where(live_slots(R), scores, NEG)
            top = jnp.max(scores, axis=0, keepdims=True)
            weights = jnp.exp(scores - top)
            total = jnp.sum(weights, axis=0, keepdims=True)
            mixed = nn(R.vct[rows], weights.astype(BF)) * (1 / total)
            R.attc[rows] = mixed.astype(BF)
            R.lse_c[2 * p + a] = top + jnp.log(total)
        return carry

    lax.fori_loop(0, heads // 2, pair, 0)


def second_part(R):
    m, z, r = place()
    second = R.first[...] + tn(R.attc[...], R.waf[CO])
    R.second[...] = second
    R.nall[m] = rms(second, R.g_ffn[...]).astype(BF)
    copies = [send(R.nall.at[m], R.nall.at[m], (R.nf_s, R.nf_r), k, peer(k)) for k in range(1, WAYS)]
    for copy in copies:
        copy.start()
    for copy in list(R.cot_copies.values()) + copies:
        copy.wait()


def first_phase(R):
    start_sends(R)
    send_cot(R)
    self_forward(R)
    forward(R, 0)
    cross_kv(R)
    forward(R, 1)
    wait_att(R)
    after_self(R)
    cross_forward(R)
    second_part(R)


def per_device(states, memory, target_mask, memory_length, norm_self, self_query, self_key, self_value, self_out,
               bias_table, norm_cross, cross_query, cross_key, cross_value, cross_out, norm_ffn, ffn_gate, ffn_up,
               ffn_down, cotangent):
    me = lax.axis_index("mp")
    ways = WAYS
    T = states.shape[0]
    D = states.shape[2]
    HW = self_query.shape[1]
    HC = bias_table.shape[1]
    hd = HW // HC
    M = memory.shape[0] * ways
    st = jnp.transpose(states, (1, 0, 2))
    mem = jnp.transpose(memory, (1, 0, 2))
    cot = jnp.transpose(cotangent, (1, 0, 2))
    wq, wk, wv = self_query.T, self_key.T, self_value.T
    ws = jnp.concatenate([wq, wk, wv], axis=0)
    wa = jnp.stack([cross_key.T, cross_value.T, self_out, cross_query.T, cross_out])
    pos = jnp.arange(T, dtype=jnp.int32)
    vec = jnp.take(bias_table, bucket_of(pos), axis=0).T[:, None]
    ins = dict(
        st=(st, V), mem=(mem, ANY), ws=(ws, V), wa=(wa, ANY), mask=(target_mask[:, :, None], V), vec=(vec, V),
        lens=(memory_length, SM), g_self=(norm_self[None], V), g_cross=(norm_cross[None], V), g_ffn=(norm_ffn[None], V),
        cot=(cot, ANY),
    )
    heads = D // hd
    outs = dict(
        att=((D, T), BF, V), qs=((ways, HW, T), BF, V), ks=((ways, T, HW), BF, V), vs=((ways, HW, T), BF, V),
        lse_s=((ways, HC, 1, T), F32, V), first=((T, D), F32, V), second=((T, D), F32, V), qc=((D, T), BF, V),
        kc=((M, D), BF, V), kct=((D, M), BF, V), vc=((M, D), BF, V), lse_c=((heads, 1, T), F32, V),
        attc=((D, T), BF, V), memf=((M, D), BF, V), waf=((5, D, D), BF, V), nall=((ways, T, D), BF, V),
        upall=((ways, T, D), BF, V),
    )
    scratch = dict(
        vct=V((D, M), BF), et=V((HC, T, T), F32), atp=V((ways, HW, T), BF), l_sem=dma(3), mem_s=dma(4), mem_r=dma(4),
        wa_s=dma(8), wa_r=dma(8), fw_s=dma(8), fw_r=dma(8), att_s=dma(4), att_r=dma(4), nf_s=dma(4), nf_r=dma(4),
        cot_s=dma(4), cot_r=dma(4),
    )
    G = types.SimpleNamespace(**run_kernel("attend", [first_phase], ins, outs, scratch, 0))
    ck, cv, so, cq, co = (G.waf[i] for i in range(5))
    att_s, first, second, att_c, memf, kc, qc, lc = G.att, G.first, G.second, G.attc, G.memf, G.kc, G.qc, G.lse_c
    vc = G.vc.T
    nall, upall = G.nall, G.upall
    QT, K, VT, LSE = G.qs, G.ks, G.vs, G.lse_s
    a2a = lambda x, si, ci: lax.all_to_all(x, "mp", si, ci, tiled=True)
    dist = jnp.maximum(pos[None, :] - pos[:, None], 0)
    ET = jnp.take(vec[:, 0], dist, axis=1)
    ok = (pos[:, None] <= pos[None, :])[None] & ((target_mask[:, :, None] != 0) | (pos[:, None] == pos[None, :])[None])
    normed = rms(st.astype(F32), norm_self).astype(BF)
    nc = rms(first, norm_cross).astype(BF)
    length = lax.dynamic_index_in_dim(memory_length, me, 0, keepdims=False)
    live = (jnp.arange(M, dtype=jnp.int32) < length)[:, None]
    nr = nall.reshape(ways * T, D)
    ur = upall.reshape(ways * T, D)
    g, u = nn(nr, ffn_gate), nn(nr, ffn_up)
    ge, gd = gelu_parts(g)
    hid = (ge * u).astype(BF)
    branch = nn(hid, ffn_down).reshape(ways, T, D)
    hg = nt(ur, ffn_down)
    gg, ug = (hg * u * gd).astype(BF), (hg * ge).astype(BF)
    down_grad = tn(hid, ur)
    gate_grad = tn(nr, gg)
    up_grad = tn(nr, ug)
    ngp = (nt(gg, ffn_gate) + nt(ug, ffn_up)).reshape(ways, T, D).astype(BF)
    branch = branch + jnp.where(jnp.arange(ways)[:, None, None] == me, second[None], 0)
    br = a2a(branch.astype(BF)[None], 2, 0)
    block_out = jnp.transpose(jnp.sum(br.astype(F32), axis=0), (1, 0, 2)).astype(BF)
    ng = jnp.sum(a2a(ngp, 0, 0).astype(F32), axis=0)
    upown = lax.dynamic_index_in_dim(upall, me, 0, keepdims=False).astype(F32)
    back, gain = rms_back(second, norm_ffn, ng)
    ffn_gain = jnp.sum(gain, axis=0)
    sgrad = upown + back
    cup = sgrad.astype(BF)
    co_grad = nn(att_c, cup)
    doT = nt(co, cup).astype(BF)
    dq, dk, dv = [], [], []
    for h in range(heads):
        sl = slice(h * hd, (h + 1) * hd)
        sT = jnp.where(live, nn(kc[:, sl], qc[sl]), NEG)
        p = jnp.exp(sT - lc[h])
        dpT = tn(vc[sl], doT[sl])
        dv.append(nt(doT[sl], p.astype(BF)).astype(BF))
        ds = (p * (dpT - jnp.sum(p * dpT, axis=0, keepdims=True))).astype(BF)
        dq.append(tn(kc[:, sl], ds).astype(BF))
        dk.append(nt(qc[sl], ds).astype(BF))
    dq, dk, dv = (jnp.concatenate(x, 0) for x in (dq, dk, dv))
    cq_grad, ck_grad, cv_grad = nn(dq, nc), nn(dk, memf), nn(dv, memf)
    mg = (tn(dk, ck) + tn(dv, cv)).astype(BF).reshape(ways, M // ways, D)
    memory_grad = jnp.transpose(a2a(mg, 0, 0).astype(F32), (1, 0, 2))
    ng = tn(dq, cq)
    back, gain = rms_back(first, norm_cross, ng)
    cross_gain = jnp.sum(gain, axis=0)
    fgrad = sgrad + back
    sup = fgrad.astype(BF)
    so_grad = nn(att_s, sup)
    doT = nt(so, sup).astype(BF)
    doT = a2a(doT[None], 1, 0)
    ngs = []
    wqg = wkg = wvg = 0
    dsum = [0] * HC
    for s in range(4):
        dq, dk, dv = [], [], []
        for h in range(HC):
            sl = slice(h * hd, (h + 1) * hd)
            sT = nn(K[s][:, sl], QT[s][sl]) + ET[h]
            sT = jnp.where(ok[s], sT, NEG)
            p = jnp.exp(sT - LSE[s][h])
            dpT = tn(VT[s][sl], doT[s][sl])
            dv.append(nt(doT[s][sl], p.astype(BF)).astype(BF))
            ds = (p * (dpT - jnp.sum(p * dpT, axis=0, keepdims=True))).astype(BF)
            dsum[h] = dsum[h] + ds.astype(F32)
            dq.append(tn(K[s][:, sl], ds).astype(BF))
            dk.append(nt(QT[s][sl], ds).astype(BF))
        dq, dk, dv = (jnp.concatenate(x, 0) for x in (dq, dk, dv))
        wqg, wkg, wvg = wqg + nn(dq, normed[s]), wkg + nn(dk, normed[s]), wvg + nn(dv, normed[s])
        ngs.append(tn(dq, wq) + tn(dk, wk) + tn(dv, wv))
    ngs = jnp.stack(ngs).astype(BF)
    ng = jnp.sum(a2a(ngs[None], 2, 0).astype(F32), axis=0)
    fg = a2a(fgrad.astype(BF)[None], 1, 0).astype(F32)
    tc = T // ways
    v = lax.dynamic_slice_in_dim(st, me * tc, tc, 1).astype(F32)
    back, gain = rms_back(v, norm_self, ng)
    self_gain = jnp.sum(gain, axis=(0, 1))
    states_grad = jnp.transpose(fg + back, (1, 0, 2))
    dd = jnp.stack(dsum)
    diag = jnp.stack([jnp.sum(jnp.where((pos[None, :] - pos[:, None] == r)[None], dd, 0), axis=(1, 2)) for r in range(T)])
    onehot = (bucket_of(pos)[:, None] == jnp.arange(bias_table.shape[0])).astype(F32)
    bias_grad = jnp.einsum("rh,rk->kh", diag, onehot, precision=lax.Precision.HIGHEST)
    cross = jnp.stack([so_grad, cq_grad, ck_grad, cv_grad, co_grad]).astype(BF)
    cross = lax.psum_scatter(cross, "mp", scatter_dimension=1, tiled=True)
    cross = lax.psum(cross.astype(F32), ("dp", "rep"))
    wqg, wkg, wvg, down_grad, gate_grad, up_grad, bias_grad = lax.psum((wqg, wkg, wvg, down_grad, gate_grad, up_grad, bias_grad), ("dp", "rep"))
    gains = lax.psum(jnp.stack([self_gain, cross_gain, ffn_gain]), ("mp", "dp", "rep"))
    return (block_out, states_grad, memory_grad, gains[0], wqg.T, wkg.T, wvg.T, cross[0], bias_grad, gains[1],
            cross[1].T, cross[2].T, cross[3].T, cross[4], gains[2], gate_grad, up_grad, down_grad)


def solution(mesh):
    seq = ("dp", "rep")
    col, row, tok = P(None, "mp"), P("mp", None), P("mp", seq, None)
    in_specs = (P(None, seq, None), tok, P(seq, None), P(seq), P(), col, col, col, row, col, P(), col, col, col, row,
                P(), col, col, row, tok)
    out_specs = (tok, tok, tok, P(), col, col, col, row, col, P(), col, col, col, row, P(), col, col, row)
    return jax.shard_map(per_device, mesh=mesh, in_specs=in_specs, out_specs=out_specs, check_vma=False)
```

```python
import math
import types

import jax
import jax.numpy as jnp
from jax import lax
from jax.experimental import pallas as pl
from jax.experimental.pallas import tpu as pltpu
from jax.sharding import PartitionSpec as P

eps = 1e-06
bucket_edges = [math.ceil(16 * 8 ** (level / 16)) for level in range(1, 16)]
BF = jnp.bfloat16
F32 = jnp.float32
NEG = -1e30
VMEM_BYTES = 64 * 2**20 - 2**17
MESH = pl.DeviceIdType.MESH
WAYS = 4
LEVELS = 4
CK, CV, SO, CQ, CO = range(5)
PARTS = ((0, 2), (2, 3))


def bucket_of(offset):
    edge_list = jnp.array(bucket_edges, dtype=jnp.int32)
    passed = jnp.sum((offset[..., None] >= edge_list).astype(jnp.int32), axis=-1)
    return jnp.minimum(offset, 16) + passed


def dots(a, b, ca, cb):
    return lax.dot_general(a, b, (((ca,), (cb,)), ((), ())), preferred_element_type=F32)


def nn(a, b):
    return dots(a, b, 1, 0)


def nt(a, b):
    return dots(a, b, 1, 1)


def tn(a, b):
    return dots(a, b, 0, 0)


def rms(v, g):
    return v * lax.rsqrt(jnp.mean(v * v, axis=-1, keepdims=True) + eps) * g


def rms_back(v, g, n):
    r = lax.rsqrt(jnp.mean(v * v, axis=-1, keepdims=True) + eps)
    ng = n * g
    return r * ng - v * (r * r * r) * jnp.mean(ng * v, axis=-1, keepdims=True), n * v * r


def gelu_parts(a):
    c = math.sqrt(2 / math.pi)
    t = jnp.tanh(c * (a + 0.044715 * a * a * a))
    half = 0.5 * (1 + t)
    return half * a, half + 0.5 * a * (1 - t * t) * c * (1 + 3 * 0.044715 * a * a)


def place():
    return lax.axis_index("mp"), lax.axis_index("dp"), lax.axis_index("rep")


def peer(k):
    m, z, r = place()
    return (m ^ k, z, r)


def partner():
    m, z, r = place()
    return (m, z, 1 - r)


def level(k):
    m, z, r = place()
    return (m, z ^ k, r)


def greet(zin):
    barrier = pltpu.get_barrier_semaphore()
    known = [peer(k) for k in range(1, WAYS)] + [partner()]
    if zin:
        known += [level(k) for k in range(1, LEVELS)]
    for one in known:
        pl.semaphore_signal(barrier, inc=1, device_id=one, device_id_type=MESH)
    pl.semaphore_wait(barrier, len(known))


def send(src, dst, sems, at, to):
    return pltpu.make_async_remote_copy(
        src_ref=src, dst_ref=dst, send_sem=sems[0].at[at], recv_sem=sems[1].at[at], device_id=to, device_id_type=MESH
    )


def run_kernel(name, phases, ins, outs, scratch, cid, flops=0):
    names = list(ins) + list(outs) + list(scratch)

    def body(*refs):
        held = types.SimpleNamespace(**dict(zip(names, refs)))
        for phase in phases:
            phase(held)

    got = pl.pallas_call(
        body,
        name=name,
        out_shape=[jax.ShapeDtypeStruct(shape, dtype) for shape, dtype, _ in outs.values()],
        in_specs=[pl.BlockSpec(memory_space=space) for _, space in ins.values()],
        out_specs=[pl.BlockSpec(memory_space=space) for _, _, space in outs.values()],
        scratch_shapes=list(scratch.values()),
        compiler_params=pltpu.CompilerParams(
            collective_id=cid, has_side_effects=True, vmem_limit_bytes=VMEM_BYTES
        ),
        cost_estimate=pl.CostEstimate(flops=flops, bytes_accessed=flops // 200, transcendentals=0),
    )(*[array for array, _ in ins.values()])
    return dict(zip(outs, got))


V, ANY, SM = pltpu.VMEM, pl.ANY, pltpu.SMEM


def dma(*shape):
    return pltpu.SemaphoreType.DMA(shape)


def aligned(start, size):
    return pl.ds(pl.multiple_of(start, size), size)


def start_sends(R):
    m, z, r = place()
    quarter = R.mem.shape[1]
    sh = R.wa.shape[1]
    half = sh // 2
    greet(R.zin)
    own = pltpu.make_async_copy(R.mem.at[m], R.memf.at[aligned(m * quarter, quarter)], R.l_sem.at[0])
    own.start()
    mine = pltpu.make_async_copy(R.wa, R.waf.at[:, aligned(m * sh, sh)], R.l_sem.at[1])
    mine.start()
    R.local = [own, mine]
    R.mem_copies, R.wa_copies, R.fw_copies, R.cot_copies = {}, {}, {}, {}
    rows = aligned(m * quarter, quarter)
    for k in range(1, WAYS):
        copy = send(R.mem.at[m ^ k], R.memf.at[rows], (R.mem_s, R.mem_r), k, peer(k))
        copy.start()
        R.mem_copies[k] = copy
    rows = pl.ds(m * sh + r * half, half)
    for part, (lo, n) in enumerate(PARTS):
        for k in range(1, WAYS):
            copy = send(
                R.wa.at[pl.ds(lo, n), aligned(r * half, half)],
                R.waf.at[pl.ds(lo, n), rows],
                (R.wa_s, R.wa_r),
                part * WAYS + k,
                peer(k),
            )
            copy.start()
            R.wa_copies[part, k] = copy


def send_cot(R):
    m, z, r = place()
    tc = R.cot.shape[1]
    rows = aligned(m * tc, tc)
    own = pltpu.make_async_copy(R.cot, R.upall.at[:, rows], R.l_sem.at[2])
    own.start()
    R.local.append(own)
    for k in range(1, WAYS):
        copy = send(R.cot, R.upall.at[:, rows], (R.cot_s, R.cot_r), k, peer(k))
        copy.start()
        R.cot_copies[k] = copy


def forward(R, part):
    m, z, r = place()
    sh = R.wa.shape[1]
    half = sh // 2
    lo, n = PARTS[part]
    for k in range(1, WAYS):
        R.wa_copies[part, k].wait_recv()
        view = R.waf.at[pl.ds(lo, n), pl.ds((m ^ k) * sh + r * half, half)]
        copy = send(view, view, (R.fw_s, R.fw_r), part * WAYS + k, partner())
        copy.start()
        R.fw_copies[part, k] = copy


def self_allowed(R, s):
    T = R.st.shape[1]
    j = lax.broadcasted_iota(jnp.int32, (T, T), 0)
    i = lax.broadcasted_iota(jnp.int32, (T, T), 1)
    return (j == i) | ((j < i) & (R.mask[s] != 0))


def toeplitz(R, h):
    T = R.st.shape[1]
    rows = jnp.broadcast_to(R.vec[h], (T, T))
    return pltpu.roll(rows, 0, 1, stride=1, stride_axis=0)


def only_head(rows, h, heads):
    zero = jnp.zeros(rows.shape, rows.dtype)
    return jnp.concatenate([rows if g == h else zero for g in range(heads)], axis=0)


def self_scores(R, s, h, allowed):
    heads = R.vec.shape[0]
    hd = R.qs.shape[1] // heads
    rows = slice(h * hd, (h + 1) * hd)
    scores = nn(R.ks[s], only_head(R.qs[s, rows], h, heads)) + R.et[h]
    return jnp.where(allowed, scores, NEG)


def self_forward(R):
    m, z, r = place()
    HW = R.ws.shape[0] // 3
    heads = R.vec.shape[0]
    hd = HW // heads
    for h in range(heads):
        R.et[h] = toeplitz(R, h)

    def one(s):
        normed = rms(R.st[s].astype(F32), R.g_self[...]).astype(BF)
        R.qs[s] = nt(R.ws[0:HW], normed).astype(BF)
        R.ks[s] = nt(normed, R.ws[HW : 2 * HW]).astype(BF)
        R.kts[s] = nt(R.ws[HW : 2 * HW], normed).astype(BF)
        R.vts[s] = nt(R.ws[2 * HW : 3 * HW], normed).astype(BF)
        R.vs[s] = nt(normed, R.ws[2 * HW : 3 * HW]).astype(BF)
        allowed = self_allowed(R, s)
        for h in range(heads):
            rows = slice(h * hd, (h + 1) * hd)
            scores = self_scores(R, s, h, allowed)
            top = jnp.max(scores, axis=0, keepdims=True)
            weights = jnp.exp(scores - top)
            total = jnp.sum(weights, axis=0, keepdims=True)
            R.atp[s, rows] = (nn(R.vts[s, rows], weights.astype(BF)) * (1 / total)).astype(BF)
            R.lse_s[s, h] = top + jnp.log(total)

    def step(k, carry):
        one(m ^ k)
        att_copy(R, k).start()
        return carry

    lax.fori_loop(1, WAYS, step, 0)
    one(m)
    R.att[aligned(m * HW, HW)] = R.atp[m]


def att_copy(R, k):
    m, z, r = place()
    HW = R.ws.shape[0] // 3
    return send(R.atp.at[m ^ k], R.att.at[aligned(m * HW, HW)], (R.att_s, R.att_r), k, peer(k))


def cross_kv(R):
    for copy in R.local:
        copy.wait()
    for copy in R.mem_copies.values():
        copy.wait()
    for k in range(1, WAYS):
        R.wa_copies[0, k].wait_send()
        R.fw_copies[0, k].wait()
    M = R.memf.shape[0]
    step = 256

    def rows(i, carry):
        at = aligned(i * step, step)
        block = R.memf[at]
        k = nt(block, R.waf[CK]).astype(BF)
        R.kc[at] = k
        v = nt(block, R.waf[CV]).astype(BF)
        R.vc[at] = v
        R.kct[:, at] = k.T
        R.vct[:, at] = v.T
        return carry

    lax.fori_loop(0, M // step, rows, 0)


def after_self(R):
    m, z, r = place()
    for k in range(1, WAYS):
        att_copy(R, k).wait()
    for k in range(1, WAYS):
        R.wa_copies[1, k].wait_send()
        R.fw_copies[1, k].wait()
    first = R.st[m].astype(F32) + tn(R.att[...], R.waf[SO])
    R.sg[...] = first
    normed = rms(first, R.g_cross[...]).astype(BF)
    R.nc[...] = normed
    R.qc[...] = nt(R.waf[CQ], normed).astype(BF)


def padded_head(ref, p, a, hd):
    rows = ref[aligned(p * 2 * hd + a * hd, hd)]
    zero = jnp.zeros(rows.shape, rows.dtype)
    return jnp.concatenate([rows, zero] if a == 0 else [zero, rows], axis=0)


def cross_scores(R, p, a, hd):
    m, z, r = place()
    M, T = R.memf.shape[0], R.qc.shape[1]
    scores = nn(R.kc[:, aligned(p * 2 * hd, 2 * hd)], padded_head(R.qc, p, a, hd))
    live = lax.broadcasted_iota(jnp.int32, (M, T), 0) < R.lens[m]
    return jnp.where(live, scores, NEG)


def cross_forward(R):
    hd = R.ws.shape[0] // 3 // R.vec.shape[0]
    heads = R.qc.shape[0] // hd

    def pair(p, carry):
        for a in range(2):
            rows = aligned(p * 2 * hd + a * hd, hd)
            scores = cross_scores(R, p, a, hd)
            top = jnp.max(scores, axis=0, keepdims=True)
            weights = jnp.exp(scores - top)
            total = jnp.sum(weights, axis=0, keepdims=True)
            R.attc[rows] = (nn(R.vct[rows], weights.astype(BF)) * (1 / total)).astype(BF)
            R.lse_c[2 * p + a] = top + jnp.log(total)
        return carry

    lax.fori_loop(0, heads // 2, pair, 0)


def nf_copy(R, k):
    m, z, r = place()
    return send(R.nall.at[m], R.nall.at[m], (R.nf_s, R.nf_r), k, peer(k))


def second_part(R):
    m, z, r = place()
    second = R.sg[...] + tn(R.attc[...], R.waf[CO])
    R.second[...] = second
    R.nall[m] = rms(second, R.g_ffn[...]).astype(BF)
    for k in range(1, WAYS):
        nf_copy(R, k).start()
    for copy in R.cot_copies.values():
        copy.wait()


def ng_copy(R, k):
    m, z, r = place()
    return send(R.part.at[m ^ k], R.ngr.at[k - 1], (R.ng_s, R.ng_r), k, peer(k))


def br_copy(R, k):
    m, z, r = place()
    tc = R.br.shape[2]
    return send(R.brp.at[:, aligned((m ^ k) * tc, tc)], R.br.at[k], (R.br_s, R.br_r), k, peer(k))


def feed_forward(R):
    m, z, r = place()
    T = R.st.shape[1]
    F = R.down.shape[0]

    def one(s, extra):
        rows = aligned(s * T, T)
        n, up = R.nall[s], R.upall[s]
        gate, lift = nn(n, R.gate[...]), nn(n, R.up[...])
        value, slope = gelu_parts(gate)
        hidden = (value * lift).astype(BF)
        R.hid[rows] = hidden
        back = nt(up, R.down[...])
        gate_grad = (back * lift * slope).astype(BF)
        up_grad = (back * value).astype(BF)
        R.gu[rows, 0:F] = gate_grad
        R.gu[rows, F : 2 * F] = up_grad
        R.part[s] = (nt(gate_grad, R.gate[...]) + nt(up_grad, R.up[...])).astype(BF)
        branch = nn(hidden, R.down[...])
        R.brp[s] = (branch + R.second[...] if extra else branch).astype(BF)

    one(m, True)

    def step(k, carry):
        nf_copy(R, k).wait_recv()
        one(m ^ k, False)
        ng_copy(R, k).start()
        return carry

    lax.fori_loop(1, WAYS, step, 0)
    for k in range(1, WAYS):
        br_copy(R, k).start()
    tc = R.br.shape[2]
    own = pltpu.make_async_copy(R.brp.at[:, aligned(m * tc, tc)], R.br.at[0], R.l_sem.at[0])
    own.start()
    R.local = [own]
    for k in range(1, WAYS):
        nf_copy(R, k).wait_send()


def ffn_grads(R):
    W, T, D = R.nall.shape
    F = R.down.shape[0]
    rows = R.nall[...].reshape(W * T, D)
    both = tn(rows, R.gu[...]).astype(BF)
    R.gg[:, 0] = both[:, 0:F].reshape(2, LEVELS, D // 2 // LEVELS, F)
    R.gg[:, 1] = both[:, F : 2 * F].reshape(2, LEVELS, D // 2 // LEVELS, F)
    R.gd[...] = tn(R.hid[...], R.upall[...].reshape(W * T, D)).astype(BF).reshape(2, LEVELS, F // 2 // LEVELS, D)


def core_start(R, name):
    m, z, r = place()
    source, sems = getattr(R, name), (getattr(R, name + "_cs"), getattr(R, name + "_cr"))
    copy = send(source.at[1 - r], getattr(R, name + "_c"), sems, 0, partner())
    copy.start()
    R.core[name] = copy


def core_sum(R, name):
    m, z, r = place()
    R.core[name].wait()
    source, other = getattr(R, name), getattr(R, name + "_c")
    source[r] = (source[r].astype(F32) + other[...].astype(F32)).astype(BF)


def chunk(ref, j):
    return ref.at[j] if len(ref.shape) == 3 else ref.at[:, j]


def halves(R, name):
    m, z, r = place()
    whole, spare = getattr(R, name).at[r], getattr(R, name + "_c")
    return (spare, whole) if name == "cr" else (whole, spare)


def level_copy(R, name, k):
    m, z, r = place()
    sems = (getattr(R, name + "_zs"), getattr(R, name + "_zr"))
    return send(chunk(halves(R, name)[0], z ^ k), getattr(R, name + "_x").at[k - 1], sems, k, level(k))


def spread_copy(R, name, k):
    m, z, r = place()
    sems = (getattr(R, name + "_as"), getattr(R, name + "_ar"))
    mine = chunk(halves(R, name)[1], z)
    return send(mine, mine, sems, k, level(k))


def level_start(R, name):
    if R.zin:
        for k in range(1, LEVELS):
            level_copy(R, name, k).start()


def level_sum(R, name):
    m, z, r = place()
    before, after = halves(R, name)
    if not R.zin:
        after[...] = before[...]
        return
    for k in range(1, LEVELS):
        level_copy(R, name, k).wait()
    total = chunk(before, z)[...].astype(F32)
    for k in range(1, LEVELS):
        total = total + getattr(R, name + "_x")[k - 1].astype(F32)
    chunk(after, z)[...] = total.astype(BF)
    for k in range(1, LEVELS):
        spread_copy(R, name, k).start()


def last_copy(R, name):
    m, z, r = place()
    mine = halves(R, name)[1]
    return send(mine, getattr(R, name).at[r], (getattr(R, name + "_cs"), getattr(R, name + "_cr")), 1, partner())


def last_start(R, name):
    m, z, r = place()
    if R.zin:
        for k in range(1, LEVELS):
            spread_copy(R, name, k).wait()
    last_copy(R, name).start()
    if name != "cr":
        getattr(R, name)[r] = getattr(R, name + "_c")[...]


def wg_core(R, i):
    m, z, r = place()
    return send(R.wg.at[i, :, 1 - r], R.wgc.at[i], (R.wgc_s, R.wgc_r), i, partner())


def wg_peer(R, i, k):
    m, z, r = place()
    return send(R.wg.at[i, m ^ k, r], R.wgr.at[k - 1, i], (R.wg_s, R.wg_r), WAYS * i + k, peer(k))


def put_grad(R, i, value):
    D = value.shape[0]
    R.wg[i] = value.astype(BF).reshape(WAYS, 2, D // WAYS // 2, D)
    wg_core(R, i).start()


def wg_spread(R, i):
    m, z, r = place()
    wg_core(R, i).wait()
    for s in range(WAYS):
        R.wg[i, s, r] = (R.wg[i, s, r].astype(F32) + R.wgc[i, s].astype(F32)).astype(BF)
    for k in range(1, WAYS):
        wg_peer(R, i, k).start()


def wg_collect(R):
    m, z, r = place()
    half = R.wgr.shape[2]
    n = R.cr.shape[2]
    flat = []
    for i in range(5):
        for k in range(1, WAYS):
            wg_peer(R, i, k).wait()
        total = R.wg[i, m, r].astype(F32)
        for k in range(1, WAYS):
            total = total + R.wgr[k - 1, i].astype(F32)
        flat.append(total.astype(BF))
    flat.append(jnp.zeros((LEVELS * n - 5 * half, flat[0].shape[1]), BF))
    R.cr_c[...] = jnp.concatenate(flat, axis=0).reshape(LEVELS, n, flat[0].shape[1])


def second_back(R):
    m, z, r = place()
    for k in range(1, WAYS):
        ng_copy(R, k).wait()
    grad = R.part[m].astype(F32)
    for k in range(1, WAYS):
        grad = grad + R.ngr[k - 1].astype(F32)
    back, gain = rms_back(R.second[...], R.g_ffn[...], grad)
    R.sm[...] = jnp.zeros(R.sm.shape, F32)
    R.sm[2:3] = jnp.sum(gain, axis=0, keepdims=True)
    total = R.upall[m].astype(F32) + back
    R.second[...] = total
    low = total.astype(BF)
    R.dot[...] = nt(R.waf[CO], low).astype(BF)
    put_grad(R, CO, nn(R.attc[...], low))


def cross_back(R, lo, hi):
    hd = R.ws.shape[0] // 3 // R.vec.shape[0]

    def pair(p, carry):
        lanes = aligned(p * 2 * hd, 2 * hd)
        for a in range(2):
            rows = aligned(p * 2 * hd + a * hd, hd)
            mix = jnp.exp(cross_scores(R, p, a, hd) - R.lse_c[2 * p + a])
            value_grad = nt(R.dot[rows], mix.astype(BF)).astype(BF)
            grad = nn(R.vc[:, lanes], padded_head(R.dot, p, a, hd))
            delta = jnp.sum(mix * grad, axis=0, keepdims=True)
            score_grad = (mix * (grad - delta)).astype(BF)
            R.attc[rows] = nn(R.kct[rows], score_grad).astype(BF)
            R.kct[rows] = value_grad
            R.vct[rows] = nt(R.qc[rows], score_grad).astype(BF)
        return carry

    lax.fori_loop(lo, hi, pair, 0)


def do_copy(R, k):
    m, z, r = place()
    HW = R.ws.shape[0] // 3
    return send(R.dot.at[aligned((m ^ k) * HW, HW)], R.atp.at[m], (R.do_s, R.do_r), k, peer(k))


def fg_copy(R, k):
    m, z, r = place()
    tc = R.fgr.shape[1]
    return send(R.fgb.at[aligned((m ^ k) * tc, tc)], R.fgr.at[m], (R.fg_s, R.fg_r), k, peer(k))


def first_back(R):
    m, z, r = place()
    HW = R.ws.shape[0] // 3
    tc = R.fgr.shape[1]
    back, gain = rms_back(R.sg[...], R.g_cross[...], tn(R.attc[...], R.waf[CQ]))
    R.sm[1:2] = jnp.sum(gain, axis=0, keepdims=True)
    low = (R.second[...] + back).astype(BF)
    R.fgb[...] = low
    R.dot[...] = nt(R.waf[SO], low).astype(BF)
    for k in range(1, WAYS):
        do_copy(R, k).start()
    for k in range(1, WAYS):
        fg_copy(R, k).start()
    R.atp[m] = R.dot[aligned(m * HW, HW)]
    R.fgr[m] = R.fgb[aligned(m * tc, tc)]
    put_grad(R, CQ, nn(R.attc[...], R.nc[...]))
    put_grad(R, SO, nn(R.att[...], low))


def mg_copy(R, k):
    m, z, r = place()
    quarter = R.mem.shape[1]
    return send(R.vc.at[aligned((m ^ k) * quarter, quarter)], R.mgo.at[m], (R.mg_s, R.mg_r), k, peer(k))


def memory_back(R):
    m, z, r = place()
    quarter = R.mem.shape[1]

    def rows(c):
        at = aligned(c * quarter, quarter)
        R.vc[at] = (tn(R.vct[:, at], R.waf[CK]) + tn(R.kct[:, at], R.waf[CV])).astype(BF)

    def step(k, carry):
        rows(m ^ k)
        mg_copy(R, k).start()
        return carry

    lax.fori_loop(1, WAYS, step, 0)
    rows(m)
    own = pltpu.make_async_copy(R.vc.at[aligned(m * quarter, quarter)], R.mgo.at[m], R.l_sem.at[1])
    own.start()
    R.local.append(own)


def kv_grads(R):
    put_grad(R, CK, nn(R.vct[...], R.memf[...]))
    put_grad(R, CV, nn(R.kct[...], R.memf[...]))


def ns_copy(R, k, kk):
    m, z, r = place()
    tc = R.fgr.shape[1]
    s = m ^ k
    return send(
        R.part.at[s, aligned((m ^ kk) * tc, tc)], R.nsr.at[kk - 1, s], (R.ns_s, R.ns_r), WAYS * k + kk, peer(kk)
    )


def ns_arrival(R, k, kk):
    m, z, r = place()
    tc = R.fgr.shape[1]
    s = m ^ kk ^ k
    return send(R.part.at[s, aligned(m * tc, tc)], R.nsr.at[kk - 1, s], (R.ns_s, R.ns_r), WAYS * k + kk, peer(kk))


def self_back(R):
    m, z, r = place()
    T = R.st.shape[1]
    HW = R.ws.shape[0] // 3
    heads = R.vec.shape[0]
    hd = HW // heads
    R.wsg[...] = jnp.zeros(R.wsg.shape, F32)
    R.dsum[...] = jnp.zeros(R.dsum.shape, F32)

    def one(k):
        s = m ^ k
        allowed = self_allowed(R, s)
        for h in range(heads):
            rows = slice(h * hd, (h + 1) * hd)
            mix = jnp.exp(self_scores(R, s, h, allowed) - R.lse_s[s, h])
            out = R.atp[s, rows]
            grad = nn(R.vs[s], only_head(out, h, heads))
            delta = jnp.sum(mix * grad, axis=0, keepdims=True)
            score_grad = (mix * (grad - delta)).astype(BF)
            R.dsum[h] += score_grad.astype(F32)
            R.dqkv[h * hd : (h + 1) * hd] = nn(R.kts[s, rows], score_grad).astype(BF)
            R.dqkv[HW + h * hd : HW + (h + 1) * hd] = nt(R.qs[s, rows], score_grad).astype(BF)
            R.dqkv[2 * HW + h * hd : 2 * HW + (h + 1) * hd] = nt(out, mix.astype(BF)).astype(BF)
        values = R.st[s].astype(F32)
        scaled = values * lax.rsqrt(jnp.mean(values * values, axis=-1, keepdims=True) + eps)
        normed = (scaled * R.g_self[...]).astype(BF)
        R.wsg[...] += nn(R.dqkv[...], normed)
        grad = tn(R.dqkv[...], R.ws[...])
        R.sm[0:1] += jnp.sum(grad * scaled, axis=0, keepdims=True)
        R.part[s] = grad.astype(BF)
        for kk in range(1, WAYS):
            ns_copy(R, k, kk).start()

    one(0)

    def step(k, carry):
        do_copy(R, k).wait()
        one(k)
        return carry

    lax.fori_loop(1, WAYS, step, 0)
    n = R.se.shape[2]
    rows = 3 * HW // 2
    for half in range(2):
        low = R.wsg[half * rows : (half + 1) * rows].astype(BF)
        pad = jnp.zeros((LEVELS * n - rows, low.shape[1]), BF)
        R.se[half] = jnp.concatenate([low, pad], axis=0).reshape(LEVELS, n, low.shape[1])


def distance_sums(R):
    heads, T, _ = R.dsum.shape
    j = lax.broadcasted_iota(jnp.int32, (T, T), 0)
    for h in range(heads):
        rows = R.dsum[h]
        bit = 1
        while bit < T:
            rows = jnp.where((j & bit) != 0, pltpu.roll(rows, T - bit, 1), rows)
            bit *= 2
        R.sm[3:4, h * T : (h + 1) * T] = jnp.sum(rows, axis=0, keepdims=True)


def states_back(R):
    m, z, r = place()
    W, tc, D = R.fgr.shape
    for k in range(WAYS):
        for kk in range(1, WAYS):
            ns_copy(R, k, kk).wait_send()
            ns_arrival(R, k, kk).wait_recv()
    for k in range(1, WAYS):
        fg_copy(R, k).wait()
    for s in range(W):
        grad = R.part[s, aligned(m * tc, tc)].astype(F32)
        for kk in range(1, WAYS):
            grad = grad + R.nsr[kk - 1, s].astype(F32)
        values = R.st[s, aligned(m * tc, tc)].astype(F32)
        back, _ = rms_back(values, R.g_self[...], grad)
        R.sg[s * tc : (s + 1) * tc] = R.fgr[s].astype(F32) + back


def small_sums(R, step):
    m, z, r = place()
    if step == 0:
        R.sm_copies = [send(R.sm, R.smr.at[k - 1], (R.sm_s, R.sm_r), k, peer(k)) for k in range(1, WAYS)]
    elif step == 1:
        total = R.sm[...]
        gains = lax.broadcasted_iota(jnp.int32, total.shape, 0) < 3
        for k in range(1, WAYS):
            total = total + jnp.where(gains, R.smr[k - 1], 0)
        R.sm2[...] = total
        R.sm_copies = [send(R.sm2, R.smr.at[3], (R.sm_s, R.sm_r), 4, partner())]
    elif step == 2:
        R.sm3[...] = R.sm2[...] + R.smr[3]
        R.sm_copies = []
        if R.zin:
            R.sm_copies = [
                send(R.sm3, R.smr.at[3 + k], (R.sm_s, R.sm_r), 4 + k, level(k)) for k in range(1, LEVELS)
            ]
    else:
        total = R.sm3[...]
        if R.zin:
            for k in range(1, LEVELS):
                total = total + R.smr[3 + k]
        R.smo[...] = total
        return
    for copy in R.sm_copies:
        copy.start()


def small_wait(R):
    for copy in R.sm_copies:
        copy.wait()


def whole_phase(R):
    start_sends(R)
    self_forward(R)
    send_cot(R)
    forward(R, 0)
    cross_kv(R)
    forward(R, 1)
    after_self(R)
    cross_forward(R)
    second_part(R)
    feed_forward(R)
    R.core = {}
    ffn_grads(R)
    core_start(R, "gg")
    core_start(R, "gd")
    second_back(R)
    heads = R.lse_c.shape[0]
    cross_back(R, 0, 1)
    core_sum(R, "gg")
    core_sum(R, "gd")
    level_start(R, "gg")
    level_start(R, "gd")
    wg_spread(R, CO)
    cross_back(R, 1, heads // 2)
    first_back(R)
    for k in range(1, WAYS):
        br_copy(R, k).wait()
    memory_back(R)
    level_sum(R, "gg")
    level_sum(R, "gd")
    wg_spread(R, CQ)
    wg_spread(R, SO)
    kv_grads(R)
    self_back(R)
    core_start(R, "se")
    wg_spread(R, CK)
    wg_spread(R, CV)
    distance_sums(R)
    small_sums(R, 0)
    last_start(R, "gg")
    last_start(R, "gd")
    core_sum(R, "se")
    level_start(R, "se")
    small_wait(R)
    small_sums(R, 1)
    wg_collect(R)
    level_start(R, "cr")
    small_wait(R)
    small_sums(R, 2)
    states_back(R)
    level_sum(R, "se")
    level_sum(R, "cr")
    small_wait(R)
    small_sums(R, 3)
    last_start(R, "se")
    last_start(R, "cr")
    for copy in R.local:
        copy.wait()
    for k in range(1, WAYS):
        mg_copy(R, k).wait()
    for name in ("gg", "gd", "se", "cr"):
        last_copy(R, name).wait()


def per_device(states, memory, target_mask, memory_length, norm_self, self_query, self_key, self_value, self_out,
               bias_table, norm_cross, cross_query, cross_key, cross_value, cross_out, norm_ffn, ffn_gate, ffn_up,
               ffn_down, cotangent):
    ways = WAYS
    zin = lax.axis_size("dp") == LEVELS
    T, _, D = states.shape
    HW = self_query.shape[1]
    HC = bias_table.shape[1]
    F = ffn_gate.shape[1]
    hd = HW // HC
    M = memory.shape[0] * ways
    heads = D // hd
    st = jnp.transpose(states, (1, 0, 2))
    mem = jnp.transpose(memory, (1, 0, 2))
    cot = jnp.transpose(cotangent, (1, 0, 2))
    ws = jnp.concatenate([self_query.T, self_key.T, self_value.T], axis=0)
    wa = jnp.stack([cross_key.T, cross_value.T, self_out, cross_query.T, cross_out])
    pos = jnp.arange(T, dtype=jnp.int32)
    vec = jnp.take(bias_table, bucket_of(pos), axis=0).T[:, None]
    ins = dict(
        st=(st, V), mem=(mem, ANY), ws=(ws, V), wa=(wa, ANY), mask=(target_mask[:, :, None], V), vec=(vec, V),
        lens=(memory_length, SM), g_self=(norm_self[None], V), g_cross=(norm_cross[None], V), g_ffn=(norm_ffn[None], V),
        cot=(cot, ANY), gate=(ffn_gate, V), up=(ffn_up, V), down=(ffn_down, V),
    )
    half = HW // 2
    n2 = -(-5 * half // (16 * LEVELS)) * 16
    n3 = -(-3 * half // (16 * LEVELS)) * 16
    tc = T // ways
    outs = dict(
        br=((ways, ways, tc, D), BF, ANY), mgo=((ways, M // ways, D), BF, ANY), sg=((T, D), F32, V),
        gg=((2, 2, LEVELS, D // 2 // LEVELS, F), BF, V), gd=((2, LEVELS, F // 2 // LEVELS, D), BF, V),
        cr=((2, LEVELS, n2, D), BF, V), se=((2, LEVELS, n3, D), BF, V), smo=((8, D), F32, V),
    )
    scratch = dict(
        att=V((D, T), BF), qs=V((ways, HW, T), BF), ks=V((ways, T, HW), BF), kts=V((ways, HW, T), BF),
        vts=V((ways, HW, T), BF), vs=V((ways, T, HW), BF), lse_s=V((ways, HC, 1, T), F32),
        second=V((T, D), F32), nc=V((T, D), BF), qc=V((D, T), BF), kc=V((M, D), BF), kct=V((D, M), BF),
        vc=V((M, D), BF), vct=V((D, M), BF), lse_c=V((heads, 1, T), F32), attc=V((D, T), BF), memf=V((M, D), BF),
        waf=V((5, D, D), BF), nall=V((ways, T, D), BF), upall=V((ways, T, D), BF), et=V((HC, T, T), F32),
        atp=V((ways, HW, T), BF), part=V((ways, T, D), BF), ngr=V((3, T, D), BF), brp=V((ways, T, D), BF),
        hid=V((ways * T, F), BF), gu=V((ways * T, 2 * F), BF),
        gg_c=V((2, LEVELS, D // 2 // LEVELS, F), BF),
        gg_x=V((3, 2, D // 2 // LEVELS, F), BF),
        gd_c=V((LEVELS, F // 2 // LEVELS, D), BF),
        gd_x=V((3, F // 2 // LEVELS, D), BF),
        cr_c=V((LEVELS, n2, D), BF), cr_x=V((3, n2, D), BF),
        se_c=V((LEVELS, n3, D), BF), se_x=V((3, n3, D), BF),
        wg=V((5, ways, 2, half, D), BF), wgc=V((5, ways, half, D), BF), wgr=V((3, 5, half, D), BF),
        dot=V((D, T), BF),
        fgb=V((T, D), BF), fgr=V((ways, tc, D), BF), nsr=V((3, ways, tc, D), BF), wsg=V((3 * HW, D), F32),
        dsum=V((HC, T, T), F32), dqkv=V((3 * HW, T), BF), sm=V((8, D), F32), sm2=V((8, D), F32), sm3=V((8, D), F32),
        smr=V((7, 8, D), F32), l_sem=dma(3),
    )
    for name, n in dict(mem=4, wa=8, fw=8, att=4, cot=4, nf=4, ng=4, br=4, do=4, fg=4, mg=4, ns=16, sm=8, wg=20, wgc=5).items():
        scratch[name + "_s"] = dma(n)
        scratch[name + "_r"] = dma(n)
    for name in ("gg", "gd", "se", "cr"):
        for kind, n in dict(cs=2, cr=2, zs=4, zr=4).items():
            scratch[name + "_" + kind] = dma(n)
        scratch[name + "_as"] = dma(4)
        scratch[name + "_ar"] = dma(4)
    def phase(R):
        R.zin = zin
        whole_phase(R)
    G = types.SimpleNamespace(**run_kernel("block", [phase], ins, outs, scratch, 0))
    block_out = jnp.transpose(jnp.sum(G.br.astype(F32), axis=0), (1, 0, 2)).astype(BF)
    memory_grad = jnp.transpose(G.mgo.astype(F32), (1, 0, 2))
    states_grad = jnp.transpose(G.sg.reshape(ways, tc, D), (1, 0, 2))
    sums = [x.astype(F32) for x in (G.gg, G.gd, G.cr, G.se, G.smo)]
    if not zin:
        sums = [lax.psum(x, "dp") for x in sums]
    gg, gd, cr, se, sm = sums
    gate_grad, up_grad = (gg[:, i].reshape(D, F) for i in range(2))
    down_grad = gd.reshape(F, D)
    cross = cr.reshape(2, -1, D)[:, : 5 * half].reshape(2, 5, half, D)
    cross = [cross[:, i].reshape(HW, D) for i in range(5)]
    own = se.reshape(2, -1, D)[:, : 3 * half].reshape(3, HW, D)
    onehot = (bucket_of(pos)[:, None] == jnp.arange(bias_table.shape[0])).astype(F32)
    bias_grad = jnp.einsum("hr,rk->kh", sm[3].reshape(HC, T), onehot, precision=lax.Precision.HIGHEST)
    return (block_out, states_grad, memory_grad, sm[0], own[0].T, own[1].T, own[2].T, cross[SO], bias_grad, sm[1],
            cross[CQ].T, cross[CK].T, cross[CV].T, cross[CO], sm[2], gate_grad, up_grad, down_grad)


def solution(mesh):
    seq = ("dp", "rep")
    col, row, tok = P(None, "mp"), P("mp", None), P("mp", seq, None)
    in_specs = (P(None, seq, None), tok, P(seq, None), P(seq), P(), col, col, col, row, col, P(), col, col, col, row,
                P(), col, col, row, tok)
    out_specs = (tok, tok, tok, P(), col, col, col, row, col, P(), col, col, col, row, P(), col, col, row)
    return jax.shard_map(per_device, mesh=mesh, in_specs=in_specs, out_specs=out_specs, check_vma=False)
```

```python
import math
import types

import jax
import jax.numpy as jnp
from jax import lax
from jax.experimental import pallas as pl
from jax.experimental.pallas import tpu as pltpu
from jax.sharding import PartitionSpec as P

eps = 1e-06
bucket_edges = [math.ceil(16 * 8 ** (level / 16)) for level in range(1, 16)]
BF = jnp.bfloat16
F32 = jnp.float32
NEG = -1e30
VMEM_BYTES = 64 * 2**20 - 2**17
MESH = pl.DeviceIdType.MESH
WAYS = 4
LEVELS = 4
CK, CV, SO, CQ, CO = range(5)
PARTS = ((0, 2), (2, 3))


def bucket_of(offset):
    edge_list = jnp.array(bucket_edges, dtype=jnp.int32)
    passed = jnp.sum((offset[..., None] >= edge_list).astype(jnp.int32), axis=-1)
    return jnp.minimum(offset, 16) + passed


def dots(a, b, ca, cb):
    return lax.dot_general(a, b, (((ca,), (cb,)), ((), ())), preferred_element_type=F32)


def nn(a, b):
    return dots(a, b, 1, 0)


def nt(a, b):
    return dots(a, b, 1, 1)


def tn(a, b):
    return dots(a, b, 0, 0)


def rms(v, g):
    return v * lax.rsqrt(jnp.mean(v * v, axis=-1, keepdims=True) + eps) * g


def rms_back(v, g, n):
    r = lax.rsqrt(jnp.mean(v * v, axis=-1, keepdims=True) + eps)
    ng = n * g
    return r * ng - v * (r * r * r) * jnp.mean(ng * v, axis=-1, keepdims=True), n * v * r


def gelu_parts(a):
    c = math.sqrt(2 / math.pi)
    t = jnp.tanh(c * (a + 0.044715 * a * a * a))
    half = 0.5 * (1 + t)
    return half * a, half + 0.5 * a * (1 - t * t) * c * (1 + 3 * 0.044715 * a * a)


def place():
    return lax.axis_index("mp"), lax.axis_index("dp"), lax.axis_index("rep")


def peer(k):
    m, z, r = place()
    return (m ^ k, z, r)


def partner():
    m, z, r = place()
    return (m, z, 1 - r)


def level(k):
    m, z, r = place()
    return (m, z ^ k, r)


def greet(zin):
    barrier = pltpu.get_barrier_semaphore()
    known = [peer(k) for k in range(1, WAYS)] + [partner()]
    known += [level(k) for k in ((1, 2) if zin else (1,))]
    for one in known:
        pl.semaphore_signal(barrier, inc=1, device_id=one, device_id_type=MESH)
    pl.semaphore_wait(barrier, len(known))


def send(src, dst, sems, at, to):
    return pltpu.make_async_remote_copy(
        src_ref=src, dst_ref=dst, send_sem=sems[0].at[at], recv_sem=sems[1].at[at], device_id=to, device_id_type=MESH
    )


def run_kernel(name, phases, ins, outs, scratch, cid, flops=0):
    names = list(ins) + list(outs) + list(scratch)

    def body(*refs):
        held = types.SimpleNamespace(**dict(zip(names, refs)))
        for phase in phases:
            phase(held)

    got = pl.pallas_call(
        body,
        name=name,
        out_shape=[jax.ShapeDtypeStruct(shape, dtype) for shape, dtype, _ in outs.values()],
        in_specs=[pl.BlockSpec(memory_space=space) for _, space in ins.values()],
        out_specs=[pl.BlockSpec(memory_space=space) for _, _, space in outs.values()],
        scratch_shapes=list(scratch.values()),
        compiler_params=pltpu.CompilerParams(
            collective_id=cid, has_side_effects=True, vmem_limit_bytes=VMEM_BYTES
        ),
        cost_estimate=pl.CostEstimate(flops=flops, bytes_accessed=flops // 200, transcendentals=0),
    )(*[array for array, _ in ins.values()])
    return dict(zip(outs, got))


V, ANY, SM = pltpu.VMEM, pl.ANY, pltpu.SMEM


def dma(*shape):
    return pltpu.SemaphoreType.DMA(shape)


def aligned(start, size):
    return pl.ds(pl.multiple_of(start, size), size)


def start_sends(R):
    m, z, r = place()
    quarter = R.mem.shape[1]
    HW = R.ck.shape[0]
    mine = aligned(m * HW, HW)
    R.own_w = [
        pltpu.make_async_copy(src, R.waf.at[i, mine], R.w_sem.at[i])
        for i, src in enumerate((R.ck, R.cv, R.so, R.cq, R.co))
    ]
    for copy in R.own_w:
        copy.start()
    R.own_s = [
        pltpu.make_async_copy(src, R.ws.at[pl.ds(i * HW, HW)], R.w_sem.at[5 + i])
        for i, src in enumerate((R.wq, R.wk, R.wv))
    ]
    for copy in R.own_s:
        copy.start()
    R.local = [
        pltpu.make_async_copy(R.mem.at[m], R.memf.at[aligned(m * quarter, quarter)], R.l_sem.at[0]),
        pltpu.make_async_copy(R.gate_in, R.gate, R.w_sem.at[8]),
        pltpu.make_async_copy(R.up_in, R.up, R.w_sem.at[9]),
        pltpu.make_async_copy(R.down_in, R.down, R.w_sem.at[10]),
    ]
    for copy in R.local:
        copy.start()
    greet(R.zin)
    R.mem_copies, R.cot_copies = {}, {}
    rows = aligned(m * quarter, quarter)
    for k in range(1, WAYS):
        copy = send(R.mem.at[m ^ k], R.memf.at[rows], (R.mem_s, R.mem_r), k, peer(k))
        copy.start()
        R.mem_copies[k] = copy
    for copy in R.own_w:
        copy.wait()
    for part in range(len(PARTS)):
        for k in range(1, WAYS):
            wa_copy(R, part, k).start()


def quarter_rows(R, part, owner, core, half):
    HW = R.ck.shape[0]
    lo, n = PARTS[part]
    return R.waf.at[pl.ds(lo, n), aligned(owner * HW + core * (HW // 2) + half * (HW // 4), HW // 4)]


def wa_copy(R, part, k):
    m, z, r = place()
    view = quarter_rows(R, part, m, r, z & 1)
    return send(view, view, (R.wa_s, R.wa_r), part * WAYS + k, peer(k))


def fz_copy(R, part, k):
    m, z, r = place()
    view = quarter_rows(R, part, m ^ k, r, z & 1)
    return send(view, view, (R.fz_s, R.fz_r), part * WAYS + k, level(1))


def fw_copy(R, part, k, second):
    m, z, r = place()
    view = quarter_rows(R, part, m ^ k, r, (z & 1) ^ second)
    return send(view, view, (R.fw_s, R.fw_r), (second * 2 + part) * WAYS + k, partner())


def send_cot(R):
    m, z, r = place()
    tc = R.cot.shape[1]
    rows = aligned(m * tc, tc)
    R.own_cot = pltpu.make_async_copy(R.cot, R.upall.at[:, rows], R.l_sem.at[2])
    R.own_cot.start()
    for k in range(1, WAYS):
        copy = send(R.cot, R.upall.at[:, rows], (R.cot_s, R.cot_r), k, peer(k))
        copy.start()
        R.cot_copies[k] = copy


def forward(R, part):
    for k in range(1, WAYS):
        wa_copy(R, part, k).wait_recv()
        fz_copy(R, part, k).start()
        fw_copy(R, part, k, 0).start()


def forward_again(R, part):
    for k in range(1, WAYS):
        fz_copy(R, part, k).wait_recv()
        fw_copy(R, part, k, 1).start()


def gathered(R, part):
    for k in range(1, WAYS):
        wa_copy(R, part, k).wait_send()
        fz_copy(R, part, k).wait_send()
        fw_copy(R, part, k, 0).wait()
        fw_copy(R, part, k, 1).wait()


def self_allowed(R, s):
    T = R.st.shape[1]
    j = lax.broadcasted_iota(jnp.int32, (T, T), 0)
    i = lax.broadcasted_iota(jnp.int32, (T, T), 1)
    return (j == i) | ((j < i) & (R.mask[s] != 0))


def buckets(R, T):
    shape = (R.table.shape[0], T)
    distance = lax.broadcasted_iota(jnp.int32, shape, 1)
    bucket = jnp.minimum(distance, 16)
    for edge in bucket_edges:
        bucket = bucket + (distance >= edge).astype(jnp.int32)
    return bucket == lax.broadcasted_iota(jnp.int32, shape, 0)


def self_setup(R):
    W, T, _ = R.st.shape
    hit = buckets(R, T)
    for h in range(R.table.shape[1]):
        by_distance = jnp.sum(jnp.where(hit, R.table[:, h : h + 1], 0), axis=0, keepdims=True)
        R.et[h] = pltpu.roll(jnp.broadcast_to(by_distance, (T, T)), 0, 1, stride=1, stride_axis=0)
    for s in range(W):
        rows = jnp.broadcast_to(R.mask_in[s : s + 1].astype(F32), (T, T))
        R.mask[s] = rows.T[:, 0:1]
    for copy in R.own_s:
        copy.wait()


def only_head(rows, h, heads):
    zero = jnp.zeros(rows.shape, rows.dtype)
    return jnp.concatenate([rows if g == h else zero for g in range(heads)], axis=0)


def self_scores(R, s, h, allowed):
    heads = R.table.shape[1]
    hd = R.qs.shape[1] // heads
    rows = slice(h * hd, (h + 1) * hd)
    scores = nn(R.ks[s], only_head(R.qs[s, rows], h, heads)) + R.et[h]
    return jnp.where(allowed, scores, NEG)


def self_forward(R):
    m, z, r = place()
    HW = R.ws.shape[0] // 3
    heads = R.table.shape[1]
    hd = HW // heads
    self_setup(R)

    def one(s):
        normed = rms(R.st[s].astype(F32), R.g_self[...][None]).astype(BF)
        R.qs[s] = nt(R.ws[0:HW], normed).astype(BF)
        R.ks[s] = nt(normed, R.ws[HW : 2 * HW]).astype(BF)
        R.kts[s] = nt(R.ws[HW : 2 * HW], normed).astype(BF)
        R.vts[s] = nt(R.ws[2 * HW : 3 * HW], normed).astype(BF)
        R.vs[s] = nt(normed, R.ws[2 * HW : 3 * HW]).astype(BF)
        allowed = self_allowed(R, s)
        for h in range(heads):
            rows = slice(h * hd, (h + 1) * hd)
            scores = self_scores(R, s, h, allowed)
            top = jnp.max(scores, axis=0, keepdims=True)
            weights = jnp.exp(scores - top)
            total = jnp.sum(weights, axis=0, keepdims=True)
            R.atp[s, rows] = (nn(R.vts[s, rows], weights.astype(BF)) * (1 / total)).astype(BF)
            R.lse_s[s, h] = top + jnp.log(total)

    def step(k, carry):
        one(m ^ k)
        att_copy(R, k).start()
        return carry

    lax.fori_loop(1, WAYS, step, 0)
    one(m)
    R.att[aligned(m * HW, HW)] = R.atp[m]


def att_copy(R, k):
    m, z, r = place()
    HW = R.ws.shape[0] // 3
    return send(R.atp.at[m ^ k], R.att.at[aligned(m * HW, HW)], (R.att_s, R.att_r), k, peer(k))


def cross_kv(R):
    for copy in R.local:
        copy.wait()
    for copy in R.mem_copies.values():
        copy.wait()
    gathered(R, 0)
    M = R.memf.shape[0]
    step = 256

    def rows(i, carry):
        at = aligned(i * step, step)
        block = R.memf[at]
        k = nt(block, R.waf[CK]).astype(BF)
        R.kc[at] = k
        v = nt(block, R.waf[CV]).astype(BF)
        R.vc[at] = v
        R.kct[:, at] = k.T
        R.vct[:, at] = v.T
        return carry

    lax.fori_loop(0, M // step, rows, 0)


def after_self(R):
    m, z, r = place()
    for k in range(1, WAYS):
        att_copy(R, k).wait()
    gathered(R, 1)
    first = R.st[m].astype(F32) + tn(R.att[...], R.waf[SO])
    R.sg[...] = first
    normed = rms(first, R.g_cross[...][None]).astype(BF)
    R.nc[...] = normed
    R.qc[...] = nt(R.waf[CQ], normed).astype(BF)


def padded_head(ref, p, a, hd):
    rows = ref[aligned(p * 2 * hd + a * hd, hd)]
    zero = jnp.zeros(rows.shape, rows.dtype)
    return jnp.concatenate([rows, zero] if a == 0 else [zero, rows], axis=0)


def cross_scores(R, p, a, hd):
    m, z, r = place()
    M, T = R.memf.shape[0], R.qc.shape[1]
    scores = nn(R.kc[:, aligned(p * 2 * hd, 2 * hd)], padded_head(R.qc, p, a, hd))
    live = lax.broadcasted_iota(jnp.int32, (M, T), 0) < R.lens[m]
    return jnp.where(live, scores, NEG)


def cross_forward(R):
    hd = R.ws.shape[0] // 3 // R.table.shape[1]
    heads = R.qc.shape[0] // hd

    def pair(p, carry):
        for a in range(2):
            rows = aligned(p * 2 * hd + a * hd, hd)
            scores = cross_scores(R, p, a, hd)
            top = jnp.max(scores, axis=0, keepdims=True)
            weights = jnp.exp(scores - top)
            total = jnp.sum(weights, axis=0, keepdims=True)
            R.attc[rows] = (nn(R.vct[rows], weights.astype(BF)) * (1 / total)).astype(BF)
            R.lse_c[2 * p + a] = top + jnp.log(total)
        return carry

    lax.fori_loop(0, heads // 2, pair, 0)


def nf_copy(R, k):
    m, z, r = place()
    return send(R.nall.at[m], R.nall.at[m], (R.nf_s, R.nf_r), k, peer(k))


def second_part(R):
    m, z, r = place()
    second = R.sg[...] + tn(R.attc[...], R.waf[CO])
    R.second[...] = second
    R.nall[m] = rms(second, R.g_ffn[...][None]).astype(BF)
    for k in range(1, WAYS):
        nf_copy(R, k).start()
    R.own_cot.wait()
    for copy in R.cot_copies.values():
        copy.wait()


def ng_copy(R, k):
    m, z, r = place()
    return send(R.part.at[m ^ k], R.ngr.at[k - 1], (R.ng_s, R.ng_r), k, peer(k))


def br_copy(R, k):
    m, z, r = place()
    tc = R.br.shape[2]
    return send(R.brp.at[:, aligned((m ^ k) * tc, tc)], R.br.at[k], (R.br_s, R.br_r), k, peer(k))


def feed_forward(R):
    m, z, r = place()
    T = R.st.shape[1]
    F = R.down.shape[0]

    def one(s, extra):
        rows = aligned(s * T, T)
        n, up = R.nall[s], R.upall[s]
        gate, lift = nn(n, R.gate[...]), nn(n, R.up[...])
        value, slope = gelu_parts(gate)
        hidden = (value * lift).astype(BF)
        R.hid[rows] = hidden
        back = nt(up, R.down[...])
        gate_grad = (back * lift * slope).astype(BF)
        up_grad = (back * value).astype(BF)
        R.gu[rows, 0:F] = gate_grad
        R.gu[rows, F : 2 * F] = up_grad
        R.part[s] = (nt(gate_grad, R.gate[...]) + nt(up_grad, R.up[...])).astype(BF)
        branch = nn(hidden, R.down[...])
        R.brp[s] = (branch + R.second[...] if extra else branch).astype(BF)

    one(m, True)

    def step(k, carry):
        nf_copy(R, k).wait_recv()
        one(m ^ k, False)
        ng_copy(R, k).start()
        return carry

    lax.fori_loop(1, WAYS, step, 0)
    for k in range(1, WAYS):
        nf_copy(R, k).wait_send()


def ffn_grads(R):
    W, T, D = R.nall.shape
    F = R.down.shape[0]
    rows = R.nall[...].reshape(W * T, D)
    both = tn(rows, R.gu[...]).astype(BF)
    R.gg[:, 0] = both[:, 0:F].reshape(2, LEVELS, D // 2 // LEVELS, F)
    R.gg[:, 1] = both[:, F : 2 * F].reshape(2, LEVELS, D // 2 // LEVELS, F)
    R.gd[...] = tn(R.hid[...], R.upall[...].reshape(W * T, D)).astype(BF).reshape(2, LEVELS, F // 2 // LEVELS, D)


def core_start(R, name):
    m, z, r = place()
    source, sems = getattr(R, name), (getattr(R, name + "_cs"), getattr(R, name + "_cr"))
    copy = send(source.at[1 - r], getattr(R, name + "_c"), sems, 0, partner())
    copy.start()
    R.core[name] = copy


def core_sum(R, name):
    m, z, r = place()
    R.core[name].wait()
    source, other = getattr(R, name), getattr(R, name + "_c")
    source[r] = (source[r].astype(F32) + other[...].astype(F32)).astype(BF)


def chunk(ref, j):
    return ref.at[j] if len(ref.shape) == 3 else ref.at[:, j]


def halves(R, name):
    m, z, r = place()
    whole, spare = getattr(R, name).at[r], getattr(R, name + "_c")
    return (spare, whole) if name == "cr" else (whole, spare)


def level_copy(R, name, n):
    m, z, r = place()
    sems = (getattr(R, name + "_zs"), getattr(R, name + "_zr"))
    source = chunk(halves(R, name)[0], z ^ (1, 3, 2)[n])
    return send(source, getattr(R, name + "_x").at[n], sems, n, level((1, 1, 2)[n]))


def spread_copy(R, name, n):
    m, z, r = place()
    sems = (getattr(R, name + "_as"), getattr(R, name + "_ar"))
    mine = chunk(halves(R, name)[1], z ^ (0, 2, 0)[n])
    return send(mine, mine, sems, n, level((1, 1, 2)[n]))


def level_sum(R, name, step):
    m, z, r = place()
    before, after = halves(R, name)
    arrived = getattr(R, name + "_x")
    if not R.zin:
        if step == 0:
            after[...] = before[...]
        return
    if step == 0:
        level_copy(R, name, 0).start()
        level_copy(R, name, 1).start()
    elif step == 1:
        for n, to in ((1, z ^ 2), (0, z)):
            level_copy(R, name, n).wait()
            place_of = chunk(before, to)
            place_of[...] = (place_of[...].astype(F32) + arrived[n].astype(F32)).astype(BF)
            if n == 1:
                level_copy(R, name, 2).start()
    elif step == 2:
        level_copy(R, name, 2).wait()
        chunk(after, z)[...] = (chunk(before, z)[...].astype(F32) + arrived[2].astype(F32)).astype(BF)
        spread_copy(R, name, 2).start()
        spread_copy(R, name, 0).start()
    else:
        spread_copy(R, name, 2).wait()
        spread_copy(R, name, 1).start()


def last_copy(R, name):
    m, z, r = place()
    mine = halves(R, name)[1]
    return send(mine, getattr(R, name).at[r], (getattr(R, name + "_cs"), getattr(R, name + "_cr")), 1, partner())


def last_start(R, name):
    m, z, r = place()
    if R.zin:
        spread_copy(R, name, 0).wait()
        spread_copy(R, name, 1).wait()
    last_copy(R, name).start()
    if name != "cr":
        getattr(R, name)[r] = getattr(R, name + "_c")[...]


def wg_core(R, i):
    m, z, r = place()
    return send(R.wg.at[i, :, 1 - r], R.wgc.at[i], (R.wgc_s, R.wgc_r), i, partner())


def wg_peer(R, i, k):
    m, z, r = place()
    return send(R.wg.at[i, m ^ k, r], R.wgr.at[k - 1, i], (R.wg_s, R.wg_r), WAYS * i + k, peer(k))


def put_grad(R, i, value):
    D = value.shape[0]
    R.wg[i] = value.astype(BF).reshape(WAYS, 2, D // WAYS // 2, D)
    wg_core(R, i).start()


def wg_spread(R, i):
    m, z, r = place()
    wg_core(R, i).wait()
    for s in range(WAYS):
        R.wg[i, s, r] = (R.wg[i, s, r].astype(F32) + R.wgc[i, s].astype(F32)).astype(BF)
    for k in range(1, WAYS):
        wg_peer(R, i, k).start()


def wg_collect(R):
    m, z, r = place()
    half = R.wgr.shape[2]
    n = R.cr.shape[2]
    flat = []
    for i in range(5):
        for k in range(1, WAYS):
            wg_peer(R, i, k).wait()
        total = R.wg[i, m, r].astype(F32)
        for k in range(1, WAYS):
            total = total + R.wgr[k - 1, i].astype(F32)
        flat.append(total.astype(BF))
    flat.append(jnp.zeros((LEVELS * n - 5 * half, flat[0].shape[1]), BF))
    R.cr_c[...] = jnp.concatenate(flat, axis=0).reshape(LEVELS, n, flat[0].shape[1])


def second_back(R):
    m, z, r = place()
    tc = R.br.shape[2]
    for k in range(1, WAYS):
        ng_copy(R, k).wait()
    for k in range(1, WAYS):
        br_copy(R, k).start()
    own = pltpu.make_async_copy(R.brp.at[:, aligned(m * tc, tc)], R.br.at[0], R.l_sem.at[0])
    own.start()
    R.local = [own]
    grad = R.part[m].astype(F32)
    for k in range(1, WAYS):
        grad = grad + R.ngr[k - 1].astype(F32)
    back, gain = rms_back(R.second[...], R.g_ffn[...][None], grad)
    R.sm[...] = jnp.zeros(R.sm.shape, F32)
    R.sm[2:3] = jnp.sum(gain, axis=0, keepdims=True)
    total = R.upall[m].astype(F32) + back
    R.second[...] = total
    low = total.astype(BF)
    R.dot[...] = nt(R.waf[CO], low).astype(BF)
    put_grad(R, CO, nn(R.attc[...], low))


def cross_back(R, lo, hi):
    hd = R.ws.shape[0] // 3 // R.table.shape[1]

    def pair(p, carry):
        lanes = aligned(p * 2 * hd, 2 * hd)
        for a in range(2):
            rows = aligned(p * 2 * hd + a * hd, hd)
            mix = jnp.exp(cross_scores(R, p, a, hd) - R.lse_c[2 * p + a])
            value_grad = nt(R.dot[rows], mix.astype(BF)).astype(BF)
            grad = nn(R.vc[:, lanes], padded_head(R.dot, p, a, hd))
            delta = jnp.sum(mix * grad, axis=0, keepdims=True)
            score_grad = (mix * (grad - delta)).astype(BF)
            R.attc[rows] = nn(R.kct[rows], score_grad).astype(BF)
            R.kct[rows] = value_grad
            R.vct[rows] = nt(R.qc[rows], score_grad).astype(BF)
        return carry

    lax.fori_loop(lo, hi, pair, 0)


def do_copy(R, k):
    m, z, r = place()
    HW = R.ws.shape[0] // 3
    return send(R.dot.at[aligned((m ^ k) * HW, HW)], R.atp.at[m], (R.do_s, R.do_r), k, peer(k))


def fg_copy(R, k):
    m, z, r = place()
    tc = R.fgr.shape[1]
    return send(R.fgb.at[aligned((m ^ k) * tc, tc)], R.fgr.at[m], (R.fg_s, R.fg_r), k, peer(k))


def first_back(R):
    m, z, r = place()
    HW = R.ws.shape[0] // 3
    tc = R.fgr.shape[1]
    back, gain = rms_back(R.sg[...], R.g_cross[...][None], tn(R.attc[...], R.waf[CQ]))
    R.sm[1:2] = jnp.sum(gain, axis=0, keepdims=True)
    low = (R.second[...] + back).astype(BF)
    R.fgb[...] = low
    R.dot[...] = nt(R.waf[SO], low).astype(BF)
    for k in range(1, WAYS):
        do_copy(R, k).start()
    for k in range(1, WAYS):
        fg_copy(R, k).start()
    R.atp[m] = R.dot[aligned(m * HW, HW)]
    R.fgr[m] = R.fgb[aligned(m * tc, tc)]
    put_grad(R, CQ, nn(R.attc[...], R.nc[...]))
    put_grad(R, SO, nn(R.att[...], low))


def mg_copy(R, k):
    m, z, r = place()
    quarter = R.mem.shape[1]
    return send(R.vc.at[aligned((m ^ k) * quarter, quarter)], R.mgo.at[m], (R.mg_s, R.mg_r), k, peer(k))


def memory_back(R):
    m, z, r = place()
    quarter = R.mem.shape[1]

    def rows(c):
        at = aligned(c * quarter, quarter)
        R.vc[at] = (tn(R.vct[:, at], R.waf[CK]) + tn(R.kct[:, at], R.waf[CV])).astype(BF)

    lax.fori_loop(0, WAYS, lambda c, carry: (rows(c), carry)[1], 0)


def memory_send(R):
    m, z, r = place()
    quarter = R.mem.shape[1]
    for k in range(1, WAYS):
        mg_copy(R, k).start()
    own = pltpu.make_async_copy(R.vc.at[aligned(m * quarter, quarter)], R.mgo.at[m], R.l_sem.at[1])
    own.start()
    R.local.append(own)


def kv_grads(R):
    put_grad(R, CK, nn(R.vct[...], R.memf[...]))
    put_grad(R, CV, nn(R.kct[...], R.memf[...]))


def ns_copy(R, k, kk):
    m, z, r = place()
    tc = R.fgr.shape[1]
    s = m ^ k
    return send(
        R.part.at[s, aligned((m ^ kk) * tc, tc)], R.nsr.at[kk - 1, s], (R.ns_s, R.ns_r), WAYS * k + kk, peer(kk)
    )


def ns_arrival(R, k, kk):
    m, z, r = place()
    tc = R.fgr.shape[1]
    s = m ^ kk ^ k
    return send(R.part.at[s, aligned(m * tc, tc)], R.nsr.at[kk - 1, s], (R.ns_s, R.ns_r), WAYS * k + kk, peer(kk))


def self_back(R):
    m, z, r = place()
    T = R.st.shape[1]
    HW = R.ws.shape[0] // 3
    heads = R.table.shape[1]
    hd = HW // heads
    R.wsg[...] = jnp.zeros(R.wsg.shape, F32)
    R.dsum[...] = jnp.zeros(R.dsum.shape, F32)

    def one(k):
        s = m ^ k
        allowed = self_allowed(R, s)
        for h in range(heads):
            rows = slice(h * hd, (h + 1) * hd)
            mix = jnp.exp(self_scores(R, s, h, allowed) - R.lse_s[s, h])
            out = R.atp[s, rows]
            grad = nn(R.vs[s], only_head(out, h, heads))
            delta = jnp.sum(mix * grad, axis=0, keepdims=True)
            score_grad = (mix * (grad - delta)).astype(BF)
            R.dsum[h] += score_grad.astype(F32)
            R.dqkv[h * hd : (h + 1) * hd] = nn(R.kts[s, rows], score_grad).astype(BF)
            R.dqkv[HW + h * hd : HW + (h + 1) * hd] = nt(R.qs[s, rows], score_grad).astype(BF)
            R.dqkv[2 * HW + h * hd : 2 * HW + (h + 1) * hd] = nt(out, mix.astype(BF)).astype(BF)
        values = R.st[s].astype(F32)
        scaled = values * lax.rsqrt(jnp.mean(values * values, axis=-1, keepdims=True) + eps)
        normed = (scaled * R.g_self[...][None]).astype(BF)
        R.wsg[...] += nn(R.dqkv[...], normed)
        grad = tn(R.dqkv[...], R.ws[...])
        R.sm[0:1] += jnp.sum(grad * scaled, axis=0, keepdims=True)
        R.part[s] = grad.astype(BF)

    one(0)

    def step(k, carry):
        do_copy(R, k).wait()
        one(k)
        return carry

    lax.fori_loop(1, WAYS, step, 0)
    n = R.se.shape[2]
    rows = 3 * HW // 2
    for half in range(2):
        low = R.wsg[half * rows : (half + 1) * rows].astype(BF)
        pad = jnp.zeros((LEVELS * n - rows, low.shape[1]), BF)
        R.se[half] = jnp.concatenate([low, pad], axis=0).reshape(LEVELS, n, low.shape[1])


def ns_send(R):
    for k in range(WAYS):
        for kk in range(1, WAYS):
            ns_copy(R, k, kk).start()


def distance_sums(R):
    heads, T, _ = R.dsum.shape
    j = lax.broadcasted_iota(jnp.int32, (T, T), 0)
    for h in range(heads):
        rows = R.dsum[h]
        bit = 1
        while bit < T:
            rows = jnp.where((j & bit) != 0, pltpu.roll(rows, T - bit, 1), rows)
            bit *= 2
        R.sm[3:4, h * T : (h + 1) * T] = jnp.sum(rows, axis=0, keepdims=True)


def states_back(R):
    m, z, r = place()
    W, tc, D = R.fgr.shape
    for k in range(WAYS):
        for kk in range(1, WAYS):
            ns_copy(R, k, kk).wait_send()
            ns_arrival(R, k, kk).wait_recv()
    for k in range(1, WAYS):
        fg_copy(R, k).wait()
    for s in range(W):
        grad = R.part[s, aligned(m * tc, tc)].astype(F32)
        for kk in range(1, WAYS):
            grad = grad + R.nsr[kk - 1, s].astype(F32)
        values = R.st[s, aligned(m * tc, tc)].astype(F32)
        back, _ = rms_back(values, R.g_self[...][None], grad)
        R.sg[s * tc : (s + 1) * tc] = R.fgr[s].astype(F32) + back


def small_sums(R, step):
    m, z, r = place()
    if step == 0:
        R.sm_copies = [send(R.sm, R.smr.at[k - 1], (R.sm_s, R.sm_r), k, peer(k)) for k in range(1, WAYS)]
    elif step == 1:
        total = R.sm[...]
        gains = lax.broadcasted_iota(jnp.int32, total.shape, 0) < 3
        for k in range(1, WAYS):
            total = total + jnp.where(gains, R.smr[k - 1], 0)
        R.sm2[...] = total
        R.sm_copies = [send(R.sm2, R.smr.at[3], (R.sm_s, R.sm_r), 4, partner())]
    elif step == 2:
        R.sm3[...] = R.sm2[...] + R.smr[3]
        R.sm_copies = [send(R.sm3, R.smr.at[4], (R.sm_s, R.sm_r), 5, level(1))] if R.zin else []
    elif step == 3:
        R.sm4[...] = R.sm3[...] + R.smr[4] if R.zin else R.sm3[...]
        R.sm_copies = [send(R.sm4, R.smr.at[5], (R.sm_s, R.sm_r), 6, level(2))] if R.zin else []
    else:
        R.smo[...] = R.sm4[...] + R.smr[5] if R.zin else R.sm4[...]
        return
    for copy in R.sm_copies:
        copy.start()


def small_wait(R):
    for copy in R.sm_copies:
        copy.wait()


def whole_phase(R):
    start_sends(R)
    self_forward(R)
    forward(R, 0)
    forward(R, 1)
    forward_again(R, 0)
    cross_kv(R)
    forward_again(R, 1)
    after_self(R)
    send_cot(R)
    cross_forward(R)
    second_part(R)
    feed_forward(R)
    R.core = {}
    ffn_grads(R)
    core_start(R, "gg")
    core_start(R, "gd")
    second_back(R)
    heads = R.lse_c.shape[0]
    cross_back(R, 0, 1)
    core_sum(R, "gg")
    core_sum(R, "gd")
    level_sum(R, "gg", 0)
    level_sum(R, "gd", 0)
    wg_spread(R, CO)
    cross_back(R, 1, heads // 2)
    first_back(R)
    level_sum(R, "gg", 1)
    kv_grads(R)
    wg_spread(R, CQ)
    wg_spread(R, SO)
    level_sum(R, "gd", 1)
    wg_spread(R, CK)
    wg_spread(R, CV)
    memory_back(R)
    level_sum(R, "gg", 2)
    level_sum(R, "gd", 2)
    self_back(R)
    core_start(R, "se")
    distance_sums(R)
    small_sums(R, 0)
    core_sum(R, "se")
    level_sum(R, "gg", 3)
    level_sum(R, "gd", 3)
    level_sum(R, "se", 0)
    small_wait(R)
    small_sums(R, 1)
    last_start(R, "gg")
    last_start(R, "gd")
    level_sum(R, "se", 1)
    wg_collect(R)
    level_sum(R, "cr", 0)
    ns_send(R)
    memory_send(R)
    level_sum(R, "se", 2)
    small_wait(R)
    small_sums(R, 2)
    level_sum(R, "se", 3)
    level_sum(R, "cr", 1)
    small_wait(R)
    small_sums(R, 3)
    level_sum(R, "cr", 2)
    last_start(R, "se")
    small_wait(R)
    small_sums(R, 4)
    level_sum(R, "cr", 3)
    states_back(R)
    last_start(R, "cr")
    for copy in R.local:
        copy.wait()
    for k in range(1, WAYS):
        mg_copy(R, k).wait()
    for k in range(1, WAYS):
        br_copy(R, k).wait()
    for name in ("gg", "gd", "se", "cr"):
        last_copy(R, name).wait()


def per_device(states, memory, target_mask, memory_length, norm_self, self_query, self_key, self_value, self_out,
               bias_table, norm_cross, cross_query, cross_key, cross_value, cross_out, norm_ffn, ffn_gate, ffn_up,
               ffn_down, cotangent):
    ways = WAYS
    zin = lax.axis_size("dp") == LEVELS
    T, _, D = states.shape
    HW = self_query.shape[1]
    HC = bias_table.shape[1]
    F = ffn_gate.shape[1]
    hd = HW // HC
    M = memory.shape[0] * ways
    heads = D // hd
    st = jnp.transpose(states, (1, 0, 2))
    mem = jnp.transpose(memory, (1, 0, 2))
    cot = jnp.transpose(cotangent, (1, 0, 2))
    pos = jnp.arange(T, dtype=jnp.int32)
    ins = dict(
        st=(st, V), mem=(mem, ANY), wq=(self_query.T, ANY), wk=(self_key.T, ANY), wv=(self_value.T, ANY),
        so=(self_out, ANY), cq=(cross_query.T, ANY), ck=(cross_key.T, ANY), cv=(cross_value.T, ANY),
        co=(cross_out, ANY), mask_in=(target_mask, V), table=(bias_table, V), lens=(memory_length, SM),
        g_self=(norm_self, V), g_cross=(norm_cross, V), g_ffn=(norm_ffn, V), cot=(cot, ANY), gate_in=(ffn_gate, ANY),
        up_in=(ffn_up, ANY), down_in=(ffn_down, ANY),
    )
    half = HW // 2
    n2 = -(-5 * half // (16 * LEVELS)) * 16
    n3 = -(-3 * half // (16 * LEVELS)) * 16
    tc = T // ways
    outs = dict(
        br=((ways, ways, tc, D), BF, ANY), mgo=((ways, M // ways, D), BF, ANY), sg=((T, D), F32, V),
        gg=((2, 2, LEVELS, D // 2 // LEVELS, F), BF, V), gd=((2, LEVELS, F // 2 // LEVELS, D), BF, V),
        cr=((2, LEVELS, n2, D), BF, V), se=((2, LEVELS, n3, D), BF, V), smo=((8, D), F32, V),
    )
    scratch = dict(
        att=V((D, T), BF), qs=V((ways, HW, T), BF), ks=V((ways, T, HW), BF), kts=V((ways, HW, T), BF),
        vts=V((ways, HW, T), BF), vs=V((ways, T, HW), BF), lse_s=V((ways, HC, 1, T), F32),
        second=V((T, D), F32), nc=V((T, D), BF), qc=V((D, T), BF), kc=V((M, D), BF), kct=V((D, M), BF),
        vc=V((M, D), BF), vct=V((D, M), BF), lse_c=V((heads, 1, T), F32), attc=V((D, T), BF), memf=V((M, D), BF),
        waf=V((5, D, D), BF), nall=V((ways, T, D), BF), upall=V((ways, T, D), BF), et=V((HC, T, T), F32),
        atp=V((ways, HW, T), BF), part=V((ways, T, D), BF), ngr=V((3, T, D), BF), brp=V((ways, T, D), BF),
        hid=V((ways * T, F), BF), gu=V((ways * T, 2 * F), BF),
        gg_c=V((2, LEVELS, D // 2 // LEVELS, F), BF),
        gg_x=V((3, 2, D // 2 // LEVELS, F), BF),
        gd_c=V((LEVELS, F // 2 // LEVELS, D), BF),
        gd_x=V((3, F // 2 // LEVELS, D), BF),
        cr_c=V((LEVELS, n2, D), BF), cr_x=V((3, n2, D), BF),
        se_c=V((LEVELS, n3, D), BF), se_x=V((3, n3, D), BF),
        wg=V((5, ways, 2, half, D), BF), wgc=V((5, ways, half, D), BF), wgr=V((3, 5, half, D), BF),
        dot=V((D, T), BF),
        fgb=V((T, D), BF), fgr=V((ways, tc, D), BF), nsr=V((3, ways, tc, D), BF), wsg=V((3 * HW, D), F32),
        dsum=V((HC, T, T), F32), dqkv=V((3 * HW, T), BF), sm=V((8, D), F32), sm2=V((8, D), F32), sm3=V((8, D), F32), sm4=V((8, D), F32),
        smr=V((6, 8, D), F32), l_sem=dma(3), w_sem=dma(11), ws=V((3 * HW, D), BF), mask=V((ways, T, 1), F32),
        gate=V((D, F), BF), up=V((D, F), BF), down=V((F, D), BF),
    )
    for name, n in dict(mem=4, wa=8, fz=8, fw=16, att=4, cot=4, nf=4, ng=4, br=4, do=4, fg=4, mg=4, ns=16, sm=8, wg=20, wgc=5).items():
        scratch[name + "_s"] = dma(n)
        scratch[name + "_r"] = dma(n)
    for name in ("gg", "gd", "se", "cr"):
        for kind, n in dict(cs=2, cr=2, zs=4, zr=4).items():
            scratch[name + "_" + kind] = dma(n)
        scratch[name + "_as"] = dma(4)
        scratch[name + "_ar"] = dma(4)
    def phase(R):
        R.zin = zin
        whole_phase(R)
    G = types.SimpleNamespace(**run_kernel("block", [phase], ins, outs, scratch, 0))
    block_out = jnp.transpose(jnp.sum(G.br.astype(F32), axis=0), (1, 0, 2)).astype(BF)
    memory_grad = jnp.transpose(G.mgo.astype(F32), (1, 0, 2))
    states_grad = jnp.transpose(G.sg.reshape(ways, tc, D), (1, 0, 2))
    sums = [x.astype(F32) for x in (G.gg, G.gd, G.cr, G.se, G.smo)]
    if not zin:
        sums = [lax.psum(x, "dp") for x in sums]
    gg, gd, cr, se, sm = sums
    gate_grad, up_grad = (gg[:, i].reshape(D, F) for i in range(2))
    down_grad = gd.reshape(F, D)
    cross = cr.reshape(2, -1, D)[:, : 5 * half].reshape(2, 5, half, D)
    cross = [cross[:, i].reshape(HW, D) for i in range(5)]
    own = se.reshape(2, -1, D)[:, : 3 * half].reshape(3, HW, D)
    onehot = (bucket_of(pos)[:, None] == jnp.arange(bias_table.shape[0])).astype(F32)
    bias_grad = jnp.einsum("hr,rk->kh", sm[3].reshape(HC, T), onehot, precision=lax.Precision.HIGHEST)
    return (block_out, states_grad, memory_grad, sm[0], own[0].T, own[1].T, own[2].T, cross[SO], bias_grad, sm[1],
            cross[CQ].T, cross[CK].T, cross[CV].T, cross[CO], sm[2], gate_grad, up_grad, down_grad)


def solution(mesh):
    seq = ("dp", "rep")
    col, row, tok = P(None, "mp"), P("mp", None), P("mp", seq, None)
    in_specs = (P(None, seq, None), tok, P(seq, None), P(seq), P(), col, col, col, row, col, P(), col, col, col, row,
                P(), col, col, row, tok)
    out_specs = (tok, tok, tok, P(), col, col, col, row, col, P(), col, col, col, row, P(), col, col, row)
    return jax.shard_map(per_device, mesh=mesh, in_specs=in_specs, out_specs=out_specs, check_vma=False)
```

```python
import math
import types

import jax
import jax.numpy as jnp
from jax import lax
from jax.experimental import pallas as pl
from jax.experimental.pallas import tpu as pltpu
from jax.sharding import PartitionSpec as P

eps = 1e-06
bucket_edges = [math.ceil(16 * 8 ** (level / 16)) for level in range(1, 16)]
BF = jnp.bfloat16
F32 = jnp.float32
NEG = -1e30
VMEM_BYTES = 64 * 2**20 - 2**17
MESH = pl.DeviceIdType.MESH
WAYS = 4
NEAR = (1, 2)
LEVELS = 4
CK, CV, SO, CQ, CO = range(5)
CROSS = ("ca", "cb")
GRAD_PARTS = ((0, 2), (2, 2), (4, 1))
PARTS = ((0, 2), (2, 3))


def dots(a, b, ca, cb):
    return lax.dot_general(a, b, (((ca,), (cb,)), ((), ())), preferred_element_type=F32)


def nn(a, b):
    return dots(a, b, 1, 0)


def nt(a, b):
    return dots(a, b, 1, 1)


def tn(a, b):
    return dots(a, b, 0, 0)


def rms(v, g):
    return v * lax.rsqrt(jnp.mean(v * v, axis=-1, keepdims=True) + eps) * g


def rms_back(v, g, n):
    r = lax.rsqrt(jnp.mean(v * v, axis=-1, keepdims=True) + eps)
    ng = n * g
    return r * ng - v * (r * r * r) * jnp.mean(ng * v, axis=-1, keepdims=True), n * v * r


def gelu_parts(a):
    c = math.sqrt(2 / math.pi)
    t = jnp.tanh(c * (a + 0.044715 * a * a * a))
    half = 0.5 * (1 + t)
    return half * a, half + 0.5 * a * (1 - t * t) * c * (1 + 3 * 0.044715 * a * a)


def place():
    return lax.axis_index("mp"), lax.axis_index("dp"), lax.axis_index("rep")


def peer(k):
    m, z, r = place()
    return (m ^ k, z, r)


def partner():
    m, z, r = place()
    return (m, z, 1 - r)


def level(k):
    m, z, r = place()
    return (m, z ^ k, r)


def greet(zin):
    barrier = pltpu.get_barrier_semaphore()
    known = [peer(k) for k in range(1, WAYS)] + [partner()]
    known += [level(k) for k in ((1, 2, 3) if zin else (1,))]
    for one in known:
        pl.semaphore_signal(barrier, inc=1, device_id=one, device_id_type=MESH)
    pl.semaphore_wait(barrier, len(known))


def send(src, dst, sems, at, to):
    return pltpu.make_async_remote_copy(
        src_ref=src, dst_ref=dst, send_sem=sems[0].at[at], recv_sem=sems[1].at[at], device_id=to, device_id_type=MESH
    )


def run_kernel(name, phases, ins, outs, scratch, cid, flops=0):
    names = list(ins) + list(outs) + list(scratch)

    def body(*refs):
        held = types.SimpleNamespace(**dict(zip(names, refs)))
        for phase in phases:
            phase(held)

    got = pl.pallas_call(
        body,
        name=name,
        out_shape=[jax.ShapeDtypeStruct(shape, dtype) for shape, dtype, _ in outs.values()],
        in_specs=[pl.BlockSpec(memory_space=space) for _, space in ins.values()],
        out_specs=[pl.BlockSpec(memory_space=space) for _, _, space in outs.values()],
        scratch_shapes=list(scratch.values()),
        compiler_params=pltpu.CompilerParams(
            collective_id=cid, has_side_effects=True, vmem_limit_bytes=VMEM_BYTES
        ),
        cost_estimate=pl.CostEstimate(flops=flops, bytes_accessed=flops // 200, transcendentals=0),
    )(*[array for array, _ in ins.values()])
    return dict(zip(outs, got))


V, ANY, SM = pltpu.VMEM, pl.ANY, pltpu.SMEM


def dma(*shape):
    return pltpu.SemaphoreType.DMA(shape)


def aligned(start, size):
    return pl.ds(pl.multiple_of(start, size), size)


def start_sends(R):
    m, z, r = place()
    quarter = R.mem.shape[1]
    HW = R.ck.shape[0]
    mine = aligned(m * HW, HW)
    R.own_w = [
        pltpu.make_async_copy(src, R.waf.at[i, mine], R.w_sem.at[i])
        for i, src in enumerate((R.ck, R.cv, R.so, R.cq, R.co))
    ]
    for copy in R.own_w:
        copy.start()
    R.own_s = [
        pltpu.make_async_copy(src, R.ws.at[pl.ds(i * HW, HW)], R.w_sem.at[5 + i])
        for i, src in enumerate((R.wq, R.wk, R.wv))
    ]
    R.own_s.append(pltpu.make_async_copy(R.st_in, R.st, R.w_sem.at[11]))
    for copy in R.own_s:
        copy.start()
    R.local = [
        pltpu.make_async_copy(R.mem.at[m], R.memf.at[aligned(m * quarter, quarter)], R.l_sem.at[0]),
        pltpu.make_async_copy(R.gate_in, R.gate, R.w_sem.at[8]),
        pltpu.make_async_copy(R.up_in, R.up, R.w_sem.at[9]),
        pltpu.make_async_copy(R.down_in, R.down, R.w_sem.at[10]),
    ]
    for copy in R.local:
        copy.start()
    greet(R.zin)
    R.mem_copies = {}
    rows = aligned(m * quarter, quarter)
    for k in range(1, WAYS):
        copy = send(R.mem.at[m ^ k], R.memf.at[rows], (R.mem_s, R.mem_r), k, peer(k))
        copy.start()
        R.mem_copies[k] = copy
    for copy in R.own_w:
        copy.wait()
    for part in range(len(PARTS)):
        for k in range(1, WAYS):
            wa_copy(R, part, k).start()


def quarter_rows(R, part, owner, core, half):
    HW = R.ck.shape[0]
    lo, n = PARTS[part]
    return R.waf.at[pl.ds(lo, n), aligned(owner * HW + core * (HW // 2) + half * (HW // 4), HW // 4)]


def wa_copy(R, part, k):
    m, z, r = place()
    view = quarter_rows(R, part, m, r, z & 1)
    return send(view, view, (R.wa_s, R.wa_r), part * WAYS + k, peer(k))


def fz_copy(R, part, k):
    m, z, r = place()
    view = quarter_rows(R, part, m ^ k, r, z & 1)
    return send(view, view, (R.fz_s, R.fz_r), part * WAYS + k, level(1))


def fw_copy(R, part, k, second):
    m, z, r = place()
    view = quarter_rows(R, part, m ^ k, r, (z & 1) ^ second)
    return send(view, view, (R.fw_s, R.fw_r), (second * 2 + part) * WAYS + k, partner())


def cot_copy(R, k):
    m, z, r = place()
    tc = R.cot.shape[1]
    return send(R.cot, R.upall.at[:, aligned(m * tc, tc)], (R.cot_s, R.cot_r), k, peer(k))


def cot_relay(R, k):
    m, z, r = place()
    tc = R.cot.shape[1]
    view = R.upall.at[pl.ds(0 if k == 2 else 2, 2), aligned((m ^ k) * tc, tc)]
    return send(view, view, (R.cot_s, R.cot_r), 2 + k, peer(3 ^ k))


def send_cot(R):
    m, z, r = place()
    tc = R.cot.shape[1]
    R.own_cot = pltpu.make_async_copy(R.cot, R.upall.at[:, aligned(m * tc, tc)], R.l_sem.at[2])
    R.own_cot.start()
    for k in NEAR:
        cot_copy(R, k).start()


def pass_cot(R):
    for k in NEAR:
        cot_copy(R, k).wait_recv()
        cot_relay(R, k).start()


def have_cot(R):
    R.own_cot.wait()
    for k in NEAR:
        cot_copy(R, k).wait_send()
        cot_relay(R, k).wait()


def forward(R, part):
    for k in range(1, WAYS):
        wa_copy(R, part, k).wait_recv()
        fz_copy(R, part, k).start()
        fw_copy(R, part, k, 0).start()


def forward_again(R, part):
    for k in range(1, WAYS):
        fz_copy(R, part, k).wait_recv()
        fw_copy(R, part, k, 1).start()


def gathered(R, part):
    for k in range(1, WAYS):
        wa_copy(R, part, k).wait_send()
        fz_copy(R, part, k).wait_send()
        fw_copy(R, part, k, 0).wait()
        fw_copy(R, part, k, 1).wait()


def self_allowed(R, s):
    T = R.st.shape[1]
    j = lax.broadcasted_iota(jnp.int32, (T, T), 0)
    i = lax.broadcasted_iota(jnp.int32, (T, T), 1)
    chosen = lax.broadcasted_iota(jnp.int32, R.mask.shape, 1) == s
    open_rows = jnp.sum(jnp.where(chosen, R.mask[...], 0), axis=1, keepdims=True)
    return (j == i) | ((j < i) & (open_rows != 0))


def buckets(R, T):
    shape = (R.table.shape[1], T)
    distance = lax.broadcasted_iota(jnp.int32, shape, 1)
    bucket = jnp.minimum(distance, 16)
    for edge in bucket_edges:
        bucket = bucket + (distance >= edge).astype(jnp.int32)
    return (bucket == lax.broadcasted_iota(jnp.int32, shape, 0)).astype(F32)


def self_setup(R):
    W, T, _ = R.st.shape
    by_distance = jnp.dot(R.table[...], buckets(R, T), precision=lax.Precision.HIGHEST, preferred_element_type=F32)
    for h in range(R.table.shape[0]):
        R.et[h] = pltpu.roll(jnp.broadcast_to(by_distance[h : h + 1], (T, T)), 0, 1, stride=1, stride_axis=0)
    rows = R.mask_in[...].astype(F32)
    R.mask[...] = jnp.concatenate([rows, jnp.zeros((8 - W, T), F32)], axis=0).T
    for copy in R.own_s:
        copy.wait()


def only_head(rows, h, heads):
    zero = jnp.zeros(rows.shape, rows.dtype)
    return jnp.concatenate([rows if g == h else zero for g in range(heads)], axis=0)


def self_scores(R, s, h, allowed):
    heads = R.table.shape[0]
    hd = R.qs.shape[1] // heads
    rows = slice(h * hd, (h + 1) * hd)
    scores = nn(R.ks[s], only_head(R.qs[s, rows], h, heads)) + R.et[h]
    return jnp.where(allowed, scores, NEG)


def self_forward(R):
    m, z, r = place()
    HW = R.ws.shape[0] // 3
    heads = R.table.shape[0]
    hd = HW // heads
    self_setup(R)

    def one(s):
        normed = rms(R.st[s].astype(F32), R.g_self[...][None]).astype(BF)
        R.qs[s] = nt(R.ws[0:HW], normed).astype(BF)
        R.ks[s] = nt(normed, R.ws[HW : 2 * HW]).astype(BF)
        R.kts[s] = nt(R.ws[HW : 2 * HW], normed).astype(BF)
        R.vts[s] = nt(R.ws[2 * HW : 3 * HW], normed).astype(BF)
        R.vs[s] = nt(normed, R.ws[2 * HW : 3 * HW]).astype(BF)
        allowed = self_allowed(R, s)
        for h in range(heads):
            rows = slice(h * hd, (h + 1) * hd)
            scores = self_scores(R, s, h, allowed)
            top = jnp.max(scores, axis=0, keepdims=True)
            weights = jnp.exp(scores - top)
            total = jnp.sum(weights, axis=0, keepdims=True)
            R.atp[s, rows] = (nn(R.vts[s, rows], weights.astype(BF)) * (1 / total)).astype(BF)
            R.lse_s[s, h] = top + jnp.log(total)

    def step(k, carry):
        one(m ^ k)
        att_copy(R, k).start()
        return carry

    lax.fori_loop(1, WAYS, step, 0)
    one(m)
    R.att[aligned(m * HW, HW)] = R.atp[m]


def att_copy(R, k):
    m, z, r = place()
    HW = R.ws.shape[0] // 3
    return send(R.atp.at[m ^ k], R.att.at[aligned(m * HW, HW)], (R.att_s, R.att_r), k, peer(k))


def cross_kv(R):
    for copy in R.local:
        copy.wait()
    for copy in R.mem_copies.values():
        copy.wait()
    gathered(R, 0)
    M = R.memf.shape[0]
    step = 256

    def rows(i, carry):
        at = aligned(i * step, step)
        block = R.memf[at]
        k = nt(block, R.waf[CK]).astype(BF)
        R.kc[at] = k
        v = nt(block, R.waf[CV]).astype(BF)
        R.vc[at] = v
        R.kct[:, at] = k.T
        R.vct[:, at] = v.T
        return carry

    lax.fori_loop(0, M // step, rows, 0)


def after_self(R):
    m, z, r = place()
    for k in range(1, WAYS):
        att_copy(R, k).wait()
    gathered(R, 1)
    first = R.st[m].astype(F32) + tn(R.att[...], R.waf[SO])
    R.sg[...] = first
    normed = rms(first, R.g_cross[...][None]).astype(BF)
    R.nc[...] = normed
    R.qc[...] = nt(R.waf[CQ], normed).astype(BF)


def padded_head(ref, p, a, hd):
    rows = ref[aligned(p * 2 * hd + a * hd, hd)]
    zero = jnp.zeros(rows.shape, rows.dtype)
    return jnp.concatenate([rows, zero] if a == 0 else [zero, rows], axis=0)


def cross_scores(R, p, a, hd):
    m, z, r = place()
    M, T = R.memf.shape[0], R.qc.shape[1]
    scores = nn(R.kc[:, aligned(p * 2 * hd, 2 * hd)], padded_head(R.qc, p, a, hd))
    live = lax.broadcasted_iota(jnp.int32, (M, T), 0) < R.lens[m]
    return jnp.where(live, scores, NEG)


def cross_forward(R):
    hd = R.ws.shape[0] // 3 // R.table.shape[0]
    heads = R.qc.shape[0] // hd

    def pair(p, carry):
        for a in range(2):
            rows = aligned(p * 2 * hd + a * hd, hd)
            scores = cross_scores(R, p, a, hd)
            top = jnp.max(scores, axis=0, keepdims=True)
            weights = jnp.exp(scores - top)
            total = jnp.sum(weights, axis=0, keepdims=True)
            R.attc[rows] = (nn(R.vct[rows], weights.astype(BF)) * (1 / total)).astype(BF)
            R.lse_c[2 * p + a] = top + jnp.log(total)
        return carry

    lax.fori_loop(0, heads // 2, pair, 0)


def nf_copy(R, k):
    m, z, r = place()
    return send(R.nall.at[m], R.nall.at[m], (R.nf_s, R.nf_r), k, peer(k))


def nf_relay(R, k):
    m, z, r = place()
    half = R.nall.shape[1] // 2
    view = R.nall.at[m ^ k, pl.ds(0 if k == 2 else half, half)]
    return send(view, view, (R.nf_s, R.nf_r), 2 + k, peer(3 ^ k))


def second_part(R):
    m, z, r = place()
    second = R.sg[...] + tn(R.attc[...], R.waf[CO])
    R.second[...] = second
    R.nall[m] = rms(second, R.g_ffn[...][None]).astype(BF)
    for k in NEAR:
        nf_copy(R, k).start()


def ng_copy(R, k):
    m, z, r = place()
    return send(R.part.at[m ^ k], R.ngr.at[k - 1], (R.ng_s, R.ng_r), k, peer(k))


def first_copy(R, name, k, relay, tag):
    m, z, r = place()
    tc = R.near.shape[3]
    to = m ^ 3 if relay else m ^ k
    source = getattr(R, name).at[pl.ds(2 * (k - 1), 2), aligned(to * tc, tc)]
    return send(source, R.near.at[k - 1, relay], (R.near_s, R.near_r), tag + 2 * (k - 1) + relay, peer(k))


def relay_copy(R, name, k, tag):
    m, z, r = place()
    tc = R.near.shape[3]
    source = getattr(R, name).at[pl.ds(2 * (k - 1), 2), aligned((m ^ 3 ^ k) * tc, tc)]
    return send(source, R.far.at[k - 1], (R.near_s, R.near_r), tag + 3 + k, peer(3 ^ k))


def scatter_start(R, name, tag):
    for k in NEAR:
        first_copy(R, name, k, 1, tag).start()
    for k in NEAR:
        first_copy(R, name, k, 0, tag).start()


def scatter_pass(R, name, tag):
    m, z, r = place()
    tc = R.near.shape[3]
    source = getattr(R, name)
    for k in NEAR:
        first_copy(R, name, k, 1, tag).wait()
        at = (pl.ds(2 * (k - 1), 2), aligned((m ^ 3 ^ k) * tc, tc))
        source[at] = (source[at].astype(F32) + R.near[k - 1, 1].astype(F32)).astype(BF)
        relay_copy(R, name, k, tag).start()


def scatter_end(R, name, tag, k):
    m, z, r = place()
    tc = R.near.shape[3]
    first_copy(R, name, k, 0, tag).wait()
    relay_copy(R, name, k, tag).wait()
    own = getattr(R, name)[pl.ds(2 * (k - 1), 2), aligned(m * tc, tc)].astype(F32)
    return own + R.near[k - 1, 0].astype(F32) + R.far[k - 1].astype(F32)


def block_end(R):
    for k in NEAR:
        R.br[2 * (k - 1) : 2 * k] = scatter_end(R, "brp", 0, k).astype(BF)


def feed_forward(R):
    m, z, r = place()
    T = R.st.shape[1]
    F = R.down.shape[0]

    def one(s, extra):
        rows = aligned(s * T, T)
        n, up = R.nall[s], R.upall[s]
        gate, lift = nn(n, R.gate[...]), nn(n, R.up[...])
        value, slope = gelu_parts(gate)
        hidden = (value * lift).astype(BF)
        R.hid[rows] = hidden
        back = nt(up, R.down[...])
        gate_grad = (back * lift * slope).astype(BF)
        up_grad = (back * value).astype(BF)
        R.gu[rows, 0:F] = gate_grad
        R.gu[rows, F : 2 * F] = up_grad
        R.part[s] = (nt(gate_grad, R.gate[...]) + nt(up_grad, R.up[...])).astype(BF)
        branch = nn(hidden, R.down[...])
        R.brp[s] = (branch + R.second[...] if extra else branch).astype(BF)

    have_cot(R)
    one(m, True)
    for k in NEAR:
        nf_copy(R, k).wait_recv()
        nf_relay(R, k).start()
    for k in range(1, WAYS):
        if k == 3:
            for near in NEAR:
                nf_relay(R, near).wait()
        one(m ^ k, False)
        ng_copy(R, k).start()
    for k in NEAR:
        nf_copy(R, k).wait_send()


def ffn_grads(R):
    W, T, D = R.nall.shape
    F = R.down.shape[0]
    rows = R.nall[...].reshape(W * T, D)
    both = tn(rows, R.gu[...]).astype(BF)
    R.gg[:, 0] = both[:, 0:F].reshape(2, 2, D // 4, F)
    R.gg[:, 1] = both[:, F : 2 * F].reshape(2, 2, D // 4, F)
    R.gd[...] = tn(R.hid[...], R.upall[...].reshape(W * T, D)).astype(BF).reshape(2, 2, F // 4, D)


def core_start(R, name):
    m, z, r = place()
    source, sems = getattr(R, name), (getattr(R, name + "_cs"), getattr(R, name + "_cr"))
    copy = send(source.at[1 - r], getattr(R, name + "_c"), sems, 0, partner())
    copy.start()
    R.core[name] = copy


def core_sum(R, name):
    m, z, r = place()
    R.core[name].wait()
    source, other = getattr(R, name), getattr(R, name + "_c")
    source[r] = (source[r].astype(F32) + other[...].astype(F32)).astype(BF)
    ready(R, name)


def part_of(ref, p):
    return ref.at[p] if len(ref.shape) == 3 else ref.at[:, p]


def halves(R, name):
    m, z, r = place()
    whole, spare = getattr(R, name).at[r], getattr(R, name + "_c")
    return (spare, whole) if name in CROSS else (whole, spare)


def inward_copy(R, name, n):
    m, z, r = place()
    before, after = halves(R, name)
    p = (z >> 1) ^ 1 ^ n
    return send(part_of(before, p), part_of(after, p), (getattr(R, name + "_zs"), getattr(R, name + "_zr")), n, level(1))


def across_copy(R, name):
    m, z, r = place()
    sems = (getattr(R, name + "_zs"), getattr(R, name + "_zr"))
    return send(part_of(halves(R, name)[0], (z >> 1) ^ 1), getattr(R, name + "_x"), sems, 2, level(3))


def spread_copy(R, name, n):
    m, z, r = place()
    sems = (getattr(R, name + "_as"), getattr(R, name + "_ar"))
    part = part_of(halves(R, name)[1], (z >> 1) ^ (0, 0, 1)[n])
    return send(part, part, sems, n, level((3, 1, 1)[n]))


def ready(R, name):
    if R.zin and name not in CROSS:
        pl.semaphore_signal(getattr(R, name + "_ok"), inc=1, device_id=level(1), device_id_type=MESH)


def level_sum(R, name, step):
    m, z, r = place()
    before, after = halves(R, name)
    if not R.zin:
        if step == 0:
            after[...] = before[...]
        return
    inner = (z == 1) | (z == 2)
    mine, other = z >> 1, (z >> 1) ^ 1
    if step == 0:
        if name not in CROSS:
            pl.semaphore_wait(getattr(R, name + "_ok"), 1)

        @pl.when(jnp.logical_not(inner))
        def _():
            inward_copy(R, name, 0).start()
            inward_copy(R, name, 1).start()

    elif step == 1:

        @pl.when(inner)
        def _():
            inward_copy(R, name, 0).wait_recv()
            held = part_of(before, other)
            held[...] = (held[...].astype(F32) + part_of(after, other)[...].astype(F32)).astype(BF)
            across_copy(R, name).start()

    elif step == 2:

        @pl.when(inner)
        def _():
            inward_copy(R, name, 1).wait_recv()
            across_copy(R, name).wait()
            held = part_of(after, mine)
            total = held[...].astype(F32) + part_of(before, mine)[...].astype(F32)
            held[...] = (total + getattr(R, name + "_x")[...].astype(F32)).astype(BF)
            spread_copy(R, name, 0).start()
            spread_copy(R, name, 1).start()

        @pl.when(jnp.logical_not(inner))
        def _():
            inward_copy(R, name, 0).wait_send()
            inward_copy(R, name, 1).wait_send()

    else:

        @pl.when(inner)
        def _():
            spread_copy(R, name, 0).wait_recv()
            spread_copy(R, name, 2).start()


def last_copy(R, name):
    m, z, r = place()
    mine = halves(R, name)[1]
    return send(mine, getattr(R, name).at[r], (getattr(R, name + "_cs"), getattr(R, name + "_cr")), 1, partner())


def last_start(R, name):
    m, z, r = place()
    if R.zin:
        inner = (z == 1) | (z == 2)

        @pl.when(inner)
        def _():
            for n in range(3):
                spread_copy(R, name, n).wait_send()

        @pl.when(jnp.logical_not(inner))
        def _():
            for n in (1, 2):
                spread_copy(R, name, n).wait_recv()

    last_copy(R, name).start()
    if name not in CROSS:
        getattr(R, name)[r] = getattr(R, name + "_c")[...]


def wg_core(R, i):
    m, z, r = place()
    return send(R.wg.at[i, :, 1 - r], R.wgc.at[i], (R.wgc_s, R.wgc_r), i, partner())


def wg_part(R, part, k, owner):
    m, z, r = place()
    rows = R.wg.shape[3] // 2
    lo, n = GRAD_PARTS[part]
    return R.wg.at[pl.ds(lo, n), owner, r, pl.ds((k - 1) * rows, rows)]


def wg_first(R, part, k, relay):
    m, z, r = place()
    lo, n = GRAD_PARTS[part]
    source = wg_part(R, part, k, m ^ 3 if relay else m ^ k)
    sems = (R.wg_s, R.wg_r)
    return send(source, R.wgr.at[k - 1, relay, pl.ds(lo, n)], sems, 6 * part + 2 * (k - 1) + relay, peer(k))


def wg_relay(R, part, k):
    m, z, r = place()
    lo, n = GRAD_PARTS[part]
    source = wg_part(R, part, k, m ^ 3 ^ k)
    return send(source, R.wgr.at[k - 1, 2, pl.ds(lo, n)], (R.wg_s, R.wg_r), 6 * part + 3 + k, peer(3 ^ k))


def put_grad(R, i, value):
    D = value.shape[0]
    R.wg[i] = value.astype(BF).reshape(WAYS, 2, D // WAYS // 2, D)
    wg_core(R, i).start()


def wg_spread(R, part):
    m, z, r = place()
    lo, n = GRAD_PARTS[part]
    for i in range(lo, lo + n):
        wg_core(R, i).wait()
        for s in range(WAYS):
            R.wg[i, s, r] = (R.wg[i, s, r].astype(F32) + R.wgc[i, s].astype(F32)).astype(BF)
    for k in NEAR:
        wg_first(R, part, k, 1).start()
    for k in NEAR:
        wg_first(R, part, k, 0).start()


def wg_pass(R, part):
    m, z, r = place()
    lo, n = GRAD_PARTS[part]
    for k in NEAR:
        wg_first(R, part, k, 1).wait()
        place_of = wg_part(R, part, k, m ^ 3 ^ k)
        place_of[...] = (place_of[...].astype(F32) + R.wgr[k - 1, 1, lo : lo + n].astype(F32)).astype(BF)
        wg_relay(R, part, k).start()


def put_cross(R, i, k, value):
    buffer, place_in = (R.cb_c, i) if i < SO else (R.ca_c, i - SO)
    n, count = buffer.shape[1], value.shape[0]
    start = (2 * place_in + k - 1) * count
    done = 0
    while done < count:
        j, at = divmod(start + done, n)
        step = min(n - at, count - done)
        buffer[j, at : at + step] = value[done : done + step]
        done += step


def wg_collect(R, part):
    m, z, r = place()
    lo, n = GRAD_PARTS[part]
    rows = R.wg.shape[3] // 2
    for k in NEAR:
        wg_first(R, part, k, 0).wait()
        wg_relay(R, part, k).wait()
        total = wg_part(R, part, k, m)[...].astype(F32)
        total = total + R.wgr[k - 1, 0, lo : lo + n].astype(F32) + R.wgr[k - 1, 2, lo : lo + n].astype(F32)
        for i in range(n):
            put_cross(R, lo + i, k, total[i].astype(BF))


def second_back(R):
    m, z, r = place()
    for k in range(1, WAYS):
        ng_copy(R, k).wait()
    scatter_start(R, "brp", 0)
    R.local = []
    grad = R.part[m].astype(F32)
    for k in range(1, WAYS):
        grad = grad + R.ngr[k - 1].astype(F32)
    back, gain = rms_back(R.second[...], R.g_ffn[...][None], grad)
    R.sm[...] = jnp.zeros(R.sm.shape, F32)
    R.sm[2:3] = jnp.sum(gain, axis=0, keepdims=True)
    total = R.upall[m].astype(F32) + back
    R.second[...] = total
    low = total.astype(BF)
    R.dot[...] = nt(R.waf[CO], low).astype(BF)
    put_grad(R, CO, nn(R.attc[...], low))


def cross_back(R, lo, hi):
    hd = R.ws.shape[0] // 3 // R.table.shape[0]

    def pair(p, carry):
        lanes = aligned(p * 2 * hd, 2 * hd)
        for a in range(2):
            rows = aligned(p * 2 * hd + a * hd, hd)
            mix = jnp.exp(cross_scores(R, p, a, hd) - R.lse_c[2 * p + a])
            value_grad = nt(R.dot[rows], mix.astype(BF)).astype(BF)
            grad = nn(R.vc[:, lanes], padded_head(R.dot, p, a, hd))
            delta = jnp.sum(mix * grad, axis=0, keepdims=True)
            score_grad = (mix * (grad - delta)).astype(BF)
            R.attc[rows] = nn(R.kct[rows], score_grad).astype(BF)
            R.kct[rows] = value_grad
            R.vct[rows] = nt(R.qc[rows], score_grad).astype(BF)
        return carry

    lax.fori_loop(lo, hi, pair, 0)


def do_copy(R, k):
    m, z, r = place()
    HW = R.ws.shape[0] // 3
    return send(R.dot.at[aligned((m ^ k) * HW, HW)], R.atp.at[m], (R.do_s, R.do_r), k, peer(k))


def fg_copy(R, k):
    m, z, r = place()
    tc = R.fgr.shape[1]
    return send(R.nall.at[0, aligned((m ^ k) * tc, tc)], R.fgr.at[m], (R.fg_s, R.fg_r), k, peer(k))


def first_back(R):
    m, z, r = place()
    HW = R.ws.shape[0] // 3
    tc = R.fgr.shape[1]
    back, gain = rms_back(R.sg[...], R.g_cross[...][None], tn(R.attc[...], R.waf[CQ]))
    R.sm[1:2] = jnp.sum(gain, axis=0, keepdims=True)
    low = (R.second[...] + back).astype(BF)
    R.nall[0] = low
    R.dot[...] = nt(R.waf[SO], low).astype(BF)
    for k in range(1, WAYS):
        do_copy(R, k).start()
    for k in range(1, WAYS):
        fg_copy(R, k).start()
    R.atp[m] = R.dot[aligned(m * HW, HW)]
    R.fgr[m] = R.nall[0, aligned(m * tc, tc)]
    put_grad(R, CQ, nn(R.attc[...], R.nc[...]))
    put_grad(R, SO, nn(R.att[...], low))


def mg_copy(R, k):
    m, z, r = place()
    quarter = R.mem.shape[1]
    return send(R.vc.at[aligned((m ^ k) * quarter, quarter)], R.mgo.at[m], (R.mg_s, R.mg_r), k, peer(k))


def memory_back(R):
    m, z, r = place()
    quarter = R.mem.shape[1]

    def rows(c):
        at = aligned(c * quarter, quarter)
        R.vc[at] = (tn(R.vct[:, at], R.waf[CK]) + tn(R.kct[:, at], R.waf[CV])).astype(BF)

    lax.fori_loop(0, WAYS, lambda c, carry: (rows(c), carry)[1], 0)


def memory_send(R):
    m, z, r = place()
    quarter = R.mem.shape[1]
    for k in range(1, WAYS):
        mg_copy(R, k).start()
    own = pltpu.make_async_copy(R.vc.at[aligned(m * quarter, quarter)], R.mgo.at[m], R.l_sem.at[1])
    own.start()
    R.local.append(own)


def kv_grads(R):
    put_grad(R, CK, nn(R.vct[...], R.memf[...]))
    put_grad(R, CV, nn(R.kct[...], R.memf[...]))


def self_back(R):
    m, z, r = place()
    T = R.st.shape[1]
    HW = R.ws.shape[0] // 3
    heads = R.table.shape[0]
    hd = HW // heads
    R.wsg[...] = jnp.zeros(R.wsg.shape, F32)
    R.dsum[...] = jnp.zeros(R.dsum.shape, F32)

    def one(k):
        s = m ^ k
        allowed = self_allowed(R, s)
        for h in range(heads):
            rows = slice(h * hd, (h + 1) * hd)
            mix = jnp.exp(self_scores(R, s, h, allowed) - R.lse_s[s, h])
            out = R.atp[s, rows]
            grad = nn(R.vs[s], only_head(out, h, heads))
            delta = jnp.sum(mix * grad, axis=0, keepdims=True)
            score_grad = (mix * (grad - delta)).astype(BF)
            R.dsum[h] += score_grad.astype(F32)
            R.dqkv[h * hd : (h + 1) * hd] = nn(R.kts[s, rows], score_grad).astype(BF)
            R.dqkv[HW + h * hd : HW + (h + 1) * hd] = nt(R.qs[s, rows], score_grad).astype(BF)
            R.dqkv[2 * HW + h * hd : 2 * HW + (h + 1) * hd] = nt(out, mix.astype(BF)).astype(BF)
        values = R.st[s].astype(F32)
        scaled = values * lax.rsqrt(jnp.mean(values * values, axis=-1, keepdims=True) + eps)
        normed = (scaled * R.g_self[...][None]).astype(BF)
        R.wsg[...] += nn(R.dqkv[...], normed)
        grad = tn(R.dqkv[...], R.ws[...])
        R.sm[0:1] += jnp.sum(grad * scaled, axis=0, keepdims=True)
        R.part[s] = grad.astype(BF)

    one(0)

    def step(k, carry):
        do_copy(R, k).wait()
        one(k)
        return carry

    lax.fori_loop(1, WAYS, step, 0)
    R.se[...] = R.wsg[...].astype(BF).reshape(R.se.shape)


def distance_sums(R):
    heads, T, _ = R.dsum.shape
    j = lax.broadcasted_iota(jnp.int32, (T, T), 0)
    for h in range(heads):
        rows = R.dsum[h]
        bit = 1
        while bit < T:
            rows = jnp.where((j & bit) != 0, pltpu.roll(rows, T - bit, 1), rows)
            bit *= 2
        R.sm[3:4, h * T : (h + 1) * T] = jnp.sum(rows, axis=0, keepdims=True)


def states_back(R):
    m, z, r = place()
    W, tc, D = R.fgr.shape
    for k in range(1, WAYS):
        fg_copy(R, k).wait()
    for k in NEAR:
        grad = scatter_end(R, "part", 6, k)
        for s in range(2 * (k - 1), 2 * k):
            values = R.st[s, aligned(m * tc, tc)].astype(F32)
            back, _ = rms_back(values, R.g_self[...][None], grad[s - 2 * (k - 1)])
            R.sg[s * tc : (s + 1) * tc] = R.fgr[s].astype(F32) + back


def small_sums(R, step):
    m, z, r = place()
    if step == 0:
        R.sm_copies = [send(R.sm, R.smr.at[k - 1], (R.sm_s, R.sm_r), k, peer(k)) for k in range(1, WAYS)]
    elif step == 1:
        total = R.sm[...]
        gains = lax.broadcasted_iota(jnp.int32, total.shape, 0) < 3
        for k in range(1, WAYS):
            total = total + jnp.where(gains, R.smr[k - 1], 0)
        R.sm2[...] = total
        R.sm_copies = [send(R.sm2, R.smr.at[3], (R.sm_s, R.sm_r), 4, partner())]
    elif step == 2:
        R.sm3[...] = R.sm2[...] + R.smr[3]
        R.sm_copies = [send(R.sm3, R.smr.at[4], (R.sm_s, R.sm_r), 5, level(1))] if R.zin else []
    elif step == 3:
        R.sm4[...] = R.sm3[...] + R.smr[4] if R.zin else R.sm3[...]
        R.sm_copies = [send(R.sm4, R.smr.at[5], (R.sm_s, R.sm_r), 6, level(2))] if R.zin else []
    else:
        R.smo[...] = R.sm4[...] + R.smr[5] if R.zin else R.sm4[...]
        heads, T = R.table.shape[0], R.st.shape[1]
        by_distance = jnp.concatenate([R.smo[3:4, h * T : (h + 1) * T] for h in range(heads)], axis=0)
        R.tg[...] = lax.dot_general(
            by_distance, buckets(R, T), (((1,), (1,)), ((), ())), precision=lax.Precision.HIGHEST,
            preferred_element_type=F32,
        )
        return
    for copy in R.sm_copies:
        copy.start()


def small_wait(R):
    for copy in R.sm_copies:
        copy.wait()


def whole_phase(R):
    start_sends(R)
    self_forward(R)
    forward(R, 0)
    forward(R, 1)
    send_cot(R)
    forward_again(R, 0)
    cross_kv(R)
    forward_again(R, 1)
    after_self(R)
    pass_cot(R)
    cross_forward(R)
    second_part(R)
    feed_forward(R)
    R.core = {}
    ffn_grads(R)
    core_start(R, "gg")
    core_start(R, "gd")
    core_sum(R, "gg")
    core_sum(R, "gd")
    level_sum(R, "gg", 0)
    level_sum(R, "gd", 0)
    second_back(R)
    heads = R.lse_c.shape[0]
    cross_back(R, 0, 1)
    wg_spread(R, 2)
    cross_back(R, 1, 3)
    scatter_pass(R, "brp", 0)
    level_sum(R, "gg", 1)
    cross_back(R, 3, 5)
    wg_pass(R, 2)
    level_sum(R, "gd", 1)
    cross_back(R, 5, heads // 2)
    first_back(R)
    kv_grads(R)
    block_end(R)
    level_sum(R, "gg", 2)
    wg_spread(R, 1)
    level_sum(R, "gd", 2)
    wg_spread(R, 0)
    memory_back(R)
    self_back(R)
    core_start(R, "se")
    wg_pass(R, 1)
    distance_sums(R)
    small_sums(R, 0)
    core_sum(R, "se")
    level_sum(R, "se", 0)
    level_sum(R, "gg", 3)
    wg_pass(R, 0)
    scatter_start(R, "part", 6)
    level_sum(R, "gd", 3)
    wg_collect(R, 2)
    wg_collect(R, 1)
    level_sum(R, "ca", 0)
    wg_collect(R, 0)
    level_sum(R, "cb", 0)
    small_wait(R)
    small_sums(R, 1)
    level_sum(R, "se", 1)
    last_start(R, "gg")
    last_start(R, "gd")
    level_sum(R, "ca", 1)
    scatter_pass(R, "part", 6)
    memory_send(R)
    small_wait(R)
    small_sums(R, 2)
    level_sum(R, "cb", 1)
    level_sum(R, "se", 2)
    level_sum(R, "ca", 2)
    small_wait(R)
    small_sums(R, 3)
    level_sum(R, "cb", 2)
    states_back(R)
    level_sum(R, "se", 3)
    level_sum(R, "ca", 3)
    level_sum(R, "cb", 3)
    small_wait(R)
    small_sums(R, 4)
    last_start(R, "se")
    last_start(R, "ca")
    last_start(R, "cb")
    for copy in R.local:
        copy.wait()
    for k in range(1, WAYS):
        mg_copy(R, k).wait()
    for name in ("gg", "gd", "se", "ca", "cb"):
        last_copy(R, name).wait()


def per_device(states, memory, target_mask, memory_length, norm_self, self_query, self_key, self_value, self_out,
               bias_table, norm_cross, cross_query, cross_key, cross_value, cross_out, norm_ffn, ffn_gate, ffn_up,
               ffn_down, cotangent):
    ways = WAYS
    zin = lax.axis_size("dp") == LEVELS
    T, _, D = states.shape
    HW = self_query.shape[1]
    HC = bias_table.shape[1]
    F = ffn_gate.shape[1]
    hd = HW // HC
    M = memory.shape[0] * ways
    heads = D // hd
    st = jnp.transpose(states, (1, 0, 2))
    mem = jnp.transpose(memory, (1, 0, 2))
    cot = jnp.transpose(cotangent, (1, 0, 2))
    ins = dict(
        st_in=(st, ANY), mem=(mem, ANY), wq=(self_query.T, ANY), wk=(self_key.T, ANY), wv=(self_value.T, ANY),
        so=(self_out, ANY), cq=(cross_query.T, ANY), ck=(cross_key.T, ANY), cv=(cross_value.T, ANY),
        co=(cross_out, ANY), mask_in=(target_mask, V), table=(bias_table.T, V), lens=(memory_length, SM),
        g_self=(norm_self, V), g_cross=(norm_cross, V), g_ffn=(norm_ffn, V), cot=(cot, ANY), gate_in=(ffn_gate, ANY),
        up_in=(ffn_up, ANY), down_in=(ffn_down, ANY),
    )
    half = HW // 2
    summed = dict(
        gg=(2, 2, 2, D // 4, F), gd=(2, 2, F // 4, D), ca=(2, 2, 3 * half // 2, D), cb=(2, 2, half, D),
        se=(2, 2, 3 * HW // 4, D),
    )
    tc = T // ways
    outs = dict(
        br=((ways, tc, D), BF, V), mgo=((ways, M // ways, D), BF, ANY), sg=((T, D), F32, V),
        smo=((8, D), F32, V), tg=((HC, bias_table.shape[0]), F32, V),
    )
    outs.update((name, (shape, BF, V)) for name, shape in summed.items())
    scratch = dict(
        att=V((D, T), BF), qs=V((ways, HW, T), BF), ks=V((ways, T, HW), BF), kts=V((ways, HW, T), BF),
        vts=V((ways, HW, T), BF), vs=V((ways, T, HW), BF), lse_s=V((ways, HC, 1, T), F32),
        second=V((T, D), F32), nc=V((T, D), BF), qc=V((D, T), BF), kc=V((M, D), BF), kct=V((D, M), BF),
        vc=V((M, D), BF), vct=V((D, M), BF), lse_c=V((heads, 1, T), F32), attc=V((D, T), BF), memf=V((M, D), BF),
        waf=V((5, D, D), BF), nall=V((ways, T, D), BF), upall=V((ways, T, D), BF), et=V((HC, T, T), F32),
        atp=V((ways, HW, T), BF), part=V((ways, T, D), BF), ngr=V((3, T, D), BF), brp=V((ways, T, D), BF),
        hid=V((ways * T, F), BF), gu=V((ways * T, 2 * F), BF),
        wg=V((5, ways, 2, half, D), BF), wgc=V((5, ways, half, D), BF), wgr=V((2, 3, 5, half // 2, D), BF),
        dot=V((D, T), BF),
        fgr=V((ways, tc, D), BF), near=V((2, 2, 2, tc, D), BF), far=V((2, 2, tc, D), BF), wsg=V((3 * HW, D), F32),
        dsum=V((HC, T, T), F32), dqkv=V((3 * HW, T), BF), sm=V((8, D), F32), sm2=V((8, D), F32), sm3=V((8, D), F32), sm4=V((8, D), F32),
        smr=V((6, 8, D), F32), l_sem=dma(3), w_sem=dma(12), ws=V((3 * HW, D), BF), st=V((ways, T, D), BF), mask=V((T, 8), F32),
        gate=V((D, F), BF), up=V((D, F), BF), down=V((F, D), BF),
    )
    for name, n in dict(mem=4, wa=8, fz=8, fw=16, att=4, cot=5, nf=5, ng=4, near=12, do=4, fg=4, mg=4, sm=8, wg=18, wgc=5).items():
        scratch[name + "_s"] = dma(n)
        scratch[name + "_r"] = dma(n)
    for name, shape in summed.items():
        scratch[name + "_c"] = V(shape[1:], BF)
        scratch[name + "_x"] = V(shape[1:-3] + shape[-2:], BF)
        scratch[name + "_ok"] = pltpu.SemaphoreType.REGULAR
        for kind, n in dict(cs=2, cr=2, zs=3, zr=3).items():
            scratch[name + "_" + kind] = dma(n)
        scratch[name + "_as"] = dma(3)
        scratch[name + "_ar"] = dma(3)
    def phase(R):
        R.zin = zin
        whole_phase(R)
    G = types.SimpleNamespace(**run_kernel("block", [phase], ins, outs, scratch, 0))
    block_out = jnp.transpose(G.br, (1, 0, 2))
    memory_grad = jnp.transpose(G.mgo.astype(F32), (1, 0, 2))
    states_grad = jnp.transpose(G.sg.reshape(ways, tc, D), (1, 0, 2))
    sums = [x.astype(F32) for x in (G.gg, G.gd, G.ca, G.cb, G.se, G.smo, G.tg)]
    if not zin:
        sums = [lax.psum(x, "dp") for x in sums]
    gg, gd, ca, cb, se, sm, tg = sums
    gate_grad, up_grad = (gg[:, i].reshape(D, F) for i in range(2))
    down_grad = gd.reshape(F, D)
    ca, cb = (x.reshape(2, -1, half, D) for x in (ca, cb))
    cross = [x[:, i].reshape(HW, D) for x in (cb, ca) for i in range(x.shape[1])]
    own = se.reshape(3, HW, D)
    return (block_out, states_grad, memory_grad, sm[0], own[0].T, own[1].T, own[2].T, cross[SO], tg.T, sm[1],
            cross[CQ].T, cross[CK].T, cross[CV].T, cross[CO], sm[2], gate_grad, up_grad, down_grad)


def solution(mesh):
    seq = ("dp", "rep")
    col, row, tok = P(None, "mp"), P("mp", None), P("mp", seq, None)
    in_specs = (P(None, seq, None), tok, P(seq, None), P(seq), P(), col, col, col, row, col, P(), col, col, col, row,
                P(), col, col, row, tok)
    out_specs = (tok, tok, tok, P(), col, col, col, row, col, P(), col, col, col, row, P(), col, col, row)
    return jax.shard_map(per_device, mesh=mesh, in_specs=in_specs, out_specs=out_specs, check_vma=False)
```

```python
import math
import types

import jax
import jax.numpy as jnp
from jax import lax
from jax.experimental import pallas as pl
from jax.experimental.pallas import tpu as pltpu
from jax.sharding import PartitionSpec as P

eps = 1e-06
bucket_edges = [math.ceil(16 * 8 ** (level / 16)) for level in range(1, 16)]
BF = jnp.bfloat16
F32 = jnp.float32
NEG = -1e30
VMEM_BYTES = 64 * 2**20 - 2**17
MESH = pl.DeviceIdType.MESH
WAYS = 4
NEAR = (1, 2)
LEVELS = 4
CK, CV, SO, CQ, CO = range(5)
CROSS = ("cb", "ca", "cc")
RELAYED = ("gg", "gd")
GRAD_PARTS = ((0, 2), (2, 2), (4, 1))
PARTS = ((0, 2), (2, 3))


def dots(a, b, ca, cb):
    return lax.dot_general(a, b, (((ca,), (cb,)), ((), ())), preferred_element_type=F32)


def nn(a, b):
    return dots(a, b, 1, 0)


def nt(a, b):
    return dots(a, b, 1, 1)


def tn(a, b):
    return dots(a, b, 0, 0)


def rms(v, g):
    return v * lax.rsqrt(jnp.mean(v * v, axis=-1, keepdims=True) + eps) * g


def rms_back(v, g, n):
    r = lax.rsqrt(jnp.mean(v * v, axis=-1, keepdims=True) + eps)
    ng = n * g
    return r * ng - v * (r * r * r) * jnp.mean(ng * v, axis=-1, keepdims=True), n * v * r


def gelu_parts(a):
    c = math.sqrt(2 / math.pi)
    t = jnp.tanh(c * (a + 0.044715 * a * a * a))
    half = 0.5 * (1 + t)
    return half * a, half + 0.5 * a * (1 - t * t) * c * (1 + 3 * 0.044715 * a * a)


def place():
    return lax.axis_index("mp"), lax.axis_index("dp"), lax.axis_index("rep")


def peer(k):
    m, z, r = place()
    return (m ^ k, z, r)


def partner():
    m, z, r = place()
    return (m, z, 1 - r)


def level(k):
    m, z, r = place()
    return (m, z ^ k, r)


def greet(zin):
    barrier = pltpu.get_barrier_semaphore()
    known = [peer(k) for k in range(1, WAYS)] + [partner()]
    known += [level(k) for k in ((1, 2, 3) if zin else (1,))]
    for one in known:
        pl.semaphore_signal(barrier, inc=1, device_id=one, device_id_type=MESH)
    pl.semaphore_wait(barrier, len(known))


def send(src, dst, sems, at, to):
    return pltpu.make_async_remote_copy(
        src_ref=src, dst_ref=dst, send_sem=sems[0].at[at], recv_sem=sems[1].at[at], device_id=to, device_id_type=MESH
    )


def run_kernel(name, phases, ins, outs, scratch, cid, flops=0):
    names = list(ins) + list(outs) + list(scratch)

    def body(*refs):
        held = types.SimpleNamespace(**dict(zip(names, refs)))
        for phase in phases:
            phase(held)

    got = pl.pallas_call(
        body,
        name=name,
        out_shape=[jax.ShapeDtypeStruct(shape, dtype) for shape, dtype, _ in outs.values()],
        in_specs=[pl.BlockSpec(memory_space=space) for _, space in ins.values()],
        out_specs=[pl.BlockSpec(memory_space=space) for _, _, space in outs.values()],
        scratch_shapes=list(scratch.values()),
        compiler_params=pltpu.CompilerParams(
            collective_id=cid, has_side_effects=True, vmem_limit_bytes=VMEM_BYTES
        ),
        cost_estimate=pl.CostEstimate(flops=flops, bytes_accessed=flops // 200, transcendentals=0),
    )(*[array for array, _ in ins.values()])
    return dict(zip(outs, got))


V, ANY, SM = pltpu.VMEM, pl.ANY, pltpu.SMEM


def dma(*shape):
    return pltpu.SemaphoreType.DMA(shape)


def aligned(start, size):
    return pl.ds(pl.multiple_of(start, size), size)


def start_sends(R):
    m, z, r = place()
    quarter = R.mem_in.shape[0]
    HW = R.ck.shape[0]
    mine = aligned(m * HW, HW)
    R.own_w = [
        pltpu.make_async_copy(src, R.waf.at[i, mine], R.w_sem.at[i])
        for i, src in enumerate((R.ck, R.cv, R.so, R.cq, R.co))
    ]
    for copy in R.own_w:
        copy.start()
    R.own_s = [
        pltpu.make_async_copy(src, R.ws.at[pl.ds(i * HW, HW)], R.w_sem.at[5 + i])
        for i, src in enumerate((R.wq, R.wk, R.wv))
    ]
    for copy in R.own_s:
        copy.start()
    R.local = [
        pltpu.make_async_copy(R.gate_in, R.gate, R.w_sem.at[8]),
        pltpu.make_async_copy(R.up_in, R.up, R.w_sem.at[9]),
        pltpu.make_async_copy(R.down_in, R.down, R.w_sem.at[10]),
    ]
    for copy in R.local:
        copy.start()
    greet(R.zin)
    for copy in R.own_w:
        copy.wait()
    for part in range(len(PARTS)):
        for k in range(1, WAYS):
            wa_copy(R, part, k).start()
    pl.run_scoped(
        lambda *stages: by_sequence(R, *stages),
        pltpu.VMEM(R.mem_in.shape, BF),
        pltpu.VMEM(R.st_in.shape, BF),
        pltpu.VMEM(R.cot_in.shape, BF),
    )


def mem_copy(R, k):
    m, z, r = place()
    quarter = R.mem_in.shape[0]
    return send(R.part.at[m ^ k], R.memf.at[aligned(m * quarter, quarter)], (R.mem_s, R.mem_r), k, peer(k))


def by_sequence(R, memory, states, cotangent):
    m, z, r = place()
    quarter, W, D = memory.shape
    tc = cotangent.shape[0]
    copies = [
        pltpu.make_async_copy(src, dst, R.in_sem.at[n])
        for n, (src, dst) in enumerate(((R.mem_in, memory), (R.st_in, states), (R.cot_in, cotangent)))
    ]
    for copy in copies:
        copy.start()
    copies[0].wait()
    for s in range(W):
        R.part[s] = memory[:, s, :]
    for k in range(1, WAYS):
        mem_copy(R, k).start()
    R.memf[aligned(m * quarter, quarter)] = R.part[m]
    copies[1].wait()
    for s in range(W):
        R.st[s] = states[:, s, :]
    copies[2].wait()
    for s in range(W):
        R.upall[s, aligned(m * tc, tc)] = cotangent[:, s, :]


def quarter_rows(R, part, owner, core, half):
    HW = R.ck.shape[0]
    lo, n = PARTS[part]
    return R.waf.at[pl.ds(lo, n), aligned(owner * HW + core * (HW // 2) + half * (HW // 4), HW // 4)]


def wa_copy(R, part, k):
    m, z, r = place()
    view = quarter_rows(R, part, m, r, z & 1)
    return send(view, view, (R.wa_s, R.wa_r), part * WAYS + k, peer(k))


def fz_copy(R, part, k):
    m, z, r = place()
    view = quarter_rows(R, part, m ^ k, r, z & 1)
    return send(view, view, (R.fz_s, R.fz_r), part * WAYS + k, level(1))


def fw_copy(R, part, k, second):
    m, z, r = place()
    view = quarter_rows(R, part, m ^ k, r, (z & 1) ^ second)
    return send(view, view, (R.fw_s, R.fw_r), (second * 2 + part) * WAYS + k, partner())


def cot_copy(R, k):
    m, z, r = place()
    tc = R.cot_in.shape[0]
    view = R.upall.at[:, aligned(m * tc, tc)]
    return send(view, view, (R.cot_s, R.cot_r), k, peer(k))


def cot_relay(R, k):
    m, z, r = place()
    tc = R.cot_in.shape[0]
    view = R.upall.at[pl.ds(0 if k == 2 else 2, 2), aligned((m ^ k) * tc, tc)]
    return send(view, view, (R.cot_s, R.cot_r), 2 + k, peer(3 ^ k))


def send_cot(R):
    for k in NEAR:
        cot_copy(R, k).start()


def pass_cot(R):
    for k in NEAR:
        cot_copy(R, k).wait_recv()
        cot_relay(R, k).start()


def have_cot(R):
    for k in NEAR:
        cot_copy(R, k).wait_send()
        cot_relay(R, k).wait()


def forward(R, part):
    for k in range(1, WAYS):
        wa_copy(R, part, k).wait_recv()
        fz_copy(R, part, k).start()
        fw_copy(R, part, k, 0).start()


def forward_again(R, part):
    for k in range(1, WAYS):
        fz_copy(R, part, k).wait_recv()
        fw_copy(R, part, k, 1).start()


def gathered(R, part):
    for k in range(1, WAYS):
        wa_copy(R, part, k).wait_send()
        fz_copy(R, part, k).wait_send()
        fw_copy(R, part, k, 0).wait()
        fw_copy(R, part, k, 1).wait()


def self_allowed(R, s):
    T = R.st.shape[1]
    j = lax.broadcasted_iota(jnp.int32, (T, T), 0)
    i = lax.broadcasted_iota(jnp.int32, (T, T), 1)
    chosen = lax.broadcasted_iota(jnp.int32, R.mask.shape, 1) == s
    open_rows = jnp.sum(jnp.where(chosen, R.mask[...], 0), axis=1, keepdims=True)
    return (j == i) | ((j < i) & (open_rows != 0))


def buckets(R, T):
    shape = (R.table.shape[1], T)
    distance = lax.broadcasted_iota(jnp.int32, shape, 1)
    bucket = jnp.minimum(distance, 16)
    for edge in bucket_edges:
        bucket = bucket + (distance >= edge).astype(jnp.int32)
    return (bucket == lax.broadcasted_iota(jnp.int32, shape, 0)).astype(F32)


def self_setup(R):
    W, T, _ = R.st.shape
    by_distance = jnp.dot(R.table[...], buckets(R, T), precision=lax.Precision.HIGHEST, preferred_element_type=F32)
    for h in range(R.table.shape[0]):
        R.et[:, h * T : (h + 1) * T] = pltpu.roll(jnp.broadcast_to(by_distance[h : h + 1], (T, T)), 0, 1, stride=1, stride_axis=0)
    rows = R.mask_in[...].astype(F32)
    R.mask[...] = jnp.concatenate([rows, jnp.zeros((8 - W, T), F32)], axis=0).T
    for copy in R.own_s:
        copy.wait()


def only_head(rows, h, heads):
    zero = jnp.zeros(rows.shape, rows.dtype)
    return jnp.concatenate([rows if g == h else zero for g in range(heads)], axis=0)


def self_scores(R, s, h, allowed):
    heads = R.table.shape[0]
    hd = R.qs.shape[1] // heads
    rows = slice(h * hd, (h + 1) * hd)
    scores = nn(R.ks[s], only_head(R.qs[s, rows], h, heads)) + R.et[:, h * R.st.shape[1] : (h + 1) * R.st.shape[1]]
    return jnp.where(allowed, scores, NEG)


def self_forward(R):
    m, z, r = place()
    HW = R.ws.shape[0] // 3
    heads = R.table.shape[0]
    hd = HW // heads
    self_setup(R)

    def one(s):
        normed = rms(R.st[s].astype(F32), R.g_self[...][None]).astype(BF)
        R.qs[s] = nt(R.ws[0:HW], normed).astype(BF)
        R.ks[s] = nt(normed, R.ws[HW : 2 * HW]).astype(BF)
        R.kts[s] = nt(R.ws[HW : 2 * HW], normed).astype(BF)
        R.vts[s] = nt(R.ws[2 * HW : 3 * HW], normed).astype(BF)
        R.vs[s] = nt(normed, R.ws[2 * HW : 3 * HW]).astype(BF)
        allowed = self_allowed(R, s)
        for h in range(heads):
            rows = slice(h * hd, (h + 1) * hd)
            scores = self_scores(R, s, h, allowed)
            top = jnp.max(scores, axis=0, keepdims=True)
            weights = jnp.exp(scores - top)
            total = jnp.sum(weights, axis=0, keepdims=True)
            R.atp[s, rows] = (nn(R.vts[s, rows], weights.astype(BF)) * (1 / total)).astype(BF)
            R.lse_s[s, h] = top + jnp.log(total)

    def step(k, carry):
        one(m ^ k)
        att_copy(R, k).start()
        return carry

    lax.fori_loop(1, WAYS, step, 0)
    one(m)
    R.att[aligned(m * HW, HW)] = R.atp[m]


def att_copy(R, k):
    m, z, r = place()
    HW = R.ws.shape[0] // 3
    return send(R.atp.at[m ^ k], R.att.at[aligned(m * HW, HW)], (R.att_s, R.att_r), k, peer(k))


def cross_kv(R):
    for copy in R.local:
        copy.wait()
    for k in range(1, WAYS):
        mem_copy(R, k).wait()
    send_cot(R)
    gathered(R, 0)
    M = R.memf.shape[0]
    step = 256

    def rows(i, carry):
        at = aligned(i * step, step)
        block = R.memf[at]
        k = nt(block, R.waf[CK]).astype(BF)
        R.kc[at] = k
        v = nt(block, R.waf[CV]).astype(BF)
        R.vc[at] = v
        R.kct[:, at] = k.T
        R.vct[:, at] = v.T
        return carry

    lax.fori_loop(0, M // step, rows, 0)


def after_self(R):
    m, z, r = place()
    for k in range(1, WAYS):
        att_copy(R, k).wait()
    gathered(R, 1)
    first = R.st[m].astype(F32) + tn(R.att[...], R.waf[SO])
    R.sg[...] = first
    normed = rms(first, R.g_cross[...][None]).astype(BF)
    R.nc[...] = normed
    R.qc[...] = nt(R.waf[CQ], normed).astype(BF)


def both_heads(ref, p, hd):
    T = ref.shape[1]
    first, second = (ref[aligned(p * 2 * hd + a * hd, hd)] for a in range(2))
    zero = jnp.zeros((hd, T), BF)
    upper = jnp.concatenate([first, zero], axis=1)
    lower = jnp.concatenate([zero, second], axis=1)
    return jnp.concatenate([upper, lower], axis=0)


def cross_scores(R, p, hd):
    m, z, r = place()
    scores = nn(R.kc[:, aligned(p * 2 * hd, 2 * hd)], both_heads(R.qc, p, hd))
    live = lax.broadcasted_iota(jnp.int32, scores.shape, 0) < R.lens[m]
    return jnp.where(live, scores, NEG)


def cross_forward(R):
    hd = R.ws.shape[0] // 3 // R.table.shape[0]
    heads = R.qc.shape[0] // hd
    T = R.qc.shape[1]

    def pair(p, carry):
        scores = cross_scores(R, p, hd)
        top = jnp.max(scores, axis=0, keepdims=True)
        weights = jnp.exp(scores - top)
        total = jnp.sum(weights, axis=0, keepdims=True)
        scale = 1 / total
        low = weights.astype(BF)
        logsum = top + jnp.log(total)
        for a in range(2):
            rows = aligned(p * 2 * hd + a * hd, hd)
            lanes = slice(a * T, (a + 1) * T)
            R.attc[rows] = (nn(R.vct[rows], low[:, lanes]) * scale[:, lanes]).astype(BF)
        R.lse_c[p] = logsum
        return carry

    lax.fori_loop(0, heads // 2, pair, 0)


def nf_copy(R, k):
    m, z, r = place()
    return send(R.nall.at[m], R.nall.at[m], (R.nf_s, R.nf_r), k, peer(k))


def nf_relay(R, k):
    m, z, r = place()
    half = R.nall.shape[1] // 2
    view = R.nall.at[m ^ k, pl.ds(0 if k == 2 else half, half)]
    return send(view, view, (R.nf_s, R.nf_r), 2 + k, peer(3 ^ k))


def second_part(R):
    m, z, r = place()
    second = R.sg[...] + tn(R.attc[...], R.waf[CO])
    R.second[...] = second
    R.nall[m] = rms(second, R.g_ffn[...][None]).astype(BF)
    for k in NEAR:
        nf_copy(R, k).start()


def ng_first(R, k, relay):
    m, z, r = place()
    half = R.ngr.shape[1]
    source = R.part.at[m ^ 3 if relay else m ^ k, pl.ds((k - 1) * half, half)]
    n = 2 * (k - 1) + relay
    return send(source, R.ngr.at[n], (R.ng_s, R.ng_r), n, peer(k))


def ng_relay(R, k):
    m, z, r = place()
    half = R.ngr.shape[1]
    source = R.part.at[m ^ 3 ^ k, pl.ds((k - 1) * half, half)]
    return send(source, R.ngr.at[3 + k], (R.ng_s, R.ng_r), 3 + k, peer(3 ^ k))


def ng_pass(R):
    m, z, r = place()
    half = R.ngr.shape[1]
    for k in NEAR:
        ng_first(R, k, 1).wait()
        at = (m ^ 3 ^ k, pl.ds((k - 1) * half, half))
        R.part[at] = (R.part[at].astype(F32) + R.ngr[2 * k - 1].astype(F32)).astype(BF)
        ng_relay(R, k).start()


def ng_end(R):
    m, z, r = place()
    half = R.ngr.shape[1]
    rows = []
    for k in NEAR:
        ng_first(R, k, 0).wait()
        ng_relay(R, k).wait()
        own = R.part[m, pl.ds((k - 1) * half, half)].astype(F32)
        rows.append(own + R.ngr[2 * k - 2].astype(F32) + R.ngr[3 + k].astype(F32))
    return jnp.concatenate(rows, axis=0)


def first_copy(R, name, k, relay, tag):
    m, z, r = place()
    tc = R.near.shape[3]
    to = m ^ 3 if relay else m ^ k
    source = getattr(R, name).at[pl.ds(2 * (k - 1), 2), aligned(to * tc, tc)]
    return send(source, R.near.at[k - 1, relay], (R.near_s, R.near_r), tag + 2 * (k - 1) + relay, peer(k))


def relay_copy(R, name, k, tag):
    m, z, r = place()
    tc = R.near.shape[3]
    source = getattr(R, name).at[pl.ds(2 * (k - 1), 2), aligned((m ^ 3 ^ k) * tc, tc)]
    return send(source, R.far.at[k - 1], (R.near_s, R.near_r), tag + 3 + k, peer(3 ^ k))


def scatter_start(R, name, tag):
    for k in NEAR:
        first_copy(R, name, k, 1, tag).start()
    for k in NEAR:
        first_copy(R, name, k, 0, tag).start()


def scatter_pass(R, name, tag):
    m, z, r = place()
    tc = R.near.shape[3]
    source = getattr(R, name)
    for k in NEAR:
        first_copy(R, name, k, 1, tag).wait()
        at = (pl.ds(2 * (k - 1), 2), aligned((m ^ 3 ^ k) * tc, tc))
        source[at] = (source[at].astype(F32) + R.near[k - 1, 1].astype(F32)).astype(BF)
        relay_copy(R, name, k, tag).start()


def scatter_end(R, name, tag, k):
    m, z, r = place()
    tc = R.near.shape[3]
    first_copy(R, name, k, 0, tag).wait()
    relay_copy(R, name, k, tag).wait()
    own = getattr(R, name)[pl.ds(2 * (k - 1), 2), aligned(m * tc, tc)].astype(F32)
    return own + R.near[k - 1, 0].astype(F32) + R.far[k - 1].astype(F32)


def block_end(R):
    for k in NEAR:
        rows = scatter_end(R, "brp", 0, k).astype(BF)
        for n in range(2):
            R.br[:, 2 * (k - 1) + n, :] = rows[n]


def feed_forward(R):
    m, z, r = place()
    T = R.st.shape[1]
    F = R.down.shape[0]

    def one(s, extra):
        rows = aligned(s * T, T)
        n, up = R.nall[s], R.upall[s]
        gate, lift = nn(n, R.gate[...]), nn(n, R.up[...])
        value, slope = gelu_parts(gate)
        hidden = (value * lift).astype(BF)
        R.hid[rows] = hidden
        back = nt(up, R.down[...])
        gate_grad = (back * lift * slope).astype(BF)
        up_grad = (back * value).astype(BF)
        R.gu[rows, 0:F] = gate_grad
        R.gu[rows, F : 2 * F] = up_grad
        R.part[s] = (nt(gate_grad, R.gate[...]) + nt(up_grad, R.up[...])).astype(BF)
        branch = nn(hidden, R.down[...])
        R.brp[s] = (branch + R.second[...] if extra else branch).astype(BF)

    have_cot(R)
    one(m, True)
    for k in NEAR:
        nf_copy(R, k).wait_recv()
        nf_relay(R, k).start()
    for k in range(1, WAYS):
        if k == 3:
            for near in NEAR:
                nf_relay(R, near).wait()
        one(m ^ k, False)
        if k == 3:
            for near in NEAR:
                ng_first(R, near, 1).start()
        else:
            ng_first(R, k, 0).start()
    for k in NEAR:
        nf_copy(R, k).wait_send()


def ffn_grads(R):
    W, T, D = R.nall.shape
    F = R.down.shape[0]
    rows = R.nall[...].reshape(W * T, D)
    both = tn(rows, R.gu[...]).astype(BF)
    R.gg[:, 0] = both[:, 0:F].reshape(2, 2, D // 4, F)
    R.gg[:, 1] = both[:, F : 2 * F].reshape(2, 2, D // 4, F)
    R.gd[...] = tn(R.hid[...], R.upall[...].reshape(W * T, D)).astype(BF).reshape(2, 2, F // 4, D)


def core_start(R, name):
    m, z, r = place()
    source, sems = getattr(R, name), (getattr(R, name + "_cs"), getattr(R, name + "_cr"))
    copy = send(source.at[1 - r], getattr(R, name + "_c"), sems, 0, partner())
    copy.start()
    R.core[name] = copy


def core_sum(R, name):
    m, z, r = place()
    R.core[name].wait()
    source, other = getattr(R, name), getattr(R, name + "_c")
    source[r] = (source[r].astype(F32) + other[...].astype(F32)).astype(BF)
    ready(R, name)


def part_of(ref, p):
    return ref.at[p] if len(ref.shape) == 3 else ref.at[:, p]


def halves(R, name):
    m, z, r = place()
    whole, spare = getattr(R, name).at[r], getattr(R, name + "_c")
    return (spare, whole) if name in CROSS else (whole, spare)


def inward_copy(R, name, n):
    m, z, r = place()
    before, after = halves(R, name)
    p = (z >> 1) ^ 1 ^ n
    return send(part_of(before, p), part_of(after, p), (getattr(R, name + "_zs"), getattr(R, name + "_zr")), n, level(1))


def across_copy(R, name):
    m, z, r = place()
    sems = (getattr(R, name + "_zs"), getattr(R, name + "_zr"))
    return send(part_of(halves(R, name)[0], (z >> 1) ^ 1), getattr(R, name + "_x"), sems, 2, level(3))


def spread_copy(R, name, n):
    m, z, r = place()
    sems = (getattr(R, name + "_as"), getattr(R, name + "_ar"))
    relayed = name in RELAYED
    part = part_of(halves(R, name)[1], (z >> 1) ^ (0, 0, int(relayed))[n])
    return send(part, part, sems, n, level((3, 1, 1 if relayed else 2)[n]))


def ready(R, name):
    if R.zin and name not in CROSS:
        pl.semaphore_signal(getattr(R, name + "_ok"), inc=1, device_id=level(1), device_id_type=MESH)


def level_sum(R, name, step):
    m, z, r = place()
    before, after = halves(R, name)
    if not R.zin:
        if step == 0:
            after[...] = before[...]
        return
    inner = (z == 1) | (z == 2)
    mine, other = z >> 1, (z >> 1) ^ 1
    if step == 0:
        if name not in CROSS:
            pl.semaphore_wait(getattr(R, name + "_ok"), 1)

        @pl.when(jnp.logical_not(inner))
        def _():
            inward_copy(R, name, 0).start()
            inward_copy(R, name, 1).start()

    elif step == 1:

        @pl.when(inner)
        def _():
            inward_copy(R, name, 0).wait_recv()
            held = part_of(before, other)
            held[...] = (held[...].astype(F32) + part_of(after, other)[...].astype(F32)).astype(BF)
            across_copy(R, name).start()

    elif step == 2:

        @pl.when(inner)
        def _():
            inward_copy(R, name, 1).wait_recv()
            across_copy(R, name).wait()
            held = part_of(after, mine)
            total = held[...].astype(F32) + part_of(before, mine)[...].astype(F32)
            held[...] = (total + getattr(R, name + "_x")[...].astype(F32)).astype(BF)
            for n in range(2 if name in RELAYED else 3):
                spread_copy(R, name, n).start()

        @pl.when(jnp.logical_not(inner))
        def _():
            inward_copy(R, name, 0).wait_send()
            inward_copy(R, name, 1).wait_send()

    else:

        @pl.when(inner)
        def _():
            spread_copy(R, name, 0).wait_recv()
            spread_copy(R, name, 2).start()


def last_copy(R, name):
    m, z, r = place()
    mine = halves(R, name)[1]
    return send(mine, getattr(R, name).at[r], (getattr(R, name + "_cs"), getattr(R, name + "_cr")), 1, partner())


def last_start(R, name):
    m, z, r = place()
    if R.zin:
        inner = (z == 1) | (z == 2)

        @pl.when(inner)
        def _():
            for n in range(3):
                spread_copy(R, name, n).wait_send()
            if name not in RELAYED:
                spread_copy(R, name, 0).wait_recv()

        @pl.when(jnp.logical_not(inner))
        def _():
            for n in (1, 2):
                spread_copy(R, name, n).wait_recv()

    last_copy(R, name).start()
    if name not in CROSS:
        getattr(R, name)[r] = getattr(R, name + "_c")[...]


def wg_core(R, i):
    m, z, r = place()
    return send(R.wg.at[i, :, 1 - r], R.wgc.at[i], (R.wgc_s, R.wgc_r), i, partner())


def wg_part(R, part, k, owner):
    m, z, r = place()
    rows = R.wg.shape[3] // 2
    lo, n = GRAD_PARTS[part]
    return R.wg.at[pl.ds(lo, n), owner, r, pl.ds((k - 1) * rows, rows)]


def wg_first(R, part, k, relay):
    m, z, r = place()
    lo, n = GRAD_PARTS[part]
    source = wg_part(R, part, k, m ^ 3 if relay else m ^ k)
    sems = (R.wg_s, R.wg_r)
    return send(source, R.wgr.at[k - 1, relay, pl.ds(lo, n)], sems, 6 * part + 2 * (k - 1) + relay, peer(k))


def wg_relay(R, part, k):
    m, z, r = place()
    lo, n = GRAD_PARTS[part]
    source = wg_part(R, part, k, m ^ 3 ^ k)
    return send(source, R.wgr.at[k - 1, 2, pl.ds(lo, n)], (R.wg_s, R.wg_r), 6 * part + 3 + k, peer(3 ^ k))


def put_grad(R, i, value):
    D = value.shape[0]
    R.wg[i] = value.astype(BF).reshape(WAYS, 2, D // WAYS // 2, D)
    wg_core(R, i).start()


def wg_spread(R, part):
    m, z, r = place()
    lo, n = GRAD_PARTS[part]
    for i in range(lo, lo + n):
        wg_core(R, i).wait()
        for s in range(WAYS):
            R.wg[i, s, r] = (R.wg[i, s, r].astype(F32) + R.wgc[i, s].astype(F32)).astype(BF)
    for k in NEAR:
        wg_first(R, part, k, 1).start()
    for k in NEAR:
        wg_first(R, part, k, 0).start()


def wg_pass(R, part):
    m, z, r = place()
    lo, n = GRAD_PARTS[part]
    for k in NEAR:
        wg_first(R, part, k, 1).wait()
        place_of = wg_part(R, part, k, m ^ 3 ^ k)
        place_of[...] = (place_of[...].astype(F32) + R.wgr[k - 1, 1, lo : lo + n].astype(F32)).astype(BF)
        wg_relay(R, part, k).start()


def put_cross(R, i, k, value):
    buffer = getattr(R, CROSS[i // 2] + "_c")
    n, count = buffer.shape[1], value.shape[0]
    j, at = divmod((2 * (i % 2) + k - 1) * count, n)
    buffer[j, at : at + count] = value


def wg_collect(R, part):
    m, z, r = place()
    lo, n = GRAD_PARTS[part]
    rows = R.wg.shape[3] // 2
    for k in NEAR:
        wg_first(R, part, k, 0).wait()
        wg_relay(R, part, k).wait()
        total = wg_part(R, part, k, m)[...].astype(F32)
        total = total + R.wgr[k - 1, 0, lo : lo + n].astype(F32) + R.wgr[k - 1, 2, lo : lo + n].astype(F32)
        for i in range(n):
            put_cross(R, lo + i, k, total[i].astype(BF))


def second_back(R):
    m, z, r = place()
    grad = ng_end(R)
    scatter_start(R, "brp", 0)
    R.local = []
    back, gain = rms_back(R.second[...], R.g_ffn[...][None], grad)
    R.sm[...] = jnp.zeros(R.sm.shape, F32)
    R.sm[2:3] = jnp.sum(gain, axis=0, keepdims=True)
    total = R.upall[m].astype(F32) + back
    R.second[...] = total
    low = total.astype(BF)
    R.dot[...] = nt(R.waf[CO], low).astype(BF)
    put_grad(R, CO, nn(R.attc[...], low))


def cross_back(R, lo, hi):
    hd = R.ws.shape[0] // 3 // R.table.shape[0]
    T = R.qc.shape[1]

    def pair(p, carry):
        mix = jnp.exp(cross_scores(R, p, hd) - R.lse_c[p])
        low = mix.astype(BF)
        grad = nn(R.vc[:, aligned(p * 2 * hd, 2 * hd)], both_heads(R.dot, p, hd))
        delta = jnp.sum(mix * grad, axis=0, keepdims=True)
        score_grad = (mix * (grad - delta)).astype(BF)
        for a in range(2):
            rows = aligned(p * 2 * hd + a * hd, hd)
            lanes = slice(a * T, (a + 1) * T)
            value_grad = nt(R.dot[rows], low[:, lanes]).astype(BF)
            R.attc[rows] = nn(R.kct[rows], score_grad[:, lanes]).astype(BF)
            R.kct[rows] = value_grad
            R.vct[rows] = nt(R.qc[rows], score_grad[:, lanes]).astype(BF)
        return carry

    lax.fori_loop(lo, hi, pair, 0)


def do_copy(R, k):
    m, z, r = place()
    HW = R.ws.shape[0] // 3
    return send(R.dot.at[aligned((m ^ k) * HW, HW)], R.atp.at[m], (R.do_s, R.do_r), k, peer(k))


def fg_copy(R, k):
    m, z, r = place()
    tc = R.fgr.shape[1]
    return send(R.upall.at[0, aligned((m ^ k) * tc, tc)], R.fgr.at[m], (R.fg_s, R.fg_r), k, peer(k))


def first_back(R):
    m, z, r = place()
    HW = R.ws.shape[0] // 3
    tc = R.fgr.shape[1]
    back, gain = rms_back(R.sg[...], R.g_cross[...][None], tn(R.attc[...], R.waf[CQ]))
    R.sm[1:2] = jnp.sum(gain, axis=0, keepdims=True)
    low = (R.second[...] + back).astype(BF)
    R.upall[0] = low
    R.dot[...] = nt(R.waf[SO], low).astype(BF)
    for k in range(1, WAYS):
        do_copy(R, k).start()
    R.atp[m] = R.dot[aligned(m * HW, HW)]
    R.fgr[m] = R.upall[0, aligned(m * tc, tc)]
    put_grad(R, CQ, nn(R.attc[...], R.nc[...]))
    put_grad(R, SO, nn(R.att[...], low))


def mg_copy(R, k):
    m, z, r = place()
    quarter = R.mem_in.shape[0]
    return send(R.vc.at[aligned((m ^ k) * quarter, quarter)], R.kc.at[aligned(m * quarter, quarter)], (R.mg_s, R.mg_r), k, peer(k))


def memory_back(R):
    m, z, r = place()
    quarter = R.mem_in.shape[0]

    def rows(c):
        at = aligned(c * quarter, quarter)
        R.vc[at] = (tn(R.vct[:, at], R.waf[CK]) + tn(R.kct[:, at], R.waf[CV])).astype(BF)

    lax.fori_loop(0, WAYS, lambda c, carry: (rows(c), carry)[1], 0)


def memory_send(R):
    m, z, r = place()
    quarter = R.mem_in.shape[0]
    for k in range(1, WAYS):
        mg_copy(R, k).start()
    rows = aligned(m * quarter, quarter)
    R.kc[rows] = R.vc[rows]


def memory_end(R):
    W, quarter = R.st.shape[0], R.mem_in.shape[0]
    for k in range(1, WAYS):
        mg_copy(R, k).wait()
    copies = []
    for s in range(W):
        stage = (R.second, R.et)[s % 2]
        if s >= 2:
            copies[s - 2].wait()
        stage[...] = R.kc[s * quarter : (s + 1) * quarter].astype(F32)
        copies.append(pltpu.make_async_copy(stage, R.mgo.at[:, s], R.mg_out.at[s]))
        copies[s].start()
    R.local += copies[W - 2 :]


def kv_grads(R):
    put_grad(R, CK, nn(R.vct[...], R.memf[...]))
    put_grad(R, CV, nn(R.kct[...], R.memf[...]))


def self_back(R):
    m, z, r = place()
    T = R.st.shape[1]
    HW = R.ws.shape[0] // 3
    heads = R.table.shape[0]
    hd = HW // heads
    R.second[...] = jnp.zeros(R.second.shape, F32)

    def one(k):
        s = m ^ k
        at = aligned(s * T, T)
        allowed = self_allowed(R, s)
        for h in range(heads):
            rows = slice(h * hd, (h + 1) * hd)
            mix = jnp.exp(self_scores(R, s, h, allowed) - R.lse_s[s, h])
            out = R.atp[s, rows]
            grad = nn(R.vs[s], only_head(out, h, heads))
            delta = jnp.sum(mix * grad, axis=0, keepdims=True)
            score_grad = (mix * (grad - delta)).astype(BF)
            R.second[:, h * T : (h + 1) * T] += score_grad.astype(F32)
            R.gu[h * hd : (h + 1) * hd, at] = nn(R.kts[s, rows], score_grad).astype(BF)
            R.gu[HW + h * hd : HW + (h + 1) * hd, at] = nt(R.qs[s, rows], score_grad).astype(BF)
            R.gu[2 * HW + h * hd : 2 * HW + (h + 1) * hd, at] = nt(out, mix.astype(BF)).astype(BF)
        values = R.st[s].astype(F32)
        scaled = values * lax.rsqrt(jnp.mean(values * values, axis=-1, keepdims=True) + eps)
        R.nall[s] = (scaled * R.g_self[...][None]).astype(BF)
        grad = tn(R.gu[0 : 3 * HW, at], R.ws[...])
        R.sm[0:1] += jnp.sum(grad * scaled, axis=0, keepdims=True)
        R.part[s] = grad.astype(BF)

    one(0)

    def step(k, carry):
        do_copy(R, k).wait()
        one(k)
        return carry

    lax.fori_loop(1, WAYS, step, 0)
    W, _, D = R.nall.shape
    R.se[...] = nn(R.gu[0 : 3 * HW], R.nall[...].reshape(W * T, D)).astype(BF).reshape(R.se.shape)


def distance_sums(R):
    heads, T = R.table.shape[0], R.st.shape[1]
    j = lax.broadcasted_iota(jnp.int32, (T, T), 0)
    for h in range(heads):
        rows = R.second[:, h * T : (h + 1) * T]
        bit = 1
        while bit < T:
            rows = jnp.where((j & bit) != 0, pltpu.roll(rows, T - bit, 1), rows)
            bit *= 2
        R.sm[3:4, h * T : (h + 1) * T] = jnp.sum(rows, axis=0, keepdims=True)


def states_back(R):
    m, z, r = place()
    W, tc, D = R.fgr.shape
    for k in range(1, WAYS):
        fg_copy(R, k).wait()
    for k in NEAR:
        grad = scatter_end(R, "part", 6, k)
        for s in range(2 * (k - 1), 2 * k):
            values = R.st[s, aligned(m * tc, tc)].astype(F32)
            back, _ = rms_back(values, R.g_self[...][None], grad[s - 2 * (k - 1)])
            R.sg[s * tc : (s + 1) * tc] = R.fgr[s].astype(F32) + back
            copy = pltpu.make_async_copy(R.sg.at[pl.ds(s * tc, tc)], R.sgo.at[:, s], R.sg_sem.at[s])
            copy.start()
            R.local.append(copy)


def small_sums(R, step):
    m, z, r = place()
    if step == 0:
        R.sm_copies = [send(R.sm, R.smr.at[k - 1], (R.sm_s, R.sm_r), k, peer(k)) for k in range(1, WAYS)]
    elif step == 1:
        total = R.sm[...]
        gains = lax.broadcasted_iota(jnp.int32, total.shape, 0) < 3
        for k in range(1, WAYS):
            total = total + jnp.where(gains, R.smr[k - 1], 0)
        R.sm2[...] = total
        R.sm_copies = [send(R.sm2, R.smr.at[3], (R.sm_s, R.sm_r), 4, partner())]
    elif step == 2:
        R.sm3[...] = R.sm2[...] + R.smr[3]
        R.sm_copies = [send(R.sm3, R.smr.at[4], (R.sm_s, R.sm_r), 5, level(1))] if R.zin else []
    elif step == 3:
        R.sm4[...] = R.sm3[...] + R.smr[4] if R.zin else R.sm3[...]
        R.sm_copies = [send(R.sm4, R.smr.at[5], (R.sm_s, R.sm_r), 6, level(2))] if R.zin else []
    else:
        R.smo[...] = R.sm4[...] + R.smr[5] if R.zin else R.sm4[...]
        heads, T = R.table.shape[0], R.st.shape[1]
        by_distance = jnp.concatenate([R.smo[3:4, h * T : (h + 1) * T] for h in range(heads)], axis=0)
        R.tg[...] = lax.dot_general(
            by_distance, buckets(R, T), (((1,), (1,)), ((), ())), precision=lax.Precision.HIGHEST,
            preferred_element_type=F32,
        )
        return
    for copy in R.sm_copies:
        copy.start()


def small_wait(R):
    for copy in R.sm_copies:
        copy.wait()


def whole_phase(R):
    start_sends(R)
    self_forward(R)
    forward(R, 0)
    forward(R, 1)
    forward_again(R, 0)
    cross_kv(R)
    forward_again(R, 1)
    after_self(R)
    pass_cot(R)
    cross_forward(R)
    second_part(R)
    feed_forward(R)
    R.core = {}
    ffn_grads(R)
    core_start(R, "gg")
    core_start(R, "gd")
    ng_pass(R)
    core_sum(R, "gg")
    core_sum(R, "gd")
    level_sum(R, "gg", 0)
    level_sum(R, "gd", 0)
    second_back(R)
    pairs = R.lse_c.shape[0]
    cross_back(R, 0, 1)
    wg_spread(R, 2)
    cross_back(R, 1, 3)
    scatter_pass(R, "brp", 0)
    level_sum(R, "gg", 1)
    cross_back(R, 3, 4)
    wg_pass(R, 2)
    level_sum(R, "gd", 1)
    cross_back(R, 4, pairs)
    first_back(R)
    kv_grads(R)
    block_end(R)
    level_sum(R, "gg", 2)
    wg_spread(R, 1)
    wg_collect(R, 2)
    level_sum(R, "cc", 0)
    wg_spread(R, 0)
    level_sum(R, "gd", 2)
    memory_back(R)
    level_sum(R, "cc", 1)
    self_back(R)
    core_start(R, "se")
    wg_pass(R, 1)
    level_sum(R, "cc", 2)
    wg_pass(R, 0)
    core_sum(R, "se")
    wg_collect(R, 1)
    level_sum(R, "ca", 0)
    wg_collect(R, 0)
    level_sum(R, "cb", 0)
    scatter_start(R, "part", 6)
    level_sum(R, "se", 0)
    for k in range(1, WAYS):
        fg_copy(R, k).start()
    level_sum(R, "gg", 3)
    level_sum(R, "gd", 3)
    distance_sums(R)
    small_sums(R, 0)
    level_sum(R, "ca", 1)
    level_sum(R, "cb", 1)
    scatter_pass(R, "part", 6)
    memory_send(R)
    level_sum(R, "se", 1)
    small_wait(R)
    small_sums(R, 1)
    last_start(R, "gg")
    last_start(R, "gd")
    level_sum(R, "ca", 2)
    level_sum(R, "cb", 2)
    level_sum(R, "se", 2)
    small_wait(R)
    small_sums(R, 2)
    last_start(R, "cc")
    small_wait(R)
    small_sums(R, 3)
    last_start(R, "ca")
    last_start(R, "cb")
    small_wait(R)
    small_sums(R, 4)
    states_back(R)
    last_start(R, "se")
    memory_end(R)
    for copy in R.local:
        copy.wait()
    for name in ("gg", "gd", "se", "ca", "cb", "cc"):
        last_copy(R, name).wait()


def per_device(states, memory, target_mask, memory_length, norm_self, self_query, self_key, self_value, self_out,
               bias_table, norm_cross, cross_query, cross_key, cross_value, cross_out, norm_ffn, ffn_gate, ffn_up,
               ffn_down, cotangent):
    ways = WAYS
    zin = lax.axis_size("dp") == LEVELS
    T, _, D = states.shape
    HW = self_query.shape[1]
    HC = bias_table.shape[1]
    F = ffn_gate.shape[1]
    hd = HW // HC
    M = memory.shape[0] * ways
    heads = D // hd
    ins = dict(
        st_in=(states, ANY), mem_in=(memory, ANY), wq=(self_query.T, ANY), wk=(self_key.T, ANY), wv=(self_value.T, ANY),
        so=(self_out, ANY), cq=(cross_query.T, ANY), ck=(cross_key.T, ANY), cv=(cross_value.T, ANY),
        co=(cross_out, ANY), mask_in=(target_mask, V), table=(bias_table.T, V), lens=(memory_length, SM),
        g_self=(norm_self, V), g_cross=(norm_cross, V), g_ffn=(norm_ffn, V), cot_in=(cotangent, ANY), gate_in=(ffn_gate, ANY),
        up_in=(ffn_up, ANY), down_in=(ffn_down, ANY),
    )
    half = HW // 2
    summed = dict(
        gg=(2, 2, 2, D // 4, F), gd=(2, 2, F // 4, D), cb=(2, 2, half, D), ca=(2, 2, half, D), cc=(2, 2, half // 2, D),
        se=(2, 2, 3 * HW // 4, D),
    )
    tc = T // ways
    outs = dict(
        br=((tc, ways, D), BF, V), mgo=((M // ways, ways, D), F32, ANY), sgo=((tc, ways, D), F32, ANY),
        smo=((8, D), F32, V), tg=((HC, bias_table.shape[0]), F32, V),
    )
    outs.update((name, (shape, BF, V)) for name, shape in summed.items())
    scratch = dict(
        att=V((D, T), BF), qs=V((ways, HW, T), BF), ks=V((ways, T, HW), BF), kts=V((ways, HW, T), BF),
        vts=V((ways, HW, T), BF), vs=V((ways, T, HW), BF), lse_s=V((ways, HC, 1, T), F32),
        second=V((T, D), F32), nc=V((T, D), BF), qc=V((D, T), BF), kc=V((M, D), BF), kct=V((D, M), BF),
        vc=V((M, D), BF), vct=V((D, M), BF), lse_c=V((heads // 2, 1, 2 * T), F32), attc=V((D, T), BF), memf=V((M, D), BF),
        waf=V((5, D, D), BF), nall=V((ways, T, D), BF), upall=V((ways, T, D), BF), et=V((T, HC * T), F32),
        atp=V((ways, HW, T), BF), part=V((ways, T, D), BF), ngr=V((6, T // 2, D), BF), brp=V((ways, T, D), BF),
        hid=V((ways * T, F), BF), gu=V((ways * T, 2 * F), BF),
        wg=V((5, ways, 2, half, D), BF), wgc=V((5, ways, half, D), BF), wgr=V((2, 3, 5, half // 2, D), BF),
        dot=V((D, T), BF),
        fgr=V((ways, tc, D), BF), near=V((2, 2, 2, tc, D), BF), far=V((2, 2, tc, D), BF),
        sm=V((8, D), F32), sm2=V((8, D), F32), sm3=V((8, D), F32), sm4=V((8, D), F32),
        smr=V((6, 8, D), F32), w_sem=dma(11), in_sem=dma(3), sg_sem=dma(4), mg_out=dma(4), sg=V((T, D), F32), ws=V((3 * HW, D), BF), st=V((ways, T, D), BF), mask=V((T, 8), F32),
        gate=V((D, F), BF), up=V((D, F), BF), down=V((F, D), BF),
    )
    for name, n in dict(mem=4, wa=8, fz=8, fw=16, att=4, cot=5, nf=5, ng=6, near=12, do=4, fg=4, mg=4, sm=8, wg=18, wgc=5).items():
        scratch[name + "_s"] = dma(n)
        scratch[name + "_r"] = dma(n)
    for name, shape in summed.items():
        scratch[name + "_c"] = V(shape[1:], BF)
        scratch[name + "_x"] = V(shape[1:-3] + shape[-2:], BF)
        scratch[name + "_ok"] = pltpu.SemaphoreType.REGULAR
        for kind, n in dict(cs=2, cr=2, zs=3, zr=3).items():
            scratch[name + "_" + kind] = dma(n)
        scratch[name + "_as"] = dma(3)
        scratch[name + "_ar"] = dma(3)
    def phase(R):
        R.zin = zin
        whole_phase(R)
    G = types.SimpleNamespace(**run_kernel("block", [phase], ins, outs, scratch, 0))
    block_out = G.br
    memory_grad = G.mgo
    states_grad = G.sgo
    sums = [x.astype(F32) for x in (G.gg, G.gd, G.cb, G.ca, G.cc, G.se, G.smo, G.tg)]
    if not zin:
        sums = [lax.psum(x, "dp") for x in sums]
    gg, gd, cb, ca, cc, se, sm, tg = sums
    gate_grad, up_grad = (gg[:, i].reshape(D, F) for i in range(2))
    down_grad = gd.reshape(F, D)
    cross = [x.reshape(2, -1, half, D) for x in (cb, ca, cc)]
    cross = [x[:, i].reshape(HW, D) for x in cross for i in range(x.shape[1])]
    own = se.reshape(3, HW, D)
    return (block_out, states_grad, memory_grad, sm[0], own[0].T, own[1].T, own[2].T, cross[SO], tg.T, sm[1],
            cross[CQ].T, cross[CK].T, cross[CV].T, cross[CO], sm[2], gate_grad, up_grad, down_grad)


def solution(mesh):
    seq = ("dp", "rep")
    col, row, tok = P(None, "mp"), P("mp", None), P("mp", seq, None)
    in_specs = (P(None, seq, None), tok, P(seq, None), P(seq), P(), col, col, col, row, col, P(), col, col, col, row,
                P(), col, col, row, tok)
    out_specs = (tok, tok, tok, P(), col, col, col, row, col, P(), col, col, col, row, P(), col, col, row)
    return jax.shard_map(per_device, mesh=mesh, in_specs=in_specs, out_specs=out_specs, check_vma=False)
```

```python
import math
import types

import jax
import jax.numpy as jnp
from jax import lax
from jax.experimental import pallas as pl
from jax.experimental.pallas import tpu as pltpu
from jax.sharding import PartitionSpec as P

eps = 1e-06
bucket_edges = [math.ceil(16 * 8 ** (level / 16)) for level in range(1, 16)]
BF = jnp.bfloat16
F32 = jnp.float32
NEG = -1e30
VMEM_BYTES = 64 * 2**20 - 2**17
MESH = pl.DeviceIdType.MESH
WAYS = 4
NEAR = (1, 2)
LEVELS = 4
CK, CV, SO, CQ, CO = range(5)
CROSS = ("cb", "ca", "cc")
RELAYED = ("gg", "gd", "ca", "cb", "se")
GRAD_PARTS = ((0, 2), (2, 2), (4, 1))
PARTS = ((0, 2), (2, 3))


def dots(a, b, ca, cb):
    return lax.dot_general(a, b, (((ca,), (cb,)), ((), ())), preferred_element_type=F32)


def nn(a, b):
    return dots(a, b, 1, 0)


def nt(a, b):
    return dots(a, b, 1, 1)


def tn(a, b):
    return dots(a, b, 0, 0)


def rms(v, g):
    return v * lax.rsqrt(jnp.mean(v * v, axis=-1, keepdims=True) + eps) * g


def rms_back(v, g, n):
    r = lax.rsqrt(jnp.mean(v * v, axis=-1, keepdims=True) + eps)
    ng = n * g
    return r * ng - v * (r * r * r) * jnp.mean(ng * v, axis=-1, keepdims=True), n * v * r


def gelu_parts(a):
    c = math.sqrt(2 / math.pi)
    t = jnp.tanh(c * (a + 0.044715 * a * a * a))
    half = 0.5 * (1 + t)
    return half * a, half + 0.5 * a * (1 - t * t) * c * (1 + 3 * 0.044715 * a * a)


def place():
    return lax.axis_index("mp"), lax.axis_index("dp"), lax.axis_index("rep")


def peer(k):
    m, z, r = place()
    return (m ^ k, z, r)


def partner():
    m, z, r = place()
    return (m, z, 1 - r)


def level(k):
    m, z, r = place()
    return (m, z ^ k, r)


def greet(zin):
    barrier = pltpu.get_barrier_semaphore()
    known = [peer(k) for k in range(1, WAYS)] + [partner()]
    known += [level(k) for k in ((1, 2, 3) if zin else (1,))]
    for one in known:
        pl.semaphore_signal(barrier, inc=1, device_id=one, device_id_type=MESH)
    pl.semaphore_wait(barrier, len(known))


def send(src, dst, sems, at, to):
    return pltpu.make_async_remote_copy(
        src_ref=src, dst_ref=dst, send_sem=sems[0].at[at], recv_sem=sems[1].at[at], device_id=to, device_id_type=MESH
    )


def run_kernel(name, phases, ins, outs, scratch, cid, flops=0):
    names = list(ins) + list(outs) + list(scratch)

    def body(*refs):
        held = types.SimpleNamespace(**dict(zip(names, refs)))
        for phase in phases:
            phase(held)

    got = pl.pallas_call(
        body,
        name=name,
        out_shape=[jax.ShapeDtypeStruct(shape, dtype) for shape, dtype, _ in outs.values()],
        in_specs=[pl.BlockSpec(memory_space=space) for _, space in ins.values()],
        out_specs=[pl.BlockSpec(memory_space=space) for _, _, space in outs.values()],
        scratch_shapes=list(scratch.values()),
        compiler_params=pltpu.CompilerParams(
            collective_id=cid, has_side_effects=True, vmem_limit_bytes=VMEM_BYTES
        ),
        cost_estimate=pl.CostEstimate(flops=flops, bytes_accessed=flops // 200, transcendentals=0),
    )(*[array for array, _ in ins.values()])
    return dict(zip(outs, got))


V, ANY, SM = pltpu.VMEM, pl.ANY, pltpu.SMEM


def dma(*shape):
    return pltpu.SemaphoreType.DMA(shape)


def aligned(start, size):
    return pl.ds(pl.multiple_of(start, size), size)


def start_sends(R):
    m, z, r = place()
    quarter = R.mem_in.shape[0]
    HW = R.ck.shape[0]
    mine = aligned(m * HW, HW)
    R.own_w = [
        pltpu.make_async_copy(src, R.waf.at[i, mine], R.w_sem.at[i])
        for i, src in enumerate((R.ck, R.cv, R.so, R.cq, R.co))
    ]
    for copy in R.own_w:
        copy.start()
    R.own_s = [
        pltpu.make_async_copy(src, R.ws.at[pl.ds(i * HW, HW)], R.w_sem.at[5 + i])
        for i, src in enumerate((R.wq, R.wk, R.wv))
    ]
    for copy in R.own_s:
        copy.start()
    R.local = [
        pltpu.make_async_copy(R.gate_in, R.gate, R.w_sem.at[8]),
        pltpu.make_async_copy(R.up_in, R.up, R.w_sem.at[9]),
        pltpu.make_async_copy(R.down_in, R.down, R.w_sem.at[10]),
    ]
    for copy in R.local:
        copy.start()
    greet(R.zin)
    for copy in R.own_w:
        copy.wait()
    for part in range(len(PARTS)):
        for k in range(1, WAYS):
            wa_copy(R, part, k).start()
    pl.run_scoped(
        lambda *stages: by_sequence(R, *stages),
        pltpu.VMEM(R.mem_in.shape, BF),
        pltpu.VMEM(R.st_in.shape, BF),
        pltpu.VMEM(R.cot_in.shape, BF),
    )


def mem_copy(R, k):
    m, z, r = place()
    quarter = R.mem_in.shape[0]
    return send(R.part.at[m ^ k], R.memf.at[aligned(m * quarter, quarter)], (R.mem_s, R.mem_r), k, peer(k))


def by_sequence(R, memory, states, cotangent):
    m, z, r = place()
    quarter, W, D = memory.shape
    tc = cotangent.shape[0]
    copies = [
        pltpu.make_async_copy(src, dst, R.in_sem.at[n])
        for n, (src, dst) in enumerate(((R.mem_in, memory), (R.st_in, states), (R.cot_in, cotangent)))
    ]
    for copy in copies:
        copy.start()
    copies[0].wait()
    for s in range(W):
        R.part[s] = memory[:, s, :]
    for k in range(1, WAYS):
        mem_copy(R, k).start()
    R.memf[aligned(m * quarter, quarter)] = R.part[m]
    copies[1].wait()
    for s in range(W):
        R.st[s] = states[:, s, :]
    copies[2].wait()
    for s in range(W):
        R.upall[s, aligned(m * tc, tc)] = cotangent[:, s, :]


def quarter_rows(R, part, owner, core, half):
    HW = R.ck.shape[0]
    lo, n = PARTS[part]
    return R.waf.at[pl.ds(lo, n), aligned(owner * HW + core * (HW // 2) + half * (HW // 4), HW // 4)]


def wa_copy(R, part, k):
    m, z, r = place()
    view = quarter_rows(R, part, m, r, z & 1)
    return send(view, view, (R.wa_s, R.wa_r), part * WAYS + k, peer(k))


def fz_copy(R, part, k):
    m, z, r = place()
    view = quarter_rows(R, part, m ^ k, r, z & 1)
    return send(view, view, (R.fz_s, R.fz_r), part * WAYS + k, level(1))


def fw_copy(R, part, k, second):
    m, z, r = place()
    view = quarter_rows(R, part, m ^ k, r, (z & 1) ^ second)
    return send(view, view, (R.fw_s, R.fw_r), (second * 2 + part) * WAYS + k, partner())


def cot_copy(R, k):
    m, z, r = place()
    tc = R.cot_in.shape[0]
    view = R.upall.at[:, aligned(m * tc, tc)]
    return send(view, view, (R.cot_s, R.cot_r), k, peer(k))


def cot_relay(R, k):
    m, z, r = place()
    tc = R.cot_in.shape[0]
    view = R.upall.at[pl.ds(0 if k == 2 else 2, 2), aligned((m ^ k) * tc, tc)]
    return send(view, view, (R.cot_s, R.cot_r), 2 + k, peer(3 ^ k))


def send_cot(R):
    for k in NEAR:
        cot_copy(R, k).start()


def pass_cot(R):
    for k in NEAR:
        cot_copy(R, k).wait_recv()
        cot_relay(R, k).start()


def have_cot(R):
    for k in NEAR:
        cot_copy(R, k).wait_send()
        cot_relay(R, k).wait()


def forward(R, part):
    for k in range(1, WAYS):
        wa_copy(R, part, k).wait_recv()
        fz_copy(R, part, k).start()
        fw_copy(R, part, k, 0).start()


def forward_again(R, part):
    for k in range(1, WAYS):
        fz_copy(R, part, k).wait_recv()
        fw_copy(R, part, k, 1).start()


def gathered(R, part):
    for k in range(1, WAYS):
        wa_copy(R, part, k).wait_send()
        fz_copy(R, part, k).wait_send()
        fw_copy(R, part, k, 0).wait()
        fw_copy(R, part, k, 1).wait()


def self_allowed(R, s):
    T = R.st.shape[1]
    j = lax.broadcasted_iota(jnp.int32, (T, T), 0)
    i = lax.broadcasted_iota(jnp.int32, (T, T), 1)
    chosen = lax.broadcasted_iota(jnp.int32, R.mask.shape, 1) == s
    open_rows = jnp.sum(jnp.where(chosen, R.mask[...], 0), axis=1, keepdims=True)
    return (j == i) | ((j < i) & (open_rows != 0))


def buckets(R, T):
    shape = (R.table.shape[1], T)
    distance = lax.broadcasted_iota(jnp.int32, shape, 1)
    bucket = jnp.minimum(distance, 16)
    for edge in bucket_edges:
        bucket = bucket + (distance >= edge).astype(jnp.int32)
    return (bucket == lax.broadcasted_iota(jnp.int32, shape, 0)).astype(F32)


def self_setup(R):
    W, T, _ = R.st.shape
    by_distance = jnp.dot(R.table[...], buckets(R, T), precision=lax.Precision.HIGHEST, preferred_element_type=F32)
    for h in range(R.table.shape[0]):
        R.et[:, h * T : (h + 1) * T] = pltpu.roll(jnp.broadcast_to(by_distance[h : h + 1], (T, T)), 0, 1, stride=1, stride_axis=0)
    rows = R.mask_in[...].astype(F32)
    R.mask[...] = jnp.concatenate([rows, jnp.zeros((8 - W, T), F32)], axis=0).T
    for copy in R.own_s:
        copy.wait()


def only_head(rows, h, heads):
    zero = jnp.zeros(rows.shape, rows.dtype)
    return jnp.concatenate([rows if g == h else zero for g in range(heads)], axis=0)


def self_scores(R, s, h, allowed):
    heads = R.table.shape[0]
    hd = R.qs.shape[1] // heads
    rows = slice(h * hd, (h + 1) * hd)
    scores = nn(R.ks[s], only_head(R.qs[s, rows], h, heads)) + R.et[:, h * R.st.shape[1] : (h + 1) * R.st.shape[1]]
    return jnp.where(allowed, scores, NEG)


def self_forward(R):
    m, z, r = place()
    HW = R.ws.shape[0] // 3
    heads = R.table.shape[0]
    hd = HW // heads
    self_setup(R)

    def one(s):
        normed = rms(R.st[s].astype(F32), R.g_self[...][None]).astype(BF)
        R.qs[s] = nt(R.ws[0:HW], normed).astype(BF)
        R.ks[s] = nt(normed, R.ws[HW : 2 * HW]).astype(BF)
        R.kts[s] = nt(R.ws[HW : 2 * HW], normed).astype(BF)
        R.vts[s] = nt(R.ws[2 * HW : 3 * HW], normed).astype(BF)
        R.vs[s] = nt(normed, R.ws[2 * HW : 3 * HW]).astype(BF)
        allowed = self_allowed(R, s)
        for h in range(heads):
            rows = slice(h * hd, (h + 1) * hd)
            scores = self_scores(R, s, h, allowed)
            top = jnp.max(scores, axis=0, keepdims=True)
            weights = jnp.exp(scores - top)
            total = jnp.sum(weights, axis=0, keepdims=True)
            R.atp[s, rows] = (nn(R.vts[s, rows], weights.astype(BF)) * (1 / total)).astype(BF)
            R.lse_s[s, h] = top + jnp.log(total)

    def step(k, carry):
        one(m ^ k)
        att_copy(R, k).start()
        return carry

    lax.fori_loop(1, WAYS, step, 0)
    one(m)
    R.att[aligned(m * HW, HW)] = R.atp[m]


def att_copy(R, k):
    m, z, r = place()
    HW = R.ws.shape[0] // 3
    return send(R.atp.at[m ^ k], R.att.at[aligned(m * HW, HW)], (R.att_s, R.att_r), k, peer(k))


def cross_kv(R):
    for copy in R.local:
        copy.wait()
    for k in range(1, WAYS):
        mem_copy(R, k).wait()
    send_cot(R)
    gathered(R, 0)
    M = R.memf.shape[0]
    step = 256

    def rows(i, carry):
        at = aligned(i * step, step)
        block = R.memf[at]
        k = nt(block, R.waf[CK]).astype(BF)
        R.kc[at] = k
        v = nt(block, R.waf[CV]).astype(BF)
        R.vc[at] = v
        R.kct[:, at] = k.T
        R.vct[:, at] = v.T
        return carry

    lax.fori_loop(0, M // step, rows, 0)


def after_self(R):
    m, z, r = place()
    for k in range(1, WAYS):
        att_copy(R, k).wait()
    gathered(R, 1)
    first = R.st[m].astype(F32) + tn(R.att[...], R.waf[SO])
    R.sg[...] = first
    normed = rms(first, R.g_cross[...][None]).astype(BF)
    R.nc[...] = normed
    R.qc[...] = nt(R.waf[CQ], normed).astype(BF)


def both_heads(ref, p, hd):
    T = ref.shape[1]
    first, second = (ref[aligned(p * 2 * hd + a * hd, hd)] for a in range(2))
    zero = jnp.zeros((hd, T), BF)
    upper = jnp.concatenate([first, zero], axis=1)
    lower = jnp.concatenate([zero, second], axis=1)
    return jnp.concatenate([upper, lower], axis=0)


def cross_scores(R, p, hd):
    m, z, r = place()
    scores = nn(R.kc[:, aligned(p * 2 * hd, 2 * hd)], both_heads(R.qc, p, hd))
    live = lax.broadcasted_iota(jnp.int32, scores.shape, 0) < R.lens[m]
    return jnp.where(live, scores, NEG)


def cross_forward(R):
    hd = R.ws.shape[0] // 3 // R.table.shape[0]
    heads = R.qc.shape[0] // hd
    T = R.qc.shape[1]

    def pair(p, carry):
        scores = cross_scores(R, p, hd)
        top = jnp.max(scores, axis=0, keepdims=True)
        weights = jnp.exp(scores - top)
        total = jnp.sum(weights, axis=0, keepdims=True)
        scale = 1 / total
        low = weights.astype(BF)
        logsum = top + jnp.log(total)
        for a in range(2):
            rows = aligned(p * 2 * hd + a * hd, hd)
            lanes = slice(a * T, (a + 1) * T)
            R.attc[rows] = (nn(R.vct[rows], low[:, lanes]) * scale[:, lanes]).astype(BF)
        R.lse_c[p] = logsum
        return carry

    lax.fori_loop(0, heads // 2, pair, 0)


def nf_copy(R, k):
    m, z, r = place()
    return send(R.nall.at[m], R.nall.at[m], (R.nf_s, R.nf_r), k, peer(k))


def nf_relay(R, k):
    m, z, r = place()
    half = R.nall.shape[1] // 2
    view = R.nall.at[m ^ k, pl.ds(0 if k == 2 else half, half)]
    return send(view, view, (R.nf_s, R.nf_r), 2 + k, peer(3 ^ k))


def second_part(R):
    m, z, r = place()
    second = R.sg[...] + tn(R.attc[...], R.waf[CO])
    R.second[...] = second
    R.nall[m] = rms(second, R.g_ffn[...][None]).astype(BF)
    for k in NEAR:
        nf_copy(R, k).start()


def ng_first(R, k, relay):
    m, z, r = place()
    half = R.ngr.shape[1]
    source = R.part.at[m ^ 3 if relay else m ^ k, pl.ds((k - 1) * half, half)]
    n = 2 * (k - 1) + relay
    return send(source, R.ngr.at[n], (R.ng_s, R.ng_r), n, peer(k))


def ng_relay(R, k):
    m, z, r = place()
    half = R.ngr.shape[1]
    source = R.part.at[m ^ 3 ^ k, pl.ds((k - 1) * half, half)]
    return send(source, R.ngr.at[3 + k], (R.ng_s, R.ng_r), 3 + k, peer(3 ^ k))


def ng_pass(R):
    m, z, r = place()
    half = R.ngr.shape[1]
    for k in NEAR:
        ng_first(R, k, 1).wait()
        at = (m ^ 3 ^ k, pl.ds((k - 1) * half, half))
        R.part[at] = (R.part[at].astype(F32) + R.ngr[2 * k - 1].astype(F32)).astype(BF)
        ng_relay(R, k).start()


def ng_end(R):
    m, z, r = place()
    half = R.ngr.shape[1]
    rows = []
    for k in NEAR:
        ng_first(R, k, 0).wait()
        ng_relay(R, k).wait()
        own = R.part[m, pl.ds((k - 1) * half, half)].astype(F32)
        rows.append(own + R.ngr[2 * k - 2].astype(F32) + R.ngr[3 + k].astype(F32))
    return jnp.concatenate(rows, axis=0)


def first_copy(R, name, k, relay, tag):
    m, z, r = place()
    tc = R.near.shape[3]
    to = m ^ 3 if relay else m ^ k
    source = getattr(R, name).at[pl.ds(2 * (k - 1), 2), aligned(to * tc, tc)]
    return send(source, R.near.at[k - 1, relay], (R.near_s, R.near_r), tag + 2 * (k - 1) + relay, peer(k))


def relay_copy(R, name, k, tag):
    m, z, r = place()
    tc = R.near.shape[3]
    source = getattr(R, name).at[pl.ds(2 * (k - 1), 2), aligned((m ^ 3 ^ k) * tc, tc)]
    return send(source, R.far.at[k - 1], (R.near_s, R.near_r), tag + 3 + k, peer(3 ^ k))


def scatter_start(R, name, tag):
    for k in NEAR:
        first_copy(R, name, k, 1, tag).start()
    for k in NEAR:
        first_copy(R, name, k, 0, tag).start()


def scatter_pass(R, name, tag):
    m, z, r = place()
    tc = R.near.shape[3]
    source = getattr(R, name)
    for k in NEAR:
        first_copy(R, name, k, 1, tag).wait()
        at = (pl.ds(2 * (k - 1), 2), aligned((m ^ 3 ^ k) * tc, tc))
        source[at] = (source[at].astype(F32) + R.near[k - 1, 1].astype(F32)).astype(BF)
        relay_copy(R, name, k, tag).start()


def scatter_end(R, name, tag, k):
    m, z, r = place()
    tc = R.near.shape[3]
    first_copy(R, name, k, 0, tag).wait()
    relay_copy(R, name, k, tag).wait()
    own = getattr(R, name)[pl.ds(2 * (k - 1), 2), aligned(m * tc, tc)].astype(F32)
    return own + R.near[k - 1, 0].astype(F32) + R.far[k - 1].astype(F32)


def block_end(R):
    for k in NEAR:
        rows = scatter_end(R, "brp", 0, k).astype(BF)
        for n in range(2):
            R.br[:, 2 * (k - 1) + n, :] = rows[n]


def feed_forward(R):
    m, z, r = place()
    T = R.st.shape[1]
    F = R.down.shape[0]

    def one(s, extra):
        rows = aligned(s * T, T)
        n, up = R.nall[s], R.upall[s]
        gate, lift = nn(n, R.gate[...]), nn(n, R.up[...])
        value, slope = gelu_parts(gate)
        hidden = (value * lift).astype(BF)
        R.hid[rows] = hidden
        back = nt(up, R.down[...])
        gate_grad = (back * lift * slope).astype(BF)
        up_grad = (back * value).astype(BF)
        R.gu[rows, 0:F] = gate_grad
        R.gu[rows, F : 2 * F] = up_grad
        R.part[s] = (nt(gate_grad, R.gate[...]) + nt(up_grad, R.up[...])).astype(BF)
        branch = nn(hidden, R.down[...])
        R.brp[s] = (branch + R.second[...] if extra else branch).astype(BF)

    have_cot(R)
    one(m, True)
    for k in NEAR:
        nf_copy(R, k).wait_recv()
        nf_relay(R, k).start()
    for k in range(1, WAYS):
        if k == 3:
            for near in NEAR:
                nf_relay(R, near).wait()
        one(m ^ k, False)
        if k == 3:
            for near in NEAR:
                ng_first(R, near, 1).start()
        else:
            ng_first(R, k, 0).start()
    for k in NEAR:
        nf_copy(R, k).wait_send()


def ffn_grads(R):
    W, T, D = R.nall.shape
    F = R.down.shape[0]
    rows = R.nall[...].reshape(W * T, D)
    both = tn(rows, R.gu[...]).astype(BF)
    R.gg[:, 0] = both[:, 0:F].reshape(2, 2, D // 4, F)
    R.gg[:, 1] = both[:, F : 2 * F].reshape(2, 2, D // 4, F)
    R.gd[...] = tn(R.hid[...], R.upall[...].reshape(W * T, D)).astype(BF).reshape(2, 2, F // 4, D)


def core_start(R, name):
    m, z, r = place()
    source, sems = getattr(R, name), (getattr(R, name + "_cs"), getattr(R, name + "_cr"))
    copy = send(source.at[1 - r], getattr(R, name + "_c"), sems, 0, partner())
    copy.start()
    R.core[name] = copy


def core_sum(R, name):
    m, z, r = place()
    R.core[name].wait()
    source, other = getattr(R, name), getattr(R, name + "_c")
    source[r] = (source[r].astype(F32) + other[...].astype(F32)).astype(BF)
    ready(R, name)


def part_of(ref, p):
    return ref.at[p] if len(ref.shape) == 3 else ref.at[:, p]


def halves(R, name):
    m, z, r = place()
    whole, spare = getattr(R, name).at[r], getattr(R, name + "_c")
    return (spare, whole) if name in CROSS else (whole, spare)


def inward_copy(R, name, n):
    m, z, r = place()
    before, after = halves(R, name)
    p = (z >> 1) ^ 1 ^ n
    return send(part_of(before, p), part_of(after, p), (getattr(R, name + "_zs"), getattr(R, name + "_zr")), n, level(1))


def across_copy(R, name):
    m, z, r = place()
    sems = (getattr(R, name + "_zs"), getattr(R, name + "_zr"))
    return send(part_of(halves(R, name)[0], (z >> 1) ^ 1), getattr(R, name + "_x"), sems, 2, level(3))


def spread_copy(R, name, n):
    m, z, r = place()
    sems = (getattr(R, name + "_as"), getattr(R, name + "_ar"))
    relayed = name in RELAYED
    part = part_of(halves(R, name)[1], (z >> 1) ^ (0, 0, int(relayed))[n])
    return send(part, part, sems, n, level((3, 1, 1 if relayed else 2)[n]))


def ready(R, name):
    if R.zin and name not in CROSS:
        pl.semaphore_signal(getattr(R, name + "_ok"), inc=1, device_id=level(1), device_id_type=MESH)


def level_sum(R, name, step):
    m, z, r = place()
    before, after = halves(R, name)
    if not R.zin:
        if step == 0:
            after[...] = before[...]
        return
    inner = (z == 1) | (z == 2)
    mine, other = z >> 1, (z >> 1) ^ 1
    if step == 0:
        if name not in CROSS:
            pl.semaphore_wait(getattr(R, name + "_ok"), 1)

        @pl.when(jnp.logical_not(inner))
        def _():
            inward_copy(R, name, 0).start()

    elif step == 1:

        @pl.when(inner)
        def _():
            inward_copy(R, name, 0).wait_recv()
            held = part_of(before, other)
            held[...] = (held[...].astype(F32) + part_of(after, other)[...].astype(F32)).astype(BF)
            across_copy(R, name).start()

        @pl.when(jnp.logical_not(inner))
        def _():
            inward_copy(R, name, 0).wait_send()
            inward_copy(R, name, 1).start()

    elif step == 2:

        @pl.when(inner)
        def _():
            inward_copy(R, name, 1).wait_recv()
            across_copy(R, name).wait()
            held = part_of(after, mine)
            total = held[...].astype(F32) + part_of(before, mine)[...].astype(F32)
            held[...] = (total + getattr(R, name + "_x")[...].astype(F32)).astype(BF)
            for n in range(2 if name in RELAYED else 3):
                spread_copy(R, name, n).start()

        @pl.when(jnp.logical_not(inner))
        def _():
            inward_copy(R, name, 1).wait_send()

    else:

        @pl.when(inner)
        def _():
            spread_copy(R, name, 0).wait_recv()
            spread_copy(R, name, 2).start()


def last_copy(R, name):
    m, z, r = place()
    mine = halves(R, name)[1]
    return send(mine, getattr(R, name).at[r], (getattr(R, name + "_cs"), getattr(R, name + "_cr")), 1, partner())


def last_start(R, name):
    m, z, r = place()
    if R.zin:
        inner = (z == 1) | (z == 2)

        @pl.when(inner)
        def _():
            for n in range(3):
                spread_copy(R, name, n).wait_send()
            if name not in RELAYED:
                spread_copy(R, name, 0).wait_recv()

        @pl.when(jnp.logical_not(inner))
        def _():
            for n in (1, 2):
                spread_copy(R, name, n).wait_recv()

    last_copy(R, name).start()
    if name not in CROSS:
        getattr(R, name)[r] = getattr(R, name + "_c")[...]


def wg_core(R, i):
    m, z, r = place()
    return send(R.wg.at[i, :, 1 - r], R.wgc.at[i], (R.wgc_s, R.wgc_r), i, partner())


def wg_part(R, part, k, owner):
    m, z, r = place()
    rows = R.wg.shape[3] // 2
    lo, n = GRAD_PARTS[part]
    return R.wg.at[pl.ds(lo, n), owner, r, pl.ds((k - 1) * rows, rows)]


def wg_first(R, part, k, relay):
    m, z, r = place()
    lo, n = GRAD_PARTS[part]
    source = wg_part(R, part, k, m ^ 3 if relay else m ^ k)
    sems = (R.wg_s, R.wg_r)
    return send(source, R.wgr.at[k - 1, relay, pl.ds(lo, n)], sems, 6 * part + 2 * (k - 1) + relay, peer(k))


def wg_relay(R, part, k):
    m, z, r = place()
    lo, n = GRAD_PARTS[part]
    source = wg_part(R, part, k, m ^ 3 ^ k)
    return send(source, R.wgr.at[k - 1, 2, pl.ds(lo, n)], (R.wg_s, R.wg_r), 6 * part + 3 + k, peer(3 ^ k))


def put_grad(R, i, value):
    D = value.shape[0]
    R.wg[i] = value.astype(BF).reshape(WAYS, 2, D // WAYS // 2, D)
    wg_core(R, i).start()


def wg_spread(R, part):
    m, z, r = place()
    lo, n = GRAD_PARTS[part]
    for i in range(lo, lo + n):
        wg_core(R, i).wait()
        for s in range(WAYS):
            R.wg[i, s, r] = (R.wg[i, s, r].astype(F32) + R.wgc[i, s].astype(F32)).astype(BF)
    for k in NEAR:
        wg_first(R, part, k, 1).start()
    for k in NEAR:
        wg_first(R, part, k, 0).start()


def wg_pass(R, part):
    m, z, r = place()
    lo, n = GRAD_PARTS[part]
    for k in NEAR:
        wg_first(R, part, k, 1).wait()
        place_of = wg_part(R, part, k, m ^ 3 ^ k)
        place_of[...] = (place_of[...].astype(F32) + R.wgr[k - 1, 1, lo : lo + n].astype(F32)).astype(BF)
        wg_relay(R, part, k).start()


def put_cross(R, i, k, value):
    buffer = getattr(R, CROSS[i // 2] + "_c")
    n, count = buffer.shape[1], value.shape[0]
    j, at = divmod((2 * (i % 2) + k - 1) * count, n)
    buffer[j, at : at + count] = value


def wg_collect(R, part):
    m, z, r = place()
    lo, n = GRAD_PARTS[part]
    rows = R.wg.shape[3] // 2
    for k in NEAR:
        wg_first(R, part, k, 0).wait()
        wg_relay(R, part, k).wait()
        total = wg_part(R, part, k, m)[...].astype(F32)
        total = total + R.wgr[k - 1, 0, lo : lo + n].astype(F32) + R.wgr[k - 1, 2, lo : lo + n].astype(F32)
        for i in range(n):
            put_cross(R, lo + i, k, total[i].astype(BF))


def second_back(R):
    m, z, r = place()
    grad = ng_end(R)
    scatter_start(R, "brp", 0)
    R.local = []
    back, gain = rms_back(R.second[...], R.g_ffn[...][None], grad)
    R.sm[...] = jnp.zeros(R.sm.shape, F32)
    R.sm[2:3] = jnp.sum(gain, axis=0, keepdims=True)
    total = R.upall[m].astype(F32) + back
    R.second[...] = total
    low = total.astype(BF)
    R.dot[...] = nt(R.waf[CO], low).astype(BF)
    put_grad(R, CO, nn(R.attc[...], low))


def cross_back(R, lo, hi):
    hd = R.ws.shape[0] // 3 // R.table.shape[0]
    T = R.qc.shape[1]

    def pair(p, carry):
        mix = jnp.exp(cross_scores(R, p, hd) - R.lse_c[p])
        low = mix.astype(BF)
        grad = nn(R.vc[:, aligned(p * 2 * hd, 2 * hd)], both_heads(R.dot, p, hd))
        delta = jnp.sum(mix * grad, axis=0, keepdims=True)
        score_grad = (mix * (grad - delta)).astype(BF)
        for a in range(2):
            rows = aligned(p * 2 * hd + a * hd, hd)
            lanes = slice(a * T, (a + 1) * T)
            value_grad = nt(R.dot[rows], low[:, lanes]).astype(BF)
            R.attc[rows] = nn(R.kct[rows], score_grad[:, lanes]).astype(BF)
            R.kct[rows] = value_grad
            R.vct[rows] = nt(R.qc[rows], score_grad[:, lanes]).astype(BF)
        return carry

    lax.fori_loop(lo, hi, pair, 0)


def do_copy(R, k):
    m, z, r = place()
    HW = R.ws.shape[0] // 3
    return send(R.dot.at[aligned((m ^ k) * HW, HW)], R.atp.at[m], (R.do_s, R.do_r), k, peer(k))


def fg_copy(R, k):
    m, z, r = place()
    tc = R.fgr.shape[1]
    return send(R.upall.at[0, aligned((m ^ k) * tc, tc)], R.fgr.at[m], (R.fg_s, R.fg_r), k, peer(k))


def first_back(R):
    m, z, r = place()
    HW = R.ws.shape[0] // 3
    tc = R.fgr.shape[1]
    back, gain = rms_back(R.sg[...], R.g_cross[...][None], tn(R.attc[...], R.waf[CQ]))
    R.sm[1:2] = jnp.sum(gain, axis=0, keepdims=True)
    low = (R.second[...] + back).astype(BF)
    R.upall[0] = low
    R.dot[...] = nt(R.waf[SO], low).astype(BF)
    for k in range(1, WAYS):
        do_copy(R, k).start()
    R.atp[m] = R.dot[aligned(m * HW, HW)]
    R.fgr[m] = R.upall[0, aligned(m * tc, tc)]
    put_grad(R, CQ, nn(R.attc[...], R.nc[...]))
    put_grad(R, SO, nn(R.att[...], low))


def mg_copy(R, k):
    m, z, r = place()
    quarter = R.mem_in.shape[0]
    return send(R.vc.at[aligned((m ^ k) * quarter, quarter)], R.kc.at[aligned(m * quarter, quarter)], (R.mg_s, R.mg_r), k, peer(k))


def memory_back(R):
    m, z, r = place()
    quarter = R.mem_in.shape[0]

    def rows(c):
        at = aligned(c * quarter, quarter)
        R.vc[at] = (tn(R.vct[:, at], R.waf[CK]) + tn(R.kct[:, at], R.waf[CV])).astype(BF)

    lax.fori_loop(0, WAYS, lambda c, carry: (rows(c), carry)[1], 0)


def memory_send(R):
    m, z, r = place()
    quarter = R.mem_in.shape[0]
    for k in range(1, WAYS):
        mg_copy(R, k).start()
    rows = aligned(m * quarter, quarter)
    R.kc[rows] = R.vc[rows]


def memory_end(R):
    W, quarter = R.st.shape[0], R.mem_in.shape[0]
    for k in range(1, WAYS):
        mg_copy(R, k).wait()
    copies = []
    for s in range(W):
        stage = (R.second, R.et)[s % 2]
        if s >= 2:
            copies[s - 2].wait()
        stage[...] = R.kc[s * quarter : (s + 1) * quarter].astype(F32)
        copies.append(pltpu.make_async_copy(stage, R.mgo.at[:, s], R.mg_out.at[s]))
        copies[s].start()
    R.local += copies[W - 2 :]


def kv_grads(R):
    put_grad(R, CK, nn(R.vct[...], R.memf[...]))
    put_grad(R, CV, nn(R.kct[...], R.memf[...]))


def self_back(R):
    m, z, r = place()
    T = R.st.shape[1]
    HW = R.ws.shape[0] // 3
    heads = R.table.shape[0]
    hd = HW // heads
    R.second[...] = jnp.zeros(R.second.shape, F32)

    def one(k):
        s = m ^ k
        at = aligned(s * T, T)
        allowed = self_allowed(R, s)
        for h in range(heads):
            rows = slice(h * hd, (h + 1) * hd)
            mix = jnp.exp(self_scores(R, s, h, allowed) - R.lse_s[s, h])
            out = R.atp[s, rows]
            grad = nn(R.vs[s], only_head(out, h, heads))
            delta = jnp.sum(mix * grad, axis=0, keepdims=True)
            score_grad = (mix * (grad - delta)).astype(BF)
            R.second[:, h * T : (h + 1) * T] += score_grad.astype(F32)
            R.gu[h * hd : (h + 1) * hd, at] = nn(R.kts[s, rows], score_grad).astype(BF)
            R.gu[HW + h * hd : HW + (h + 1) * hd, at] = nt(R.qs[s, rows], score_grad).astype(BF)
            R.gu[2 * HW + h * hd : 2 * HW + (h + 1) * hd, at] = nt(out, mix.astype(BF)).astype(BF)
        values = R.st[s].astype(F32)
        scaled = values * lax.rsqrt(jnp.mean(values * values, axis=-1, keepdims=True) + eps)
        R.nall[s] = (scaled * R.g_self[...][None]).astype(BF)
        grad = tn(R.gu[0 : 3 * HW, at], R.ws[...])
        R.sm[0:1] += jnp.sum(grad * scaled, axis=0, keepdims=True)
        R.part[s] = grad.astype(BF)

    one(0)

    def step(k, carry):
        do_copy(R, k).wait()
        one(k)
        return carry

    lax.fori_loop(1, WAYS, step, 0)
    W, _, D = R.nall.shape
    R.se[...] = nn(R.gu[0 : 3 * HW], R.nall[...].reshape(W * T, D)).astype(BF).reshape(R.se.shape)


def distance_sums(R):
    heads, T = R.table.shape[0], R.st.shape[1]
    j = lax.broadcasted_iota(jnp.int32, (T, T), 0)
    for h in range(heads):
        rows = R.second[:, h * T : (h + 1) * T]
        bit = 1
        while bit < T:
            rows = jnp.where((j & bit) != 0, pltpu.roll(rows, T - bit, 1), rows)
            bit *= 2
        R.sm[3:4, h * T : (h + 1) * T] = jnp.sum(rows, axis=0, keepdims=True)


def states_back(R):
    m, z, r = place()
    W, tc, D = R.fgr.shape
    for k in range(1, WAYS):
        fg_copy(R, k).wait()
    for k in NEAR:
        grad = scatter_end(R, "part", 6, k)
        for s in range(2 * (k - 1), 2 * k):
            values = R.st[s, aligned(m * tc, tc)].astype(F32)
            back, _ = rms_back(values, R.g_self[...][None], grad[s - 2 * (k - 1)])
            R.sg[s * tc : (s + 1) * tc] = R.fgr[s].astype(F32) + back
            copy = pltpu.make_async_copy(R.sg.at[pl.ds(s * tc, tc)], R.sgo.at[:, s], R.sg_sem.at[s])
            copy.start()
            R.local.append(copy)


def small_sums(R, step):
    m, z, r = place()
    if step == 0:
        R.sm_copies = [send(R.sm, R.smr.at[k - 1], (R.sm_s, R.sm_r), k, peer(k)) for k in range(1, WAYS)]
    elif step == 1:
        total = R.sm[...]
        gains = lax.broadcasted_iota(jnp.int32, total.shape, 0) < 3
        for k in range(1, WAYS):
            total = total + jnp.where(gains, R.smr[k - 1], 0)
        R.sm2[...] = total
        R.sm_copies = [send(R.sm2, R.smr.at[3], (R.sm_s, R.sm_r), 4, partner())]
    elif step == 2:
        R.sm3[...] = R.sm2[...] + R.smr[3]
        R.sm_copies = [send(R.sm3, R.smr.at[4], (R.sm_s, R.sm_r), 5, level(1))] if R.zin else []
    elif step == 3:
        R.sm4[...] = R.sm3[...] + R.smr[4] if R.zin else R.sm3[...]
        R.sm_copies = [send(R.sm4, R.smr.at[5], (R.sm_s, R.sm_r), 6, level(2))] if R.zin else []
    else:
        R.smo[...] = R.sm4[...] + R.smr[5] if R.zin else R.sm4[...]
        heads, T = R.table.shape[0], R.st.shape[1]
        by_distance = jnp.concatenate([R.smo[3:4, h * T : (h + 1) * T] for h in range(heads)], axis=0)
        R.tg[...] = lax.dot_general(
            by_distance, buckets(R, T), (((1,), (1,)), ((), ())), precision=lax.Precision.HIGHEST,
            preferred_element_type=F32,
        )
        return
    for copy in R.sm_copies:
        copy.start()


def small_wait(R):
    for copy in R.sm_copies:
        copy.wait()


def whole_phase(R):
    start_sends(R)
    self_forward(R)
    forward(R, 0)
    forward(R, 1)
    forward_again(R, 0)
    cross_kv(R)
    forward_again(R, 1)
    after_self(R)
    pass_cot(R)
    cross_forward(R)
    second_part(R)
    feed_forward(R)
    R.core = {}
    ffn_grads(R)
    core_start(R, "gg")
    core_start(R, "gd")
    ng_pass(R)
    core_sum(R, "gg")
    core_sum(R, "gd")
    level_sum(R, "gg", 0)
    level_sum(R, "gd", 0)
    second_back(R)
    pairs = R.lse_c.shape[0]
    cross_back(R, 0, 1)
    wg_spread(R, 2)
    cross_back(R, 1, 3)
    scatter_pass(R, "brp", 0)
    level_sum(R, "gg", 1)
    cross_back(R, 3, 4)
    wg_pass(R, 2)
    level_sum(R, "gd", 1)
    cross_back(R, 4, pairs)
    first_back(R)
    kv_grads(R)
    block_end(R)
    level_sum(R, "gg", 2)
    wg_spread(R, 1)
    wg_collect(R, 2)
    level_sum(R, "cc", 0)
    wg_spread(R, 0)
    level_sum(R, "gd", 2)
    memory_back(R)
    level_sum(R, "cc", 1)
    self_back(R)
    core_start(R, "se")
    wg_pass(R, 1)
    level_sum(R, "cc", 2)
    wg_pass(R, 0)
    core_sum(R, "se")
    wg_collect(R, 1)
    level_sum(R, "ca", 0)
    wg_collect(R, 0)
    level_sum(R, "cb", 0)
    level_sum(R, "se", 0)
    scatter_start(R, "part", 6)
    for k in range(1, WAYS):
        fg_copy(R, k).start()
    level_sum(R, "gg", 3)
    level_sum(R, "gd", 3)
    distance_sums(R)
    small_sums(R, 0)
    level_sum(R, "ca", 1)
    level_sum(R, "cb", 1)
    level_sum(R, "se", 1)
    scatter_pass(R, "part", 6)
    memory_send(R)
    level_sum(R, "ca", 2)
    small_wait(R)
    small_sums(R, 1)
    level_sum(R, "cb", 2)
    level_sum(R, "se", 2)
    small_wait(R)
    small_sums(R, 2)
    last_start(R, "gg")
    last_start(R, "gd")
    last_start(R, "cc")
    level_sum(R, "ca", 3)
    level_sum(R, "cb", 3)
    small_wait(R)
    small_sums(R, 3)
    level_sum(R, "se", 3)
    last_start(R, "ca")
    small_wait(R)
    small_sums(R, 4)
    last_start(R, "cb")
    states_back(R)
    last_start(R, "se")
    memory_end(R)
    for copy in R.local:
        copy.wait()
    for name in ("gg", "gd", "se", "ca", "cb", "cc"):
        last_copy(R, name).wait()


def per_device(states, memory, target_mask, memory_length, norm_self, self_query, self_key, self_value, self_out,
               bias_table, norm_cross, cross_query, cross_key, cross_value, cross_out, norm_ffn, ffn_gate, ffn_up,
               ffn_down, cotangent):
    ways = WAYS
    zin = lax.axis_size("dp") == LEVELS
    T, _, D = states.shape
    HW = self_query.shape[1]
    HC = bias_table.shape[1]
    F = ffn_gate.shape[1]
    hd = HW // HC
    M = memory.shape[0] * ways
    heads = D // hd
    ins = dict(
        st_in=(states, ANY), mem_in=(memory, ANY), wq=(self_query.T, ANY), wk=(self_key.T, ANY), wv=(self_value.T, ANY),
        so=(self_out, ANY), cq=(cross_query.T, ANY), ck=(cross_key.T, ANY), cv=(cross_value.T, ANY),
        co=(cross_out, ANY), mask_in=(target_mask, V), table=(bias_table.T, V), lens=(memory_length, SM),
        g_self=(norm_self, V), g_cross=(norm_cross, V), g_ffn=(norm_ffn, V), cot_in=(cotangent, ANY), gate_in=(ffn_gate, ANY),
        up_in=(ffn_up, ANY), down_in=(ffn_down, ANY),
    )
    half = HW // 2
    summed = dict(
        gg=(2, 2, 2, D // 4, F), gd=(2, 2, F // 4, D), cb=(2, 2, half, D), ca=(2, 2, half, D), cc=(2, 2, half // 2, D),
        se=(2, 2, 3 * HW // 4, D),
    )
    tc = T // ways
    outs = dict(
        br=((tc, ways, D), BF, V), mgo=((M // ways, ways, D), F32, ANY), sgo=((tc, ways, D), F32, ANY),
        smo=((8, D), F32, V), tg=((HC, bias_table.shape[0]), F32, V),
    )
    outs.update((name, (shape, BF, V)) for name, shape in summed.items())
    scratch = dict(
        att=V((D, T), BF), qs=V((ways, HW, T), BF), ks=V((ways, T, HW), BF), kts=V((ways, HW, T), BF),
        vts=V((ways, HW, T), BF), vs=V((ways, T, HW), BF), lse_s=V((ways, HC, 1, T), F32),
        second=V((T, D), F32), nc=V((T, D), BF), qc=V((D, T), BF), kc=V((M, D), BF), kct=V((D, M), BF),
        vc=V((M, D), BF), vct=V((D, M), BF), lse_c=V((heads // 2, 1, 2 * T), F32), attc=V((D, T), BF), memf=V((M, D), BF),
        waf=V((5, D, D), BF), nall=V((ways, T, D), BF), upall=V((ways, T, D), BF), et=V((T, HC * T), F32),
        atp=V((ways, HW, T), BF), part=V((ways, T, D), BF), ngr=V((6, T // 2, D), BF), brp=V((ways, T, D), BF),
        hid=V((ways * T, F), BF), gu=V((ways * T, 2 * F), BF),
        wg=V((5, ways, 2, half, D), BF), wgc=V((5, ways, half, D), BF), wgr=V((2, 3, 5, half // 2, D), BF),
        dot=V((D, T), BF),
        fgr=V((ways, tc, D), BF), near=V((2, 2, 2, tc, D), BF), far=V((2, 2, tc, D), BF),
        sm=V((8, D), F32), sm2=V((8, D), F32), sm3=V((8, D), F32), sm4=V((8, D), F32),
        smr=V((6, 8, D), F32), w_sem=dma(11), in_sem=dma(3), sg_sem=dma(4), mg_out=dma(4), sg=V((T, D), F32), ws=V((3 * HW, D), BF), st=V((ways, T, D), BF), mask=V((T, 8), F32),
        gate=V((D, F), BF), up=V((D, F), BF), down=V((F, D), BF),
    )
    for name, n in dict(mem=4, wa=8, fz=8, fw=16, att=4, cot=5, nf=5, ng=6, near=12, do=4, fg=4, mg=4, sm=8, wg=18, wgc=5).items():
        scratch[name + "_s"] = dma(n)
        scratch[name + "_r"] = dma(n)
    for name, shape in summed.items():
        scratch[name + "_c"] = V(shape[1:], BF)
        scratch[name + "_x"] = V(shape[1:-3] + shape[-2:], BF)
        scratch[name + "_ok"] = pltpu.SemaphoreType.REGULAR
        for kind, n in dict(cs=2, cr=2, zs=3, zr=3).items():
            scratch[name + "_" + kind] = dma(n)
        scratch[name + "_as"] = dma(3)
        scratch[name + "_ar"] = dma(3)
    def phase(R):
        R.zin = zin
        whole_phase(R)
    G = types.SimpleNamespace(**run_kernel("block", [phase], ins, outs, scratch, 0))
    block_out = G.br
    memory_grad = G.mgo
    states_grad = G.sgo
    sums = [x.astype(F32) for x in (G.gg, G.gd, G.cb, G.ca, G.cc, G.se, G.smo, G.tg)]
    if not zin:
        sums = [lax.psum(x, "dp") for x in sums]
    gg, gd, cb, ca, cc, se, sm, tg = sums
    gate_grad, up_grad = (gg[:, i].reshape(D, F) for i in range(2))
    down_grad = gd.reshape(F, D)
    cross = [x.reshape(2, -1, half, D) for x in (cb, ca, cc)]
    cross = [x[:, i].reshape(HW, D) for x in cross for i in range(x.shape[1])]
    own = se.reshape(3, HW, D)
    return (block_out, states_grad, memory_grad, sm[0], own[0].T, own[1].T, own[2].T, cross[SO], tg.T, sm[1],
            cross[CQ].T, cross[CK].T, cross[CV].T, cross[CO], sm[2], gate_grad, up_grad, down_grad)


def solution(mesh):
    seq = ("dp", "rep")
    col, row, tok = P(None, "mp"), P("mp", None), P("mp", seq, None)
    in_specs = (P(None, seq, None), tok, P(seq, None), P(seq), P(), col, col, col, row, col, P(), col, col, col, row,
                P(), col, col, row, tok)
    out_specs = (tok, tok, tok, P(), col, col, col, row, col, P(), col, col, col, row, P(), col, col, row)
    return jax.shard_map(per_device, mesh=mesh, in_specs=in_specs, out_specs=out_specs, check_vma=False)
```
